512 devices in a mesh: fiber: 32 (over y, x), tm: 16 (over z, core).
Axes of the slice: x: 4, y: 8, z: 8, core: 2. Of those that a mesh axis runs over, the one named last changes fastest.
Arguments:
- strain: bfloat16 [1024, 65536], P('tm', 'fiber'), may hold values from -6 to 6
- fan_cut: int32 [64], replicated, may hold values from 0 to 32768
- sta_len: int32 [65536], P('fiber'), may hold values from 8 to 64
- lta_len: int32 [65536], P('fiber'), may hold values from 128 to 2048
- drift_code: int32 [65536], P('fiber'), may hold values from 0 to 64
- threshold: int32 [65536], P('fiber'), may hold values from 16 to 128
Outputs:
- filtered: bfloat16 [1024, 65536], P('tm', 'fiber')
- ratio: float32 [1024, 65536], P('tm', 'fiber')
- ph: float32 [1024, 65536], P('tm', 'fiber')
The draws below stay inside these ranges and needn't reach their ends.
All inputs are finite; a program needn't handle non-finite values.
Results may differ from the reference program's by a relative error of at most 0.0029.
Values may be sent and summed in bfloat16 or wider, within the bound.
A program may use at most 192 MiB of HBM per device.

```python
import math
import jax
import jax.numpy as jnp
from jax import lax

FRAME = 128
BINS = 64
CHANNELS = 65536
TIME = 1024


def fan_table(key):
    cuts = jax.random.randint(jax.random.fold_in(key, 101), (BINS,), 0, CHANNELS // 2 + 1)
    bin_index = jnp.arange(BINS, dtype=jnp.int32)
    cuts = jnp.where(bin_index == 0, 0, cuts)
    cuts = jnp.where(bin_index == BINS - 1, CHANNELS // 2, cuts)
    return cuts.astype(jnp.int32)


def draw_fan_cut(key, part):
    return fan_table(key)


def draw_strain(key, part):
    cuts = fan_table(key)
    key = jax.random.fold_in(key, 7)
    count = min(16, BINS - 2)
    key_bins, key_offset, key_amp, key_phase, key_noise = jax.random.split(key, 5)
    chosen = (1 + jax.random.permutation(key_bins, BINS - 2)[:count]).astype(jnp.int32)
    offsets = jax.random.randint(key_offset, (count,), -1, 3)
    wavenum = jnp.clip(cuts[chosen] + offsets, 0, CHANNELS // 2).astype(jnp.int32)
    phases = jax.random.uniform(key_phase, (count,), jnp.float32, 0.0, 2.0 * math.pi)
    amps = jax.random.uniform(key_amp, (count,), jnp.float32, 0.22, 0.28)
    noise = 0.3 * jnp.clip(jax.random.normal(key_noise, (TIME, CHANNELS), jnp.float32), -6.0, 6.0)
    channel_idx = jnp.arange(CHANNELS, dtype=jnp.int32)
    channel_high = channel_idx // 256
    channel_low = channel_idx % 256
    time_idx = jnp.arange(TIME, dtype=jnp.int32)

    def add_wave(index, total):
        wave_k = wavenum[index]
        wave_f = chosen[index]
        spatial = ((wave_k * channel_high % CHANNELS * 256 + wave_k * channel_low) % CHANNELS).astype(jnp.float32)
        temporal = (wave_f * time_idx % FRAME).astype(jnp.float32)
        angle = 2.0 * math.pi / CHANNELS * spatial[None, :] + 2.0 * math.pi / FRAME * temporal[:, None] + phases[index]
        return total + amps[index] * jnp.cos(angle)
    total = lax.fori_loop(0, count, add_wave, noise)
    return jnp.clip(total, -6.0, 6.0).astype(jnp.bfloat16)


def touch_ends(result, stream_key, least, largest):
    place = [jax.random.randint(jax.random.fold_in(stream_key, axis), (), 0, length) for axis, length in enumerate(result.shape)]
    main_axis = result.shape.index(max(result.shape))
    next_to = place[:main_axis] + [(place[main_axis] + 1) % result.shape[main_axis]] + place[main_axis + 1:]
    return result.at[tuple(place)].set(least).at[tuple(next_to)].set(largest)


def setup_inputs(seed: int = 0) -> dict:
    streams_of = jax.random.split(jax.random.key(seed), 7)
    return {
        "strain": draw_strain(jax.random.fold_in(streams_of[6], 71), 0),
        "fan_cut": draw_fan_cut(jax.random.fold_in(streams_of[6], 71), 0),
        "sta_len": touch_ends(jax.random.randint(streams_of[2], (CHANNELS,), 8, 65), jax.random.fold_in(streams_of[2], 1), 8, 64).astype(jnp.int32),
        "lta_len": touch_ends(jax.random.randint(streams_of[3], (CHANNELS,), TIME // 8, 2 * TIME + 1), jax.random.fold_in(streams_of[3], 1), TIME // 8, 2 * TIME).astype(jnp.int32),
        "drift_code": touch_ends(jax.random.randint(streams_of[4], (CHANNELS,), 0, 65), jax.random.fold_in(streams_of[4], 1), 0, 64).astype(jnp.int32),
        "threshold": touch_ends(jax.random.randint(streams_of[5], (CHANNELS,), 16, 129), jax.random.fold_in(streams_of[5], 1), 16, 128).astype(jnp.int32),
    }


HIGH = lax.Precision.HIGHEST


def time_tables(frame):
    stride = frame // 2
    samples = jnp.arange(frame, dtype=jnp.int32)
    bin_index = jnp.arange(stride, dtype=jnp.int32)
    window = 0.5 - 0.5 * jnp.cos((2.0 * math.pi / frame) * samples.astype(jnp.float32))
    angles = (2.0 * math.pi / frame) * ((samples[:, None] * bin_index[None, :]) % frame).astype(jnp.float32)
    analysis = jnp.stack([window[:, None] * jnp.cos(angles), -window[:, None] * jnp.sin(angles)])
    weights = jnp.where(bin_index == 0, 1.0, 2.0).astype(jnp.float32) / frame
    synthesis = jnp.stack([weights[:, None] * jnp.cos(angles.T), -weights[:, None] * jnp.sin(angles.T)])
    return analysis, synthesis


def reference(strain, fan_cut, sta_len, lta_len, drift_code, threshold):
    stride = FRAME // 2
    analysis, synthesis = time_tables(FRAME)
    padded = jnp.concatenate([jnp.zeros((stride, CHANNELS), strain.dtype), strain], axis=0)
    wavenum = jnp.arange(CHANNELS, dtype=jnp.int32)
    wavenum = jnp.minimum(wavenum, CHANNELS - wavenum)
    passband = wavenum[None, :] <= fan_cut[:, None]

    def frame_step(previous, frame_index):
        segment = lax.dynamic_slice_in_dim(padded, frame_index * stride, FRAME, 0).astype(jnp.float32)
        spectrum = jnp.einsum('nc,snb->sbc', segment, analysis, precision=HIGH)
        waves = jnp.fft.fft(lax.complex(spectrum[0], spectrum[1]), axis=1)
        kept_wave = jnp.where(passband, waves, jnp.zeros_like(waves))
        restored = jnp.fft.ifft(kept_wave, axis=1)
        stacked = jnp.stack([jnp.real(restored), jnp.imag(restored)])
        pieces = jnp.einsum('sbc,sbn->nc', stacked, synthesis, precision=HIGH)
        return pieces[stride:], previous + pieces[:stride]

    frame_count = TIME // stride
    tail_block, blocks = lax.scan(frame_step, jnp.zeros((stride, CHANNELS), jnp.float32),
                                  jnp.arange(frame_count, dtype=jnp.int32))
    joined = jnp.concatenate([blocks[1:], tail_block[None]], axis=0).reshape(TIME, CHANNELS)
    filtered = joined.astype(jnp.bfloat16)
    energy = filtered.astype(jnp.float32) ** 2
    keep_short = 1.0 - 1.0 / sta_len.astype(jnp.float32)
    keep_long = 1.0 - 1.0 / lta_len.astype(jnp.float32)
    drift_rate = 0.5 + drift_code.astype(jnp.float32) / 64.0
    limits = threshold.astype(jnp.float32)

    def tick(state, energy_row):
        short_avg, long_avg, climb, lowest = state
        short_avg = keep_short * short_avg + (1.0 - keep_short) * energy_row
        long_avg = keep_long * long_avg + (1.0 - keep_long) * energy_row
        ratio = short_avg / long_avg
        climb = climb + (ratio - drift_rate)
        lowest = jnp.minimum(lowest, climb)
        return (short_avg, long_avg, climb, lowest), (ratio, (climb - lowest) / limits)

    unit_vec = jnp.ones((CHANNELS,), jnp.float32)
    zero_vec = jnp.zeros((CHANNELS,), jnp.float32)
    final_state, outputs = lax.scan(tick, (unit_vec, unit_vec, zero_vec, zero_vec), energy)
    return filtered, outputs[0], outputs[1]
```

```python
import functools
import math

import jax
import jax.numpy as jnp
import numpy as np
from jax import lax
from jax.experimental import pallas as pl
from jax.experimental.pallas import tpu as pltpu
from jax.sharding import PartitionSpec as P

FRAME = 128
HOP = 64
BINS = 64
LANES = 128
ROWS = 16
BLOCK = 128
TOP = 32512.0
MESH = pl.DeviceIdType.MESH
F32 = jnp.float32
BF16 = jnp.bfloat16


def halves(table):
    high = table.astype(np.float32).astype(jnp.bfloat16)
    low = (table - high.astype(np.float64)).astype(np.float32).astype(jnp.bfloat16)
    return high, low


def time_order():
    rows = np.arange(HOP)
    return 8 * (rows % 8) + rows // 8


def tables(total):
    rows = total // LANES
    n = np.arange(FRAME)
    f = np.arange(BINS)
    angle = 2.0 * math.pi / FRAME * ((f[:, None] * n[None, :]) % FRAME)
    window = 0.5 - 0.5 * np.cos(2.0 * math.pi / FRAME * n)
    analysis = np.concatenate([window * np.cos(angle), -window * np.sin(angle)], 0)
    weight = np.where(f == 0, 1.0, 2.0)[:, None] / FRAME
    synthesis = np.concatenate([weight * np.cos(angle), -weight * np.sin(angle)], 0).T
    order = time_order()
    synthesis = synthesis[np.concatenate([order, HOP + order])]
    a = np.arange(rows)
    outer = 2.0 * math.pi / rows * ((a[:, None] * a[None, :]) % rows)
    blocks = rows // BLOCK
    outer = np.stack(
        [np.cos(outer).reshape(blocks, BLOCK, rows), -np.sin(outer).reshape(blocks, BLOCK, rows)], 1
    ).reshape(blocks, 2 * BLOCK, rows)
    b = np.arange(LANES)
    turn = 2.0 * math.pi / total * ((a[:, None] * b[None, :]) % total)
    turn = np.concatenate([np.cos(turn), -np.sin(turn)], 1)
    inner = 2.0 * math.pi / LANES * ((b[:, None] * b[None, :]) % LANES)
    cos, sin = np.cos(inner), np.sin(inner)
    forward = np.block([[cos, -sin], [sin, cos]])
    inverse = np.block([[cos, sin], [-sin, cos]]) / total
    ah, al = halves(analysis)
    sh, sl = halves(synthesis)
    oh, ol = halves(outer)
    fh, fl = halves(forward)
    ih, il = halves(inverse)
    return (
        np.concatenate([ah, al], 0),
        np.concatenate([sh, sh, sl], 1),
        np.concatenate([oh, oh, ol], 2),
        turn.astype(np.float32),
        np.concatenate([fh, fh, fl], 0),
        np.concatenate([ih, ih, il], 0),
    )


def split(x):
    high = x.astype(BF16)
    return high, (x - high.astype(F32)).astype(BF16)


def across(x):
    high, low = split(x)
    return jnp.concatenate([high, low, high], axis=1)


def peak_of(x):
    top = jnp.max(jnp.max(jnp.abs(x), axis=0, keepdims=True), axis=1, keepdims=True)
    return jnp.maximum(top, 1e-30)


def coded(x, gain):
    return jnp.round(x * gain).astype(jnp.int32).astype(jnp.int16)


def kernel(
    nf,
    nt,
    strain,
    cut,
    sta,
    lta,
    drift,
    limit,
    ana,
    syn,
    outer,
    turn,
    fwd,
    inv,
    filtered,
    ratio,
    ph,
    rim,
    spec,
    snd1,
    rcv1,
    scs1,
    scr1,
    x3,
    z3,
    snd2,
    rcv2,
    scs2,
    scr2,
    deco,
    head,
    tail,
    sps,
    spr,
    sss,
    ssr,
    lev,
    seg,
    cars,
    carr,
    sums,
    sumr,
    temp,
    rim_sem,
    s1s,
    s1r,
    c1s,
    c1r,
    s2s,
    s2r,
    c2s,
    c2r,
    sp_s,
    sp_r,
    ss_s,
    ss_r,
    ca_s,
    ca_r,
    su_s,
    su_r,
):
    me = lax.axis_index("fiber")
    tm = lax.axis_index("tm")
    per = BINS // nf
    rows = nf * ROWS
    blocks = rows // BLOCK
    total = rows * LANES
    chans = ROWS * LANES
    later, earlier = lax.rem(tm + 1, nt), lax.rem(tm + nt - 1, nt)

    def remote(src, dst, send, recv, **to):
        return pltpu.make_async_remote_copy(
            src_ref=src, dst_ref=dst, send_sem=send, recv_sem=recv, device_id=to, device_id_type=MESH
        )

    barrier = pltpu.get_barrier_semaphore()

    def greet_fiber(j, c):
        pl.semaphore_signal(
            barrier, inc=1, device_id={"fiber": lax.rem(me + j, nf)}, device_id_type=MESH
        )
        return c

    def greet_tm(j, c):
        pl.semaphore_signal(
            barrier, inc=1, device_id={"tm": lax.rem(tm + j, nt)}, device_id_type=MESH
        )
        return c

    lax.fori_loop(1, nf, greet_fiber, 0)
    lax.fori_loop(1, nt, greet_tm, 0)
    pl.semaphore_wait(barrier, nf - 1 + nt - 1)

    rim_copy = remote(strain, rim, rim_sem.at[0], rim_sem.at[1], tm=later)
    rim_copy.start()
    rim_copy.wait()
    has_rim = jnp.where(tm > 0, 1.0, 0.0).astype(F32)

    peak = jnp.zeros((1, 1), F32)
    for q in range(0, ROWS, 2):
        cols = slice(q * LANES, (q + 2) * LANES)
        before = (rim[:, cols].astype(F32) * has_rim).astype(BF16)
        frame = jnp.concatenate([before, strain[:, cols]], axis=0)
        both = jnp.dot(ana[...], frame, preferred_element_type=F32)
        got = both[:FRAME] + both[FRAME:]
        spec[:, q, :] = got[:, :LANES]
        spec[:, q + 1, :] = got[:, LANES:]
        peak = jnp.maximum(peak, peak_of(got))
    gain = TOP / peak
    scs1[0] = jnp.broadcast_to(peak * (1.0 / TOP), (1, LANES))
    scr1[me] = scs1[0]

    def code1(f):
        snd1[f, :, 0:LANES] = coded(spec[f], gain)
        snd1[f, :, LANES : 2 * LANES] = coded(spec[BINS + f], gain)

    def scale1(j):
        to = lax.rem(me + j, nf)
        return remote(scs1.at[0], scr1.at[me], c1s.at[j], c1r.at[j], fiber=to)

    def data1(b, j):
        to = lax.rem(me + j, nf)
        return remote(
            snd1.at[to * per + b],
            rcv1.at[b, pl.ds(pl.multiple_of(me * ROWS, ROWS), ROWS), :],
            s1s.at[b, j],
            s1r.at[b, j],
            fiber=to,
        )

    def from1(b, j):
        back = lax.rem(me + nf - j, nf)
        return remote(
            snd1.at[0],
            rcv1.at[b, pl.ds(pl.multiple_of(back * ROWS, ROWS), ROWS), :],
            s1s.at[b, j],
            s1r.at[b, j],
            fiber=back,
        )

    def out_scale(j, c):
        scale1(j).start()
        return c

    lax.fori_loop(1, nf, out_scale, 0)

    def out_bins(b, c):
        def out_peer(j, c):
            code1(lax.rem(me + j, nf) * per + b)
            data1(b, j).start()
            return c

        lax.fori_loop(1, nf, out_peer, 0)
        code1(me * per + b)
        rcv1[b, pl.ds(pl.multiple_of(me * ROWS, ROWS), ROWS), :] = snd1[me * per + b]
        return c

    lax.fori_loop(0, per, out_bins, 0)

    def in_scale(j, c):
        back = lax.rem(me + nf - j, nf)
        remote(scs1.at[0], scr1.at[back], c1s.at[j], c1r.at[j], fiber=back).wait_recv()
        return c

    lax.fori_loop(1, nf, in_scale, 0)

    peers = BLOCK // ROWS

    def scale2(b, blk, to):
        j = lax.rem(to - me + nf, nf)
        return remote(
            scs2.at[b, blk], scr2.at[me * per + b], c2s.at[b, j], c2r.at[b, j], fiber=to
        )

    def data2(b, to):
        j = lax.rem(to - me + nf, nf)
        return remote(
            snd2.at[b, pl.ds(pl.multiple_of(to * ROWS, ROWS), ROWS), :],
            rcv2.at[me * per + b],
            s2s.at[b, j],
            s2r.at[b, j],
            fiber=to,
        )

    lane = lax.broadcasted_iota(jnp.int32, (BLOCK, LANES), 1)
    row = lax.broadcasted_iota(jnp.int32, (BLOCK, LANES), 0)

    def one_bin(b, c):
        def in_peer(j, c):
            from1(b, j).wait_recv()
            return c

        lax.fori_loop(1, nf, in_peer, 0)
        limit_k = cut[me * per + b]

        def decode(p, c):
            at = pl.multiple_of(p * ROWS, ROWS)
            scale = scr1[p]
            x = rcv1[b, pl.ds(at, ROWS), :].astype(F32)
            x = x * jnp.concatenate([scale, scale], axis=1)
            high, low = split(x)
            x3[pl.ds(at, ROWS), :] = high
            x3[pl.ds(pl.multiple_of(rows + at, ROWS), ROWS), :] = low
            x3[pl.ds(pl.multiple_of(2 * rows + at, ROWS), ROWS), :] = high
            return c

        lax.fori_loop(0, nf, decode, 0)

        def to_waves(blk, c):
            at = pl.multiple_of(blk * BLOCK, BLOCK)
            pq = jnp.dot(outer[blk], x3[...], preferred_element_type=F32)
            re = pq[:BLOCK, :LANES] - pq[BLOCK:, LANES:]
            im = pq[:BLOCK, LANES:] + pq[BLOCK:, :LANES]
            tr = turn[pl.ds(at, BLOCK), 0:LANES]
            ti = turn[pl.ds(at, BLOCK), LANES : 2 * LANES]
            y = jnp.concatenate([re * tr - im * ti, re * ti + im * tr], axis=1)
            w = jnp.dot(across(y), fwd[...], preferred_element_type=F32)
            k = row + blk * BLOCK + rows * lane
            keep = jnp.minimum(k, total - k) <= limit_k
            w = jnp.concatenate(
                [jnp.where(keep, w[:, :LANES], 0.0), jnp.where(keep, w[:, LANES:], 0.0)], axis=1
            )
            z = jnp.dot(across(w), inv[...], preferred_element_type=F32)
            re, im = z[:, :LANES], z[:, LANES:]
            z = jnp.concatenate([re * tr + im * ti, im * tr - re * ti], axis=1)
            high, low = split(z)
            z3[pl.ds(at, BLOCK), :] = high
            z3[pl.ds(pl.multiple_of(rows + at, BLOCK), BLOCK), :] = low
            z3[pl.ds(pl.multiple_of(2 * rows + at, BLOCK), BLOCK), :] = high
            return c

        lax.fori_loop(0, blocks, to_waves, 0)

        def to_channels(blk, c):
            at = pl.multiple_of(blk * BLOCK, BLOCK)
            pq = jnp.dot(outer[blk], z3[...], preferred_element_type=F32)
            re = pq[:BLOCK, :LANES] + pq[BLOCK:, LANES:]
            im = pq[:BLOCK, LANES:] - pq[BLOCK:, :LANES]
            x = jnp.concatenate([re, im], axis=1)
            top = peak_of(x)
            scs2[b, blk] = jnp.broadcast_to(top * (1.0 / TOP), (1, LANES))
            snd2[b, pl.ds(at, BLOCK), :] = coded(x, TOP / top)

            def out_peer(i, c):
                to = blk * peers + i

                @pl.when(to != me)
                def _():
                    scale2(b, blk, to).start()
                    data2(b, to).start()

                @pl.when(to == me)
                def _():
                    scr2[me * per + b] = scs2[b, blk]
                    mine = pl.multiple_of(me * ROWS, ROWS)
                    rcv2[me * per + b] = snd2[b, pl.ds(mine, ROWS), :]

                return c

            lax.fori_loop(0, peers, out_peer, 0)
            return c

        lax.fori_loop(0, blocks, to_channels, 0)
        return c

    lax.fori_loop(0, per, one_bin, 0)

    def in_back(j, c):
        back = lax.rem(me + nf - j, nf)

        def in_bin(b, c):
            f = back * per + b
            remote(scs2.at[0, 0], scr2.at[f], c2s.at[b, j], c2r.at[b, j], fiber=back).wait_recv()
            remote(
                snd2.at[0, pl.ds(0, ROWS), :], rcv2.at[f], s2s.at[b, j], s2r.at[b, j], fiber=back
            ).wait_recv()
            return c

        lax.fori_loop(0, per, in_bin, 0)
        return c

    lax.fori_loop(1, nf, in_back, 0)

    def decode2(f, c):
        x = rcv2[f].astype(F32)
        scale = scr2[f]
        deco[0, f] = x[:, :LANES] * scale
        deco[1, f] = x[:, LANES:] * scale
        return c

    lax.fori_loop(0, BINS, decode2, 0)

    chunks = 4
    wide = ROWS // chunks

    def spill(c):
        span = pl.ds(c * wide, wide)
        return remote(sps.at[span], spr.at[span], sp_s.at[c], sp_r.at[c], tm=earlier)

    def spill_scale(c):
        return remote(sss.at[c], ssr.at[c], ss_s.at[c], ss_r.at[c], tm=earlier)

    for chunk in range(chunks):
        top = jnp.full((1, 1), 1e-30, F32)
        for q in range(chunk * wide, (chunk + 1) * wide, 2):
            x = jnp.concatenate(
                [
                    jnp.concatenate([deco[0, :, q, :], deco[1, :, q, :]], axis=0),
                    jnp.concatenate([deco[0, :, q + 1, :], deco[1, :, q + 1, :]], axis=0),
                ],
                axis=1,
            )
            high, low = split(x)
            got = jnp.dot(
                syn[...], jnp.concatenate([high, low, high], axis=0), preferred_element_type=F32
            )
            for i in range(2):
                head[q + i] = got[:HOP, i * LANES : (i + 1) * LANES]
                tail[q + i] = got[HOP:, i * LANES : (i + 1) * LANES]
            top = jnp.maximum(top, peak_of(got[:HOP]))
        sss[chunk] = jnp.broadcast_to(top * (1.0 / TOP), (1, LANES))
        spill_scale(chunk).start()
        for q in range(chunk * wide, (chunk + 1) * wide):
            sps[q] = coded(head[q], TOP / top)
        spill(chunk).start()

    has_next = jnp.where(tm < nt - 1, 1.0, 0.0).astype(F32)
    seg_id = lax.broadcasted_iota(jnp.int32, (8, LANES), 0)

    def shifted(x, by, fill):
        return jnp.where(seg_id >= by, pltpu.roll(x, by, 0), fill)

    def rate_of(length):
        return 1.0 - 1.0 / length

    def natural(vectors):
        for i in range(8):
            temp[pl.ds(i, 8, stride=8), :] = vectors[i]
        return temp[...]

    for chunk in range(chunks):
        spill_scale(chunk).wait_recv()
        spill(chunk).wait_recv()

        def scan_row(q, c):
            at = pl.ds(q, 1)
            cols = pl.ds(pl.multiple_of(q * LANES, LANES), LANES)
            heads = spr[q].astype(F32) * (ssr[chunk] * has_next)
            rounded = (tail[q] + heads).astype(BF16).astype(F32)
            part = [rounded[8 * i : 8 * i + 8] for i in range(8)]
            filtered[:, cols] = natural(part).astype(BF16)
            energy = [v * v for v in part]
            for s, ref in enumerate((sta, lta)):
                keep = jnp.broadcast_to(rate_of(ref[at, :]), (8, LANES))
                gain = 1.0 - keep
                level = gain * energy[0]
                lev[s, q, 0:8] = level
                for i in range(1, 8):
                    level = keep * level + gain * energy[i]
                    lev[s, q, 8 * i : 8 * i + 8] = level
                power = keep * keep
                power = power * power
                power = power * power
                for by in (1, 2, 4):
                    level = level + power * shifted(level, by, 0.0)
                    power = power * power
                seg[s, q] = shifted(level, 1, 0.0)
                cars[s, at, :] = level[7:8]
            return c

        lax.fori_loop(chunk * wide, (chunk + 1) * wide, scan_row, 0)

    def to_later(snd, rcv, send, recv, j):
        return remote(snd, rcv.at[tm], send.at[j], recv.at[j], tm=lax.rem(tm + j, nt))

    def from_earlier(snd, rcv, send, recv, j):
        back = lax.rem(tm + nt - j, nt)
        return remote(snd, rcv.at[back], send.at[j], recv.at[j], tm=back)

    def pass_on(snd, rcv, send, recv):
        def out(j, c):
            to_later(snd, rcv, send, recv, j).start()
            return c

        lax.fori_loop(1, nt - tm, out, 0)

        def come(j, c):
            from_earlier(snd, rcv, send, recv, j).wait_recv()
            return c

        lax.fori_loop(1, tm + 1, come, 0)

    pass_on(cars, carr, ca_s, ca_r)
    decay = []
    for ref in (sta, lta):
        power = rate_of(ref[...])
        for _ in range(6):
            power = power * power
        decay.append(power)

    def lap(k, state):
        return tuple(decay[s] * state[s] + carr[k, s] for s in range(2))

    ones = jnp.ones((ROWS, LANES), F32)
    start = lax.fori_loop(0, tm, lap, (ones, ones))
    head[0, 0:ROWS] = start[0]
    head[1, 0:ROWS] = start[1]

    def climb_row(q, c):
        at = pl.ds(q, 1)
        cols = pl.ds(pl.multiple_of(q * LANES, LANES), LANES)
        avg = []
        for s, ref in enumerate((sta, lta)):
            keep = jnp.broadcast_to(rate_of(ref[at, :]), (8, LANES))
            carry = jnp.broadcast_to(head[s, at, :], (8, LANES))
            power = keep * keep
            power = power * power
            power = power * power
            for bit in (1, 2, 4):
                carry = jnp.where((seg_id // bit) % 2 == 1, carry * power, carry)
                power = power * power
            entry = seg[s, q] + carry
            values = []
            for i in range(8):
                entry = entry * keep
                values.append(lev[s, q, 8 * i : 8 * i + 8] + entry)
            avg.append(values)
        quotient = [avg[0][i] / avg[1][i] for i in range(8)]
        ratio[:, cols] = natural(quotient)
        rate = jnp.broadcast_to(0.5 + drift[at, :] * (1.0 / 64.0), (8, LANES))
        climb = quotient[0] - rate
        low = climb
        climbs, lows = [climb], [low]
        for i in range(1, 8):
            climb = climb + (quotient[i] - rate)
            low = jnp.minimum(low, climb)
            climbs.append(climb)
            lows.append(low)
        whole = climb
        for by in (1, 2, 4):
            whole = whole + shifted(whole, by, 0.0)
        base = shifted(whole, 1, 0.0)
        least = base + low
        for by in (1, 2, 4):
            least = jnp.minimum(least, shifted(least, by, jnp.inf))
        floor = shifted(least, 1, jnp.inf)
        for i in range(8):
            up = base + climbs[i]
            lev[0, q, 8 * i : 8 * i + 8] = up
            lev[1, q, 8 * i : 8 * i + 8] = jnp.minimum(floor, base + lows[i])
        sums[0, at, :] = whole[7:8]
        sums[1, at, :] = least[7:8]
        return c

    lax.fori_loop(0, ROWS, climb_row, 0)

    pass_on(sums, sumr, su_s, su_r)

    def lap2(k, state):
        total_up, low = state
        return total_up + sumr[k, 0], jnp.minimum(low, total_up + sumr[k, 1])

    zeros = jnp.zeros((ROWS, LANES), F32)
    before, low = lax.fori_loop(0, tm, lap2, (zeros, zeros))
    head[2, 0:ROWS] = before
    head[3, 0:ROWS] = low

    def ph_row(q, c):
        at = pl.ds(q, 1)
        cols = pl.ds(pl.multiple_of(q * LANES, LANES), LANES)
        base = jnp.broadcast_to(head[2, at, :], (8, LANES))
        low = jnp.broadcast_to(head[3, at, :], (8, LANES))
        scale = jnp.broadcast_to(1.0 / limit[at, :], (8, LANES))
        out = []
        for i in range(8):
            climb = base + lev[0, q, 8 * i : 8 * i + 8]
            lowest = jnp.minimum(low, base + lev[1, q, 8 * i : 8 * i + 8])
            out.append((climb - lowest) * scale)
        ph[:, cols] = natural(out)
        return c

    lax.fori_loop(0, ROWS, ph_row, 0)


    def sent1(j, c):
        scale1(j).wait_send()

        def sent_bin(b, c):
            data1(b, j).wait_send()
            to = lax.rem(me + j, nf)
            scale2(b, 0, to).wait_send()
            data2(b, to).wait_send()
            return c

        lax.fori_loop(0, per, sent_bin, 0)
        return c

    lax.fori_loop(1, nf, sent1, 0)
    for chunk in range(chunks):
        spill_scale(chunk).wait_send()
        spill(chunk).wait_send()

    def sent_on(j, c):
        to_later(sums, carr, ca_s, ca_r, j).wait_send()
        to_later(sums, sumr, su_s, su_r, j).wait_send()
        return c

    lax.fori_loop(1, nt - tm, sent_on, 0)


def body(nf, nt, strain, fan_cut, sta_len, lta_len, drift_code, threshold):
    per = BINS // nf
    rows = nf * ROWS
    total = rows * LANES
    blocks = rows // BLOCK
    tabs = [jnp.asarray(t) for t in tables(total)]
    per_chan = [v.astype(F32).reshape(ROWS, LANES) for v in (sta_len, lta_len, drift_code, threshold)]
    vmem = pl.BlockSpec(memory_space=pltpu.VMEM)
    smem = pl.BlockSpec(memory_space=pltpu.SMEM)
    dma = pltpu.SemaphoreType.DMA
    i16 = jnp.int16
    chans = ROWS * LANES
    return pl.pallas_call(
        functools.partial(kernel, nf, nt),
        out_shape=(
            jax.ShapeDtypeStruct((HOP, chans), BF16),
            jax.ShapeDtypeStruct((HOP, chans), F32),
            jax.ShapeDtypeStruct((HOP, chans), F32),
        ),
        in_specs=[vmem, smem] + [vmem] * 10,
        out_specs=(vmem, vmem, vmem),
        scratch_shapes=[
            pltpu.VMEM((HOP, chans), BF16),
            pltpu.VMEM((FRAME, ROWS, LANES), F32),
            pltpu.VMEM((BINS, ROWS, 2 * LANES), i16),
            pltpu.VMEM((per, rows, 2 * LANES), i16),
            pltpu.VMEM((1, 1, LANES), F32),
            pltpu.VMEM((nf, 1, LANES), F32),
            pltpu.VMEM((3 * rows, 2 * LANES), BF16),
            pltpu.VMEM((3 * rows, 2 * LANES), BF16),
            pltpu.VMEM((per, rows, 2 * LANES), i16),
            pltpu.VMEM((BINS, ROWS, 2 * LANES), i16),
            pltpu.VMEM((per, blocks, 1, LANES), F32),
            pltpu.VMEM((BINS, 1, LANES), F32),
            pltpu.VMEM((2, BINS, ROWS, LANES), F32),
            pltpu.VMEM((ROWS, HOP, LANES), F32),
            pltpu.VMEM((ROWS, HOP, LANES), F32),
            pltpu.VMEM((ROWS, HOP, LANES), i16),
            pltpu.VMEM((ROWS, HOP, LANES), i16),
            pltpu.VMEM((4, 1, LANES), F32),
            pltpu.VMEM((4, 1, LANES), F32),
            pltpu.VMEM((2, ROWS, HOP, LANES), F32),
            pltpu.VMEM((2, ROWS, 8, LANES), F32),
            pltpu.VMEM((2, ROWS, LANES), F32),
            pltpu.VMEM((nt, 2, ROWS, LANES), F32),
            pltpu.VMEM((2, ROWS, LANES), F32),
            pltpu.VMEM((nt, 2, ROWS, LANES), F32),
            pltpu.VMEM((HOP, LANES), F32),
            dma((2,)),
            dma((per, nf)),
            dma((per, nf)),
            dma((nf,)),
            dma((nf,)),
            dma((per, nf)),
            dma((per, nf)),
            dma((per, nf)),
            dma((per, nf)),
            dma((4,)),
            dma((4,)),
            dma((4,)),
            dma((4,)),
            dma((nt,)),
            dma((nt,)),
            dma((nt,)),
            dma((nt,)),
        ],
        compiler_params=pltpu.CompilerParams(
            collective_id=0, has_side_effects=True, vmem_limit_bytes=48 * 1024 * 1024
        ),
    )(strain, fan_cut, *per_chan, *tabs)


def solution(mesh):
    return jax.shard_map(
        functools.partial(body, mesh.shape["fiber"], mesh.shape["tm"]),
        mesh=mesh,
        in_specs=(P("tm", "fiber"), P(), P("fiber"), P("fiber"), P("fiber"), P("fiber")),
        out_specs=(P("tm", "fiber"), P("tm", "fiber"), P("tm", "fiber")),
        check_vma=False,
    )
```

```python
import functools
import math

import jax
import jax.numpy as jnp
import numpy as np
from jax import lax
from jax.experimental import pallas as pl
from jax.experimental.pallas import tpu as pltpu
from jax.sharding import PartitionSpec as P

FRAME = 128
HOP = 64
BINS = 64
LANES = 128
ROWS = 16
GROUP = 4
TOP = 32512.0
MESH = pl.DeviceIdType.MESH
F32 = jnp.float32
BF16 = jnp.bfloat16


def time_order():
    rows = np.arange(HOP)
    return 8 * (rows % 8) + rows // 8


def tables(total):
    rows = total // LANES
    half = rows // 2
    n = np.arange(FRAME)
    f = np.arange(BINS)
    angle = 2.0 * math.pi / FRAME * ((f[:, None] * n[None, :]) % FRAME)
    window = 0.5 - 0.5 * np.cos(2.0 * math.pi / FRAME * n)
    analysis = np.concatenate([window * np.cos(angle), -window * np.sin(angle)], 0)
    weight = np.where(f == 0, 1.0, 2.0)[:, None] / FRAME
    synthesis = np.concatenate([weight * np.cos(angle), -weight * np.sin(angle)], 0).T
    order = time_order()
    synthesis = synthesis[np.concatenate([order, HOP + order])]
    a = np.arange(half)
    outer = 2.0 * math.pi / half * ((a[:, None] * a[None, :]) % half)
    outer = np.concatenate([np.cos(outer), -np.sin(outer)], 0)
    step = np.broadcast_to(2.0 * math.pi / rows * a[:, None], (half, LANES))
    step = np.concatenate([np.cos(step), -np.sin(step)], 1)
    b = np.arange(LANES)
    wave = np.concatenate([2 * a, 2 * a + 1])
    turn = 2.0 * math.pi / total * ((wave[:, None] * b[None, :]) % total)
    turn = np.concatenate([np.cos(turn), -np.sin(turn)], 1)
    inner = 2.0 * math.pi / LANES * ((b[:, None] * b[None, :]) % LANES)
    cos, sin = np.cos(inner), np.sin(inner)
    forward = np.block([[cos, -sin], [sin, cos]])
    inverse = np.block([[cos, sin], [-sin, cos]]) / total
    return [t.astype(np.float32) for t in (analysis, outer, forward, inverse, synthesis, step, turn)]


def split(x):
    high = x.astype(BF16)
    return high, (x - high.astype(F32)).astype(BF16)


def across(x):
    high, low = split(x)
    return jnp.concatenate([high, low, high], axis=1)


def peak_of(x):
    top = jnp.max(jnp.max(jnp.abs(x), axis=0, keepdims=True), axis=1, keepdims=True)
    return jnp.maximum(top, 1e-30)


def coded(x, gain):
    return jnp.round(x * gain).astype(jnp.int32).astype(jnp.int16)


def kernel(
    nf,
    nt,
    *refs,
):
    (
        strain_far,
        cut_far,
        sta_far,
        lta_far,
        drift_far,
        limit_far,
        ana_far,
        outer_far,
        fwd_far,
        inv_far,
        syn_far,
        step_far,
        turn_far,
        filtered_far,
        ratio_far,
        ph_far,
        strain,
        cut,
        chan,
        ana_raw,
        outer_raw,
        fwd_raw,
        inv_raw,
        syn_raw,
        step,
        turn,
        ana,
        outer,
        fwd,
        inv,
        syn,
        filtered,
        ratio,
        ph,
        rim,
        spec,
        snd1,
        rcv1,
        scs1,
        scr1,
        x3,
        z3,
        snd2,
        rcv2,
        scs2,
        scr2,
        deco,
        head,
        tail,
        sps,
        spr,
        sss,
        ssr,
        lev,
        seg,
        cars,
        carr,
        sums,
        sumr,
        temp,
        rim_s,
        rim_r,
        s1s,
        s1r,
        c1s,
        c1r,
        s2s,
        s2r,
        c2s,
        c2r,
        sp_s,
        sp_r,
        ss_s,
        ss_r,
        ca_s,
        ca_r,
        su_s,
        su_r,
        load_sem,
        store_sem,
    ) = refs
    me = lax.axis_index("fiber")
    tm = lax.axis_index("tm")
    per = BINS // nf
    rows = nf * ROWS
    half = rows // 2
    total = rows * LANES
    later, earlier = lax.rem(tm + 1, nt), lax.rem(tm + nt - 1, nt)

    def remote(src, dst, send, recv, **to):
        return pltpu.make_async_remote_copy(
            src_ref=src, dst_ref=dst, send_sem=send, recv_sem=recv, device_id=to, device_id_type=MESH
        )

    barrier = pltpu.get_barrier_semaphore()

    def greet_fiber(j, c):
        pl.semaphore_signal(
            barrier, inc=1, device_id={"fiber": lax.rem(me + j, nf)}, device_id_type=MESH
        )
        return c

    def greet_tm(j, c):
        pl.semaphore_signal(
            barrier, inc=1, device_id={"tm": lax.rem(tm + j, nt)}, device_id_type=MESH
        )
        return c

    lax.fori_loop(1, nt, greet_tm, 0)
    lax.fori_loop(1, nf, greet_fiber, 0)

    loads = [
        pltpu.make_async_copy(src, dst, load_sem.at[i])
        for i, (src, dst) in enumerate(
            [
                (ana_far, ana_raw),
                (strain_far, strain),
                (outer_far, outer_raw),
                (fwd_far, fwd_raw),
                (inv_far, inv_raw),
                (syn_far, syn_raw),
                (step_far, step),
                (turn_far, turn),
                (cut_far, cut),
                (sta_far, chan.at[0]),
                (lta_far, chan.at[1]),
                (drift_far, chan.at[2]),
                (limit_far, chan.at[3]),
            ]
        )
    ]
    for load in loads:
        load.start()

    def rates(i, at):
        return chan[i, at, :].astype(F32)

    pl.semaphore_wait(barrier, nf - 1 + nt - 1)

    chunks = 4
    wide = ROWS // chunks

    def rim_copy(c):
        span = pl.ds(c * wide * LANES, wide * LANES)
        return remote(strain_far.at[:, span], rim.at[:, span], rim_s.at[c], rim_r.at[c], tm=later)

    for chunk in range(chunks):
        rim_copy(chunk).start()

    for load in loads[:6]:
        load.wait()
    high, low = split(ana_raw[...])
    ana[...] = jnp.concatenate([high, low], axis=0)
    high, low = split(syn_raw[...])
    syn[...] = jnp.concatenate([high, high, low], axis=1)
    for raw, table in ((fwd_raw, fwd), (inv_raw, inv)):
        high, low = split(raw[...])
        table[...] = jnp.concatenate([high, high, low], axis=0)
    high, low = split(outer_raw[...])
    outer[...] = jnp.concatenate([high, high, low], axis=1)

    peak = jnp.zeros((1, 2 * LANES), F32)
    for chunk in range(chunks):
        rim_copy(chunk).wait_recv()
        for q in range(chunk * wide, (chunk + 1) * wide, 2):
            cols = slice(q * LANES, (q + 2) * LANES)
            before = jnp.where(tm > 0, rim[:, cols].astype(F32), 0.0).astype(BF16)
            frame = jnp.concatenate([before, strain[:, cols]], axis=0)
            both = jnp.dot(ana[...], frame, preferred_element_type=F32)
            got = both[:FRAME] + both[FRAME:]
            spec[:, q, :] = got[:, :LANES]
            spec[:, q + 1, :] = got[:, LANES:]
            peak = jnp.maximum(peak, jnp.max(jnp.abs(got), axis=0, keepdims=True))
    peak = peak_of(peak)
    gain = TOP / peak
    scs1[0] = jnp.broadcast_to(peak * (1.0 / TOP), (1, LANES))
    scr1[me] = scs1[0]

    def code1(i, c):
        at = pl.ds(i * 8, 8)
        snd1[at, :, 0:LANES] = coded(spec[at], gain)
        snd1[at, :, LANES : 2 * LANES] = coded(spec[pl.ds(BINS + i * 8, 8)], gain)
        return c

    def scale1(j):
        to = lax.rem(me + j, nf)
        return remote(scs1.at[0], scr1.at[me], c1s.at[j], c1r.at[j], fiber=to)

    def data1(b, j):
        to = lax.rem(me + j, nf)
        return remote(
            snd1.at[to * per + b],
            rcv1.at[b, pl.ds(pl.multiple_of(me * ROWS, ROWS), ROWS), :],
            s1s.at[b, j],
            s1r.at[b, j],
            fiber=to,
        )

    def from1(b, j):
        back = lax.rem(me + nf - j, nf)
        return remote(
            snd1.at[0],
            rcv1.at[b, pl.ds(pl.multiple_of(back * ROWS, ROWS), ROWS), :],
            s1s.at[b, j],
            s1r.at[b, j],
            fiber=back,
        )

    def out_scale(j, c):
        scale1(j).start()
        return c

    lax.fori_loop(1, nf, out_scale, 0)
    lax.fori_loop(0, BINS // 8, code1, 0)

    def out_bins(b, c):
        def out_peer(j, c):
            data1(b, j).start()
            return c

        lax.fori_loop(1, nf, out_peer, 0)
        rcv1[b, pl.ds(pl.multiple_of(me * ROWS, ROWS), ROWS), :] = snd1[me * per + b]
        return c

    lax.fori_loop(0, per, out_bins, 0)

    def in_scale(j, c):
        back = lax.rem(me + nf - j, nf)
        remote(scs1.at[0], scr1.at[back], c1s.at[j], c1r.at[j], fiber=back).wait_recv()
        return c

    lax.fori_loop(1, nf, in_scale, 0)

    for load in loads[6:]:
        load.wait()
    peers = nf // 2

    def scale2(b, blk, to):
        j = lax.rem(to - me + nf, nf)
        return remote(
            scs2.at[b, blk], scr2.at[me * per + b], c2s.at[b, j], c2r.at[b, j], fiber=to
        )

    def data2(b, to):
        j = lax.rem(to - me + nf, nf)
        return remote(
            snd2.at[b, pl.ds(pl.multiple_of(to * ROWS, ROWS), ROWS), :],
            rcv2.at[me * per + b],
            s2s.at[b, j],
            s2r.at[b, j],
            fiber=to,
        )

    lane = lax.broadcasted_iota(jnp.int32, (half, LANES), 1)
    row = lax.broadcasted_iota(jnp.int32, (half, LANES), 0)

    def parts(x):
        return x[:, :LANES], x[:, LANES:]

    def put(ref, e, at, size, x):
        high, low = split(x)
        for i, part in enumerate((high, low, high)):
            ref[e, pl.ds(pl.multiple_of(i * half + at, ROWS), size), :] = part

    def one_bin(b, c):
        def in_peer(j, c):
            from1(b, j).wait_recv()
            return c

        lax.fori_loop(1, nf, in_peer, 0)
        limit_k = cut[me * per + b]

        def values(p):
            x = rcv1[b, pl.ds(pl.multiple_of(p * ROWS, ROWS), ROWS), :].astype(F32)
            return x * jnp.concatenate([scr1[p], scr1[p]], axis=1)

        def decode(g, c):
            for i in range(GROUP):
                p = g * GROUP + i
                at = pl.multiple_of(p * ROWS, ROWS)
                early, late = values(p), values(p + peers)
                wr, wi = parts(step[pl.ds(at, ROWS), :])
                put(x3, 0, at, ROWS, early + late)
                re, im = parts(early - late)
                x = jnp.concatenate([re * wr - im * wi, re * wi + im * wr], axis=1)
                put(x3, 1, at, ROWS, x)
            return c

        lax.fori_loop(0, peers // GROUP, decode, 0)

        for e in range(2):
            pq = jnp.dot(outer[...], x3[e], preferred_element_type=F32)
            pr, pi = parts(pq[:half])
            qr, qi = parts(pq[half:])
            re, im = pr - qi, pi + qr
            tr, ti = parts(turn[e * half : (e + 1) * half, :])
            y = jnp.concatenate([re * tr - im * ti, re * ti + im * tr], axis=1)
            wr, wi = parts(jnp.dot(across(y), fwd[...], preferred_element_type=F32))
            k = 2 * row + e + rows * lane
            keep = jnp.minimum(k, total - k) <= limit_k
            w = jnp.concatenate([jnp.where(keep, wr, 0.0), jnp.where(keep, wi, 0.0)], axis=1)
            re, im = parts(jnp.dot(across(w), inv[...], preferred_element_type=F32))
            put(z3, e, 0, half, jnp.concatenate([re * tr + im * ti, im * tr - re * ti], axis=1))

        back = []
        for e in range(2):
            pq = jnp.dot(outer[...], z3[e], preferred_element_type=F32)
            pr, pi = parts(pq[:half])
            qr, qi = parts(pq[half:])
            back.append((pr + qi, pi - qr))
        (ur, ui), (re, im) = back
        wr, wi = parts(step[...])
        vr, vi = re * wr + im * wi, im * wr - re * wi
        for blk, x in enumerate(
            (jnp.concatenate([ur + vr, ui + vi], axis=1), jnp.concatenate([ur - vr, ui - vi], axis=1))
        ):
            top = peak_of(x)
            scs2[b, blk] = jnp.broadcast_to(top * (1.0 / TOP), (1, LANES))
            snd2[b, blk * half : (blk + 1) * half, :] = coded(x, TOP / top)

        def out_peer(j, c):
            to = lax.rem(me + j, nf)
            scale2(b, to // peers, to).start()
            data2(b, to).start()
            return c

        lax.fori_loop(1, nf, out_peer, 0)
        scr2[me * per + b] = scs2[b, me // peers]
        rcv2[me * per + b] = snd2[b, pl.ds(pl.multiple_of(me * ROWS, ROWS), ROWS), :]
        return c

    lax.fori_loop(0, per, one_bin, 0)

    def in_back(j, c):
        back = lax.rem(me + nf - j, nf)

        def in_bin(b, c):
            f = back * per + b
            remote(scs2.at[0, 0], scr2.at[f], c2s.at[b, j], c2r.at[b, j], fiber=back).wait_recv()
            remote(
                snd2.at[0, pl.ds(0, ROWS), :], rcv2.at[f], s2s.at[b, j], s2r.at[b, j], fiber=back
            ).wait_recv()
            return c

        lax.fori_loop(0, per, in_bin, 0)
        return c

    lax.fori_loop(1, nf, in_back, 0)

    def decode2(i, c):
        at = pl.ds(i * 8, 8)
        x = rcv2[at].astype(F32)
        deco[0, at] = x[:, :, :LANES] * scr2[at]
        deco[1, at] = x[:, :, LANES:] * scr2[at]
        return c

    lax.fori_loop(0, BINS // 8, decode2, 0)

    def spill(c):
        span = pl.ds(c * wide, wide)
        return remote(sps.at[span], spr.at[span], sp_s.at[c], sp_r.at[c], tm=earlier)

    def spill_scale(c):
        return remote(sss.at[c], ssr.at[c], ss_s.at[c], ss_r.at[c], tm=earlier)

    for chunk in range(chunks):
        top = jnp.full((1, 1), 1e-30, F32)
        for q in range(chunk * wide, (chunk + 1) * wide, 2):
            x = jnp.concatenate(
                [
                    jnp.concatenate([deco[0, :, q, :], deco[1, :, q, :]], axis=0),
                    jnp.concatenate([deco[0, :, q + 1, :], deco[1, :, q + 1, :]], axis=0),
                ],
                axis=1,
            )
            high, low = split(x)
            got = jnp.dot(
                syn[...], jnp.concatenate([high, low, high], axis=0), preferred_element_type=F32
            )
            for i in range(2):
                head[q + i] = got[:HOP, i * LANES : (i + 1) * LANES]
                tail[q + i] = got[HOP:, i * LANES : (i + 1) * LANES]
            top = jnp.maximum(top, peak_of(got[:HOP]))
        sss[chunk] = jnp.broadcast_to(top * (1.0 / TOP), (1, LANES))
        spill_scale(chunk).start()
        for q in range(chunk * wide, (chunk + 1) * wide):
            sps[q] = coded(head[q], TOP / top)
        spill(chunk).start()

    has_next = jnp.where(tm < nt - 1, 1.0, 0.0).astype(F32)
    seg_id = lax.broadcasted_iota(jnp.int32, (8, LANES), 0)

    def shifted(x, by, fill):
        return jnp.where(seg_id >= by, pltpu.roll(x, by, 0), fill)

    def rate_of(length):
        return 1.0 - 1.0 / length

    def natural(g, vectors):
        for i in range(8):
            temp[g, pl.ds(i, 8, stride=8), :] = vectors[i]
        return temp[g]

    def grouped(one):
        def group(i, c):
            for g in range(GROUP):
                one(i * GROUP + g, g)
            return c

        return group

    for chunk in range(chunks):
        spill_scale(chunk).wait_recv()
        spill(chunk).wait_recv()

        def scan_row(q, g):
            at = pl.ds(q, 1)
            cols = pl.ds(pl.multiple_of(q * LANES, LANES), LANES)
            heads = spr[q].astype(F32) * (ssr[chunk] * has_next)
            rounded = (tail[q] + heads).astype(BF16).astype(F32)
            part = [rounded[8 * i : 8 * i + 8] for i in range(8)]
            filtered[:, cols] = natural(g, part).astype(BF16)
            energy = [v * v for v in part]
            for s in range(2):
                keep = jnp.broadcast_to(rate_of(rates(s, at)), (8, LANES))
                gain = 1.0 - keep
                level = gain * energy[0]
                lev[s, q, 0:8] = level
                for i in range(1, 8):
                    level = keep * level + gain * energy[i]
                    lev[s, q, 8 * i : 8 * i + 8] = level
                power = keep * keep
                power = power * power
                power = power * power
                for by in (1, 2, 4):
                    level = level + power * shifted(level, by, 0.0)
                    power = power * power
                seg[s, q] = shifted(level, 1, 0.0)
                cars[s, at, :] = level[7:8]

        for g in range(wide):
            scan_row(chunk * wide + g, g)

    stores = [
        pltpu.make_async_copy(src, dst, store_sem.at[i])
        for i, (src, dst) in enumerate([(filtered, filtered_far), (ratio, ratio_far), (ph, ph_far)])
    ]
    stores[0].start()

    def to_later(snd, rcv, send, recv, j):
        return remote(snd, rcv.at[tm], send.at[j], recv.at[j], tm=lax.rem(tm + j, nt))

    def from_earlier(snd, rcv, send, recv, j):
        back = lax.rem(tm + nt - j, nt)
        return remote(snd, rcv.at[back], send.at[j], recv.at[j], tm=back)

    def pass_on(snd, rcv, send, recv):
        def out(j, c):
            to_later(snd, rcv, send, recv, j).start()
            return c

        lax.fori_loop(1, nt - tm, out, 0)

        def come(j, c):
            from_earlier(snd, rcv, send, recv, j).wait_recv()
            return c

        lax.fori_loop(1, tm + 1, come, 0)

    pass_on(cars, carr, ca_s, ca_r)
    decay = []
    for s in range(2):
        power = rate_of(chan[s].astype(F32))
        for _ in range(6):
            power = power * power
        decay.append(power)

    def lap(k, state):
        return tuple(decay[s] * state[s] + carr[k, s] for s in range(2))

    ones = jnp.ones((ROWS, LANES), F32)
    start = lax.fori_loop(0, tm, lap, (ones, ones))
    head[0, 0:ROWS] = start[0]
    head[1, 0:ROWS] = start[1]

    def climb_row(q, g):
        at = pl.ds(q, 1)
        cols = pl.ds(pl.multiple_of(q * LANES, LANES), LANES)
        avg = []
        for s in range(2):
            keep = jnp.broadcast_to(rate_of(rates(s, at)), (8, LANES))
            carry = jnp.broadcast_to(head[s, at, :], (8, LANES))
            power = keep * keep
            power = power * power
            power = power * power
            for bit in (1, 2, 4):
                carry = jnp.where((seg_id // bit) % 2 == 1, carry * power, carry)
                power = power * power
            entry = seg[s, q] + carry
            values = []
            for i in range(8):
                entry = entry * keep
                values.append(lev[s, q, 8 * i : 8 * i + 8] + entry)
            avg.append(values)
        quotient = [avg[0][i] / avg[1][i] for i in range(8)]
        ratio[:, cols] = natural(g, quotient)
        rate = jnp.broadcast_to(0.5 + rates(2, at) * (1.0 / 64.0), (8, LANES))
        climb = quotient[0] - rate
        low = climb
        climbs, lows = [climb], [low]
        for i in range(1, 8):
            climb = climb + (quotient[i] - rate)
            low = jnp.minimum(low, climb)
            climbs.append(climb)
            lows.append(low)
        whole = climb
        for by in (1, 2, 4):
            whole = whole + shifted(whole, by, 0.0)
        base = shifted(whole, 1, 0.0)
        least = base + low
        for by in (1, 2, 4):
            least = jnp.minimum(least, shifted(least, by, jnp.inf))
        floor = shifted(least, 1, jnp.inf)
        for i in range(8):
            up = base + climbs[i]
            lev[0, q, 8 * i : 8 * i + 8] = up
            lev[1, q, 8 * i : 8 * i + 8] = jnp.minimum(floor, base + lows[i])
        sums[0, at, :] = whole[7:8]
        sums[1, at, :] = least[7:8]

    lax.fori_loop(0, ROWS // GROUP, grouped(climb_row), 0)

    stores[1].start()
    pass_on(sums, sumr, su_s, su_r)

    def lap2(k, state):
        total_up, low = state
        return total_up + sumr[k, 0], jnp.minimum(low, total_up + sumr[k, 1])

    zeros = jnp.zeros((ROWS, LANES), F32)
    before, low = lax.fori_loop(0, tm, lap2, (zeros, zeros))
    head[2, 0:ROWS] = before
    head[3, 0:ROWS] = low

    def ph_row(q, g):
        at = pl.ds(q, 1)
        cols = pl.ds(pl.multiple_of(q * LANES, LANES), LANES)
        base = jnp.broadcast_to(head[2, at, :], (8, LANES))
        low = jnp.broadcast_to(head[3, at, :], (8, LANES))
        scale = jnp.broadcast_to(1.0 / rates(3, at), (8, LANES))
        out = []
        for i in range(8):
            climb = base + lev[0, q, 8 * i : 8 * i + 8]
            lowest = jnp.minimum(low, base + lev[1, q, 8 * i : 8 * i + 8])
            out.append((climb - lowest) * scale)
        ph[:, cols] = natural(g, out)

    lax.fori_loop(0, ROWS // GROUP, grouped(ph_row), 0)

    stores[2].start()

    for chunk in range(chunks):
        rim_copy(chunk).wait_send()

    def sent1(j, c):
        scale1(j).wait_send()

        def sent_bin(b, c):
            data1(b, j).wait_send()
            to = lax.rem(me + j, nf)
            scale2(b, 0, to).wait_send()
            data2(b, to).wait_send()
            return c

        lax.fori_loop(0, per, sent_bin, 0)
        return c

    lax.fori_loop(1, nf, sent1, 0)
    for chunk in range(chunks):
        spill_scale(chunk).wait_send()
        spill(chunk).wait_send()

    def sent_on(j, c):
        to_later(sums, carr, ca_s, ca_r, j).wait_send()
        to_later(sums, sumr, su_s, su_r, j).wait_send()
        return c

    lax.fori_loop(1, nt - tm, sent_on, 0)
    for store in stores:
        store.wait()


def hand_over(*refs):
    copies = [pltpu.make_async_copy(refs[i], refs[3 + i], refs[6].at[i]) for i in range(3)]
    for copy in copies:
        copy.start()
    for copy in copies:
        copy.wait()


def body(nf, nt, strain, fan_cut, sta_len, lta_len, drift_code, threshold):
    per = BINS // nf
    rows = nf * ROWS
    total = rows * LANES
    half = rows // 2
    tabs = [jnp.asarray(t) for t in tables(total)]
    per_chan = [v.reshape(ROWS, LANES) for v in (sta_len, lta_len, drift_code, threshold)]
    far = pl.BlockSpec(memory_space=pl.ANY)
    dma = pltpu.SemaphoreType.DMA
    i16 = jnp.int16
    chans = ROWS * LANES
    results = pl.pallas_call(
        functools.partial(kernel, nf, nt),
        out_shape=(
            jax.ShapeDtypeStruct((HOP, chans), BF16),
            jax.ShapeDtypeStruct((HOP, chans), F32),
            jax.ShapeDtypeStruct((HOP, chans), F32),
        ),
        in_specs=[far] * 13,
        out_specs=(far, far, far),
        scratch_shapes=[
            pltpu.VMEM((HOP, chans), BF16),
            pltpu.SMEM((BINS,), jnp.int32),
            pltpu.VMEM((4, ROWS, LANES), jnp.int32),
        ]
        + [pltpu.VMEM(t.shape, F32) for t in tabs]
        + [
            pltpu.VMEM((2 * FRAME, FRAME), BF16),
            pltpu.VMEM((rows, 3 * half), BF16),
            pltpu.VMEM((6 * LANES, 2 * LANES), BF16),
            pltpu.VMEM((6 * LANES, 2 * LANES), BF16),
            pltpu.VMEM((FRAME, 3 * FRAME), BF16),
            pltpu.VMEM((HOP, chans), BF16),
            pltpu.VMEM((HOP, chans), F32),
            pltpu.VMEM((HOP, chans), F32),
            pltpu.VMEM((HOP, chans), BF16),
            pltpu.VMEM((FRAME, ROWS, LANES), F32),
            pltpu.VMEM((BINS, ROWS, 2 * LANES), i16),
            pltpu.VMEM((per, rows, 2 * LANES), i16),
            pltpu.VMEM((1, 1, LANES), F32),
            pltpu.VMEM((nf, 1, LANES), F32),
            pltpu.VMEM((2, 3 * half, 2 * LANES), BF16),
            pltpu.VMEM((2, 3 * half, 2 * LANES), BF16),
            pltpu.VMEM((per, rows, 2 * LANES), i16),
            pltpu.VMEM((BINS, ROWS, 2 * LANES), i16),
            pltpu.VMEM((per, 2, 1, LANES), F32),
            pltpu.VMEM((BINS, 1, LANES), F32),
            pltpu.VMEM((2, BINS, ROWS, LANES), F32),
            pltpu.VMEM((ROWS, HOP, LANES), F32),
            pltpu.VMEM((ROWS, HOP, LANES), F32),
            pltpu.VMEM((ROWS, HOP, LANES), i16),
            pltpu.VMEM((ROWS, HOP, LANES), i16),
            pltpu.VMEM((4, 1, LANES), F32),
            pltpu.VMEM((4, 1, LANES), F32),
            pltpu.VMEM((2, ROWS, HOP, LANES), F32),
            pltpu.VMEM((2, ROWS, 8, LANES), F32),
            pltpu.VMEM((2, ROWS, LANES), F32),
            pltpu.VMEM((nt, 2, ROWS, LANES), F32),
            pltpu.VMEM((2, ROWS, LANES), F32),
            pltpu.VMEM((nt, 2, ROWS, LANES), F32),
            pltpu.VMEM((GROUP, HOP, LANES), F32),
            dma((4,)),
            dma((4,)),
            dma((per, nf)),
            dma((per, nf)),
            dma((nf,)),
            dma((nf,)),
            dma((per, nf)),
            dma((per, nf)),
            dma((per, nf)),
            dma((per, nf)),
            dma((4,)),
            dma((4,)),
            dma((4,)),
            dma((4,)),
            dma((nt,)),
            dma((nt,)),
            dma((nt,)),
            dma((nt,)),
            dma((13,)),
            dma((3,)),
        ],
        compiler_params=pltpu.CompilerParams(
            collective_id=0, has_side_effects=True, vmem_limit_bytes=64 * 1024 * 1024
        ),
    )(strain, fan_cut, *per_chan, *tabs)
    return pl.pallas_call(
        hand_over,
        out_shape=tuple(jax.ShapeDtypeStruct(r.shape, r.dtype) for r in results),
        in_specs=[far] * 3,
        out_specs=(far,) * 3,
        scratch_shapes=[dma((3,))],
        compiler_params=pltpu.CompilerParams(vmem_limit_bytes=64 * 1024 * 1024),
    )(*results)


def solution(mesh):
    return jax.shard_map(
        functools.partial(body, mesh.shape["fiber"], mesh.shape["tm"]),
        mesh=mesh,
        in_specs=(P("tm", "fiber"), P(), P("fiber"), P("fiber"), P("fiber"), P("fiber")),
        out_specs=(P("tm", "fiber"), P("tm", "fiber"), P("tm", "fiber")),
        check_vma=False,
    )
```

```python
import functools
import math

import jax
import jax.numpy as jnp
import numpy as np
from jax import lax
from jax.experimental import pallas as pl
from jax.experimental.pallas import tpu as pltpu
from jax.sharding import PartitionSpec as P

FRAME = 128
HOP = 64
BINS = 64
LANES = 128
ROWS = 16
GROUP = 4
TOP = 32512.0
MESH = pl.DeviceIdType.MESH
F32 = jnp.float32
BF16 = jnp.bfloat16


def time_order():
    rows = np.arange(HOP)
    return 8 * (rows % 8) + rows // 8


def tables(total):
    rows = total // LANES
    half = rows // 2
    n = np.arange(FRAME)
    f = np.arange(BINS)
    angle = 2.0 * math.pi / FRAME * ((f[:, None] * n[None, :]) % FRAME)
    window = 0.5 - 0.5 * np.cos(2.0 * math.pi / FRAME * n)
    analysis = np.concatenate([window * np.cos(angle), -window * np.sin(angle)], 0)
    weight = np.where(f == 0, 1.0, 2.0)[:, None] / FRAME
    synthesis = np.concatenate([weight * np.cos(angle), -weight * np.sin(angle)], 0).T
    order = time_order()
    synthesis = synthesis[np.concatenate([order, HOP + order])]
    a = np.arange(half)
    outer = 2.0 * math.pi / half * ((a[:, None] * a[None, :]) % half)
    outer = np.concatenate([np.cos(outer), -np.sin(outer)], 0)
    step = np.broadcast_to(2.0 * math.pi / rows * a[:, None], (half, LANES))
    step = np.concatenate([np.cos(step), -np.sin(step)], 1)
    b = np.arange(LANES)
    wave = np.concatenate([2 * a, 2 * a + 1])
    turn = 2.0 * math.pi / total * ((wave[:, None] * b[None, :]) % total)
    turn = np.concatenate([np.cos(turn), -np.sin(turn)], 1)
    inner = 2.0 * math.pi / LANES * ((b[:, None] * b[None, :]) % LANES)
    cos, sin = np.cos(inner), np.sin(inner)
    forward = np.block([[cos, -sin], [sin, cos]])
    inverse = np.block([[cos, sin], [-sin, cos]]) / total
    return [t.astype(np.float32) for t in (analysis, outer, forward, inverse, synthesis, step, turn)]


def split(x):
    high = x.astype(BF16)
    return high, (x - high.astype(F32)).astype(BF16)


def across(x):
    high, low = split(x)
    return jnp.concatenate([high, low, high], axis=1)


def peak_of(x):
    top = jnp.max(jnp.max(jnp.abs(x), axis=0, keepdims=True), axis=1, keepdims=True)
    return jnp.maximum(top, 1e-30)


def in_order(temp, g, vectors):
    for i in range(8):
        temp[g, pl.ds(i, 8, stride=8), :] = vectors[i]
    return temp[g]


def coded(x, gain):
    return jnp.round(x * gain).astype(jnp.int32).astype(jnp.int16)


def kernel(
    nf,
    nt,
    *refs,
):
    (
        strain_far,
        cut_far,
        sta_far,
        lta_far,
        drift_far,
        ana_far,
        outer_far,
        fwd_far,
        inv_far,
        syn_far,
        step_far,
        turn_far,
        filtered_far,
        ratio_far,
        lev_far,
        prior_far,
        strain,
        cut,
        chan,
        ana_raw,
        outer_raw,
        fwd_raw,
        inv_raw,
        syn_raw,
        step,
        turn,
        ana,
        outer,
        fwd,
        inv,
        syn,
        filtered,
        ratio,
        rim,
        spec,
        snd1,
        rcv1,
        scs1,
        scr1,
        x3,
        z3,
        snd2,
        rcv2,
        scs2,
        scr2,
        deco,
        head,
        tail,
        sps,
        spr,
        sss,
        ssr,
        lev,
        seg,
        cars,
        carr,
        sums,
        sumr,
        temp,
        rim_s,
        rim_r,
        s1s,
        s1r,
        c1s,
        c1r,
        s2s,
        s2r,
        c2s,
        c2r,
        sp_s,
        sp_r,
        ss_s,
        ss_r,
        ca_s,
        ca_r,
        su_s,
        su_r,
        load_sem,
        store_sem,
    ) = refs
    me = lax.axis_index("fiber")
    tm = lax.axis_index("tm")
    per = BINS // nf
    rows = nf * ROWS
    half = rows // 2
    total = rows * LANES
    later, earlier = lax.rem(tm + 1, nt), lax.rem(tm + nt - 1, nt)

    def remote(src, dst, send, recv, **to):
        return pltpu.make_async_remote_copy(
            src_ref=src, dst_ref=dst, send_sem=send, recv_sem=recv, device_id=to, device_id_type=MESH
        )

    barrier = pltpu.get_barrier_semaphore()

    def greet_fiber(j, c):
        pl.semaphore_signal(
            barrier, inc=1, device_id={"fiber": lax.rem(me + j, nf)}, device_id_type=MESH
        )
        return c

    def greet_tm(j, c):
        pl.semaphore_signal(
            barrier, inc=1, device_id={"tm": lax.rem(tm + j, nt)}, device_id_type=MESH
        )
        return c

    lax.fori_loop(1, nt, greet_tm, 0)
    lax.fori_loop(1, nf, greet_fiber, 0)

    loads = [
        pltpu.make_async_copy(src, dst, load_sem.at[i])
        for i, (src, dst) in enumerate(
            [
                (ana_far, ana_raw),
                (strain_far, strain),
                (outer_far, outer_raw),
                (fwd_far, fwd_raw),
                (inv_far, inv_raw),
                (syn_far, syn_raw),
                (step_far, step),
                (turn_far, turn),
                (cut_far, cut),
                (sta_far, chan.at[0]),
                (lta_far, chan.at[1]),
                (drift_far, chan.at[2]),
            ]
        )
    ]
    for load in loads:
        load.start()

    def rates(i, at):
        return chan[i, at, :].astype(F32)

    pl.semaphore_wait(barrier, nf - 1 + nt - 1)

    chunks = 4
    wide = ROWS // chunks

    def rim_copy(c):
        span = pl.ds(c * wide * LANES, wide * LANES)
        return remote(strain_far.at[:, span], rim.at[:, span], rim_s.at[c], rim_r.at[c], tm=later)

    for chunk in range(chunks):
        rim_copy(chunk).start()

    for load in loads[:6]:
        load.wait()
    high, low = split(ana_raw[...])
    ana[...] = jnp.concatenate([high, low], axis=0)
    high, low = split(syn_raw[...])
    syn[...] = jnp.concatenate([high, high, low], axis=1)
    for raw, table in ((fwd_raw, fwd), (inv_raw, inv)):
        high, low = split(raw[...])
        table[...] = jnp.concatenate([high, high, low], axis=0)
    high, low = split(outer_raw[...])
    outer[...] = jnp.concatenate([high, high, low], axis=1)

    tall = ROWS // 2

    def scale1(h, j):
        to = lax.rem(me + j, nf)
        return remote(scs1.at[h], scr1.at[h, me], c1s.at[h, j], c1r.at[h, j], fiber=to)

    def data1(i, j):
        to = lax.rem(me + j, nf)
        if i == 0:
            src, dst = snd1.at[0, pl.ds(to * per, per)], rcv1.at[0, me]
        else:
            src, dst = snd1.at[1, to * per + i - 1], rcv1.at[1, me, i - 1]
        return remote(src, dst, s1s.at[i, j], s1r.at[i, j], fiber=to)

    def from1(i, j):
        back = lax.rem(me + nf - j, nf)
        if i == 0:
            src, dst = snd1.at[0, pl.ds(0, per)], rcv1.at[0, back]
        else:
            src, dst = snd1.at[1, 0], rcv1.at[1, back, i - 1]
        return remote(src, dst, s1s.at[i, j], s1r.at[i, j], fiber=back)

    def each_peer(act):
        def one(j, c):
            act(j)
            return c

        lax.fori_loop(1, nf, one, 0)

    for h in range(2):
        peak = jnp.zeros((1, 2 * LANES), F32)
        for chunk in range(h * chunks // 2, (h + 1) * chunks // 2):
            rim_copy(chunk).wait_recv()
            for q in range(chunk * wide, (chunk + 1) * wide, 2):
                cols = slice(q * LANES, (q + 2) * LANES)
                before = jnp.where(tm > 0, rim[:, cols].astype(F32), 0.0).astype(BF16)
                frame = jnp.concatenate([before, strain[:, cols]], axis=0)
                both = jnp.dot(ana[...], frame, preferred_element_type=F32)
                got = both[:FRAME] + both[FRAME:]
                spec[:, q, :] = got[:, :LANES]
                spec[:, q + 1, :] = got[:, LANES:]
                peak = jnp.maximum(peak, jnp.max(jnp.abs(got), axis=0, keepdims=True))
        peak = peak_of(peak)
        gain = TOP / peak
        scs1[h] = jnp.broadcast_to(peak * (1.0 / TOP), (1, LANES))
        scr1[h, me] = scs1[h]

        def code1(i, c):
            half_rows = slice(h * tall, (h + 1) * tall)
            re = spec[pl.ds(i * 8, 8), half_rows, :]
            im = spec[pl.ds(BINS + i * 8, 8), half_rows, :]
            snd1[h, pl.ds(i * 8, 8)] = coded(jnp.concatenate([re, im], axis=1), gain)
            return c

        lax.fori_loop(0, BINS // 8, code1, 0)
        if h == 0:

            def send0(j):
                scale1(0, j).start()
                data1(0, j).start()

            each_peer(send0)
        else:

            def send1(j):
                scale1(1, j).start()
                data1(1, j).start()

            each_peer(send1)
            for b in range(1, per):
                each_peer(lambda j: data1(1 + b, j).start())
        rcv1[h, me] = snd1[h, pl.ds(me * per, per)]

    def first_scales(j):
        back = lax.rem(me + nf - j, nf)
        for h in range(2):
            remote(
                scs1.at[h], scr1.at[h, back], c1s.at[h, j], c1r.at[h, j], fiber=back
            ).wait_recv()

    each_peer(lambda j: from1(0, j).wait_recv())

    for load in loads[6:]:
        load.wait()
    peers = nf // 2

    final = per - 1

    def scale2(b, j):
        to = lax.rem(me + j, nf)
        return remote(
            scs2.at[b, to // peers], scr2.at[me * per + b], c2s.at[b, j], c2r.at[b, j], fiber=to
        )

    def data2(i, j):
        to = lax.rem(me + j, nf)
        if i < final:
            src, dst = snd2.at[i, to], rcv2.at[me * per + i]
        else:
            src, dst = snd2.at[final, to, i - final], rcv2.at[me * per + final, i - final]
        return remote(src, dst, s2s.at[i, j], s2r.at[i, j], fiber=to)

    def from2(i, j):
        back = lax.rem(me + nf - j, nf)
        if i < final:
            src, dst = snd2.at[i, 0], rcv2.at[back * per + i]
        else:
            src, dst = snd2.at[final, 0, 0], rcv2.at[back * per + final, i - final]
        return remote(src, dst, s2s.at[i, j], s2r.at[i, j], fiber=back)

    lane = lax.broadcasted_iota(jnp.int32, (half, LANES), 1)
    row = lax.broadcasted_iota(jnp.int32, (half, LANES), 0)

    def parts(x):
        return x[:, :LANES], x[:, LANES:]

    def put(ref, e, at, size, x):
        high, low = split(x)
        for i, part in enumerate((high, low, high)):
            ref[e, pl.ds(pl.multiple_of(i * half + at, ROWS), size), :] = part

    for b in range(per):
        if b == 0:
            each_peer(first_scales)
        each_peer(lambda j: from1(1 + b, j).wait_recv())
        limit_k = cut[me * per + b]

        def values(p):
            pieces = [rcv1[h, p, b].astype(F32) * scr1[h, p] for h in range(2)]
            return jnp.concatenate(
                [jnp.concatenate([x[i * tall : (i + 1) * tall] for x in pieces], 0) for i in range(2)],
                axis=1,
            )

        def decode(g, c):
            for i in range(GROUP):
                p = g * GROUP + i
                at = pl.multiple_of(p * ROWS, ROWS)
                early, late = values(p), values(p + peers)
                wr, wi = parts(step[pl.ds(at, ROWS), :])
                put(x3, 0, at, ROWS, early + late)
                re, im = parts(early - late)
                x = jnp.concatenate([re * wr - im * wi, re * wi + im * wr], axis=1)
                put(x3, 1, at, ROWS, x)
            return c

        lax.fori_loop(0, peers // GROUP, decode, 0)

        for e in range(2):
            pq = jnp.dot(outer[...], x3[e], preferred_element_type=F32)
            pr, pi = parts(pq[:half])
            qr, qi = parts(pq[half:])
            re, im = pr - qi, pi + qr
            tr, ti = parts(turn[e * half : (e + 1) * half, :])
            y = jnp.concatenate([re * tr - im * ti, re * ti + im * tr], axis=1)
            wr, wi = parts(jnp.dot(across(y), fwd[...], preferred_element_type=F32))
            k = 2 * row + e + rows * lane
            keep = jnp.minimum(k, total - k) <= limit_k
            w = jnp.concatenate([jnp.where(keep, wr, 0.0), jnp.where(keep, wi, 0.0)], axis=1)
            re, im = parts(jnp.dot(across(w), inv[...], preferred_element_type=F32))
            put(z3, e, 0, half, jnp.concatenate([re * tr + im * ti, im * tr - re * ti], axis=1))

        back = []
        for e in range(2):
            pq = jnp.dot(outer[...], z3[e], preferred_element_type=F32)
            pr, pi = parts(pq[:half])
            qr, qi = parts(pq[half:])
            back.append((pr + qi, pi - qr))
        (ur, ui), (re, im) = back
        wr, wi = parts(step[...])
        vr, vi = re * wr + im * wi, im * wr - re * wi
        for blk, (re, im) in enumerate(((ur + vr, ui + vi), (ur - vr, ui - vi))):
            top = peak_of(jnp.maximum(jnp.abs(re), jnp.abs(im)))
            scs2[b, blk] = jnp.broadcast_to(top * (1.0 / TOP), (1, LANES))
            re = re.reshape(peers, 2, tall, LANES)
            im = im.reshape(peers, 2, tall, LANES)
            code = coded(jnp.concatenate([re, im], axis=2), TOP / top)
            snd2[b, blk * peers : (blk + 1) * peers] = code

        def send2(j):
            scale2(b, j).start()
            data2(b, j).start()

        each_peer(send2)
        if b == final:
            each_peer(lambda j: data2(per, j).start())
        scr2[me * per + b] = scs2[b, me // peers]
        rcv2[me * per + b] = snd2[b, me]

    def second_scales(j):
        back = lax.rem(me + nf - j, nf)
        for b in range(per):
            remote(
                scs2.at[0, 0], scr2.at[back * per + b], c2s.at[b, j], c2r.at[b, j], fiber=back
            ).wait_recv()

    def back_again(h):
        if h == 0:
            for i in range(per):
                each_peer(lambda j: from2(i, j).wait_recv())
            each_peer(second_scales)
        else:
            each_peer(lambda j: from2(per, j).wait_recv())

        def decode2(i, c):
            at = pl.ds(i * 8, 8)
            x = rcv2[at, h].astype(F32) * scr2[at]
            deco[0, at, h * tall : (h + 1) * tall] = x[:, :tall]
            deco[1, at, h * tall : (h + 1) * tall] = x[:, tall:]
            return c

        lax.fori_loop(0, BINS // 8, decode2, 0)

    def spill(c):
        span = pl.ds(c * wide, wide)
        return remote(sps.at[span], spr.at[span], sp_s.at[c], sp_r.at[c], tm=earlier)

    def spill_scale(c):
        return remote(sss.at[c], ssr.at[c], ss_s.at[c], ss_r.at[c], tm=earlier)

    for chunk in range(chunks):
        if chunk % (chunks // 2) == 0:
            back_again(chunk // (chunks // 2))
        top = jnp.full((1, 1), 1e-30, F32)
        for q in range(chunk * wide, (chunk + 1) * wide, 2):
            x = jnp.concatenate(
                [
                    jnp.concatenate([deco[0, :, q, :], deco[1, :, q, :]], axis=0),
                    jnp.concatenate([deco[0, :, q + 1, :], deco[1, :, q + 1, :]], axis=0),
                ],
                axis=1,
            )
            high, low = split(x)
            got = jnp.dot(
                syn[...], jnp.concatenate([high, low, high], axis=0), preferred_element_type=F32
            )
            for i in range(2):
                head[q + i] = got[:HOP, i * LANES : (i + 1) * LANES]
                tail[q + i] = got[HOP:, i * LANES : (i + 1) * LANES]
            top = jnp.maximum(top, peak_of(got[:HOP]))
        sss[chunk] = jnp.broadcast_to(top * (1.0 / TOP), (1, LANES))
        spill_scale(chunk).start()
        for q in range(chunk * wide, (chunk + 1) * wide):
            sps[q] = coded(head[q], TOP / top)
        spill(chunk).start()

    has_next = jnp.where(tm < nt - 1, 1.0, 0.0).astype(F32)
    seg_id = lax.broadcasted_iota(jnp.int32, (8, LANES), 0)

    def shifted(x, by, fill):
        return jnp.where(seg_id >= by, pltpu.roll(x, by, 0), fill)

    def rate_of(length):
        return 1.0 - 1.0 / length

    def natural(g, vectors):
        return in_order(temp, g, vectors)

    def grouped(one):
        def group(i, c):
            for g in range(GROUP):
                one(i * GROUP + g, g)
            return c

        return group

    for chunk in range(chunks):
        spill_scale(chunk).wait_recv()
        spill(chunk).wait_recv()

        def scan_row(q, g):
            at = pl.ds(q, 1)
            cols = pl.ds(pl.multiple_of(q * LANES, LANES), LANES)
            heads = spr[q].astype(F32) * (ssr[chunk] * has_next)
            rounded = (tail[q] + heads).astype(BF16).astype(F32)
            part = [rounded[8 * i : 8 * i + 8] for i in range(8)]
            filtered[:, cols] = natural(g, part).astype(BF16)
            energy = [v * v for v in part]
            for s in range(2):
                keep = jnp.broadcast_to(rate_of(rates(s, at)), (8, LANES))
                gain = 1.0 - keep
                level = gain * energy[0]
                lev[s, q, 0:8] = level
                for i in range(1, 8):
                    level = keep * level + gain * energy[i]
                    lev[s, q, 8 * i : 8 * i + 8] = level
                power = keep * keep
                power = power * power
                power = power * power
                for by in (1, 2, 4):
                    level = level + power * shifted(level, by, 0.0)
                    power = power * power
                seg[s, q] = shifted(level, 1, 0.0)
                cars[s, at, :] = level[7:8]

        for g in range(wide):
            scan_row(chunk * wide + g, g)

    stores = [
        pltpu.make_async_copy(src, dst, store_sem.at[i])
        for i, (src, dst) in enumerate([(filtered, filtered_far), (ratio, ratio_far), (lev, lev_far)])
    ]
    stores[0].start()

    def to_later(snd, rcv, send, recv, j):
        return remote(snd, rcv.at[tm], send.at[j], recv.at[j], tm=lax.rem(tm + j, nt))

    def from_earlier(snd, rcv, send, recv, j):
        back = lax.rem(tm + nt - j, nt)
        return remote(snd, rcv.at[back], send.at[j], recv.at[j], tm=back)

    def pass_on(snd, rcv, send, recv):
        def out(j, c):
            to_later(snd, rcv, send, recv, j).start()
            return c

        lax.fori_loop(1, nt - tm, out, 0)

        def come(j, c):
            from_earlier(snd, rcv, send, recv, j).wait_recv()
            return c

        lax.fori_loop(1, tm + 1, come, 0)

    pass_on(cars, carr, ca_s, ca_r)
    decay = []
    for s in range(2):
        power = rate_of(chan[s].astype(F32))
        for _ in range(6):
            power = power * power
        decay.append(power)

    def lap(k, state):
        return tuple(decay[s] * state[s] + carr[k, s] for s in range(2))

    ones = jnp.ones((ROWS, LANES), F32)
    start = lax.fori_loop(0, tm, lap, (ones, ones))
    head[0, 0:ROWS] = start[0]
    head[1, 0:ROWS] = start[1]

    def climb_row(q, g):
        at = pl.ds(q, 1)
        cols = pl.ds(pl.multiple_of(q * LANES, LANES), LANES)
        avg = []
        for s in range(2):
            keep = jnp.broadcast_to(rate_of(rates(s, at)), (8, LANES))
            carry = jnp.broadcast_to(head[s, at, :], (8, LANES))
            power = keep * keep
            power = power * power
            power = power * power
            for bit in (1, 2, 4):
                carry = jnp.where((seg_id // bit) % 2 == 1, carry * power, carry)
                power = power * power
            entry = seg[s, q] + carry
            values = []
            for i in range(8):
                entry = entry * keep
                values.append(lev[s, q, 8 * i : 8 * i + 8] + entry)
            avg.append(values)
        quotient = [avg[0][i] / avg[1][i] for i in range(8)]
        ratio[:, cols] = natural(g, quotient)
        rate = jnp.broadcast_to(0.5 + rates(2, at) * (1.0 / 64.0), (8, LANES))
        climb = quotient[0] - rate
        low = climb
        climbs, lows = [climb], [low]
        for i in range(1, 8):
            climb = climb + (quotient[i] - rate)
            low = jnp.minimum(low, climb)
            climbs.append(climb)
            lows.append(low)
        whole = climb
        for by in (1, 2, 4):
            whole = whole + shifted(whole, by, 0.0)
        base = shifted(whole, 1, 0.0)
        least = base + low
        for by in (1, 2, 4):
            least = jnp.minimum(least, shifted(least, by, jnp.inf))
        floor = shifted(least, 1, jnp.inf)
        for i in range(8):
            up = base + climbs[i]
            lev[0, q, 8 * i : 8 * i + 8] = up
            lev[1, q, 8 * i : 8 * i + 8] = jnp.minimum(floor, base + lows[i])
        sums[0, at, :] = whole[7:8]
        sums[1, at, :] = least[7:8]

    lax.fori_loop(0, ROWS // GROUP, grouped(climb_row), 0)

    stores[1].start()
    stores[2].start()
    pass_on(sums, sumr, su_s, su_r)

    def lap2(k, state):
        total_up, low = state
        return total_up + sumr[k, 0], jnp.minimum(low, total_up + sumr[k, 1])

    zeros = jnp.zeros((ROWS, LANES), F32)
    before, low = lax.fori_loop(0, tm, lap2, (zeros, zeros))
    head[2, 0:ROWS] = before
    head[3, 0:ROWS] = low
    last = pltpu.make_async_copy(head.at[pl.ds(2, 2), pl.ds(0, ROWS), :], prior_far, store_sem.at[3])
    last.start()

    for chunk in range(chunks):
        rim_copy(chunk).wait_send()

    def all_sent(j):
        for h in range(2):
            scale1(h, j).wait_send()
        for b in range(per):
            scale2(b, j).wait_send()
        for i in range(per + 1):
            data1(i, j).wait_send()
            data2(i, j).wait_send()

    each_peer(all_sent)
    for chunk in range(chunks):
        spill_scale(chunk).wait_send()
        spill(chunk).wait_send()

    def sent_on(j, c):
        to_later(sums, carr, ca_s, ca_r, j).wait_send()
        to_later(sums, sumr, su_s, su_r, j).wait_send()
        return c

    lax.fori_loop(1, nt - tm, sent_on, 0)
    for store in stores:
        store.wait()
    last.wait()


def finish(
    filtered_far,
    ratio_far,
    lev_far,
    prior_far,
    limit_far,
    filtered_out,
    ratio_out,
    ph_out,
    filtered,
    ratio,
    lev,
    prior,
    limit,
    ph,
    temp,
    load_sem,
    store_sem,
):
    groups = ROWS // GROUP
    loads = [
        pltpu.make_async_copy(src, dst, load_sem.at[i])
        for i, (src, dst) in enumerate(
            [(prior_far, prior), (limit_far, limit), (filtered_far, filtered), (ratio_far, ratio)]
            + [(lev_far.at[:, pl.ds(4 * i, 4)], lev.at[:, pl.ds(4 * i, 4)]) for i in range(groups)]
        )
    ]
    for i in (0, 1, 4, 5, 6, 7, 2, 3):
        loads[i].start()
    stores = [
        pltpu.make_async_copy(filtered, filtered_out, store_sem.at[0]),
        pltpu.make_async_copy(ratio, ratio_out, store_sem.at[1]),
    ]
    loads[0].wait()
    loads[1].wait()
    for i in range(groups):
        loads[4 + i].wait()
        for g in range(GROUP):
            q = i * GROUP + g
            base = jnp.broadcast_to(prior[0, q : q + 1, :], (8, LANES))
            low = jnp.broadcast_to(prior[1, q : q + 1, :], (8, LANES))
            scale = jnp.broadcast_to(1.0 / limit[q : q + 1, :].astype(F32), (8, LANES))
            out = []
            for k in range(8):
                climb = base + lev[0, q, 8 * k : 8 * k + 8]
                lowest = jnp.minimum(low, base + lev[1, q, 8 * k : 8 * k + 8])
                out.append((climb - lowest) * scale)
            ph[:, q * LANES : (q + 1) * LANES] = in_order(temp, g, out)
        span = pl.ds(i * GROUP * LANES, GROUP * LANES)
        stores.append(
            pltpu.make_async_copy(ph.at[:, span], ph_out.at[:, span], store_sem.at[2 + i])
        )
        stores[-1].start()
        if i < 2:
            loads[2 + i].wait()
            stores[i].start()
    for store in stores:
        store.wait()


def body(nf, nt, strain, fan_cut, sta_len, lta_len, drift_code, threshold):
    per = BINS // nf
    rows = nf * ROWS
    total = rows * LANES
    half = rows // 2
    tabs = [jnp.asarray(t) for t in tables(total)]
    per_chan = [v.reshape(ROWS, LANES) for v in (sta_len, lta_len, drift_code, threshold)]
    far = pl.BlockSpec(memory_space=pl.ANY)
    dma = pltpu.SemaphoreType.DMA
    i16 = jnp.int16
    chans = ROWS * LANES
    results = pl.pallas_call(
        functools.partial(kernel, nf, nt),
        out_shape=(
            jax.ShapeDtypeStruct((HOP, chans), BF16),
            jax.ShapeDtypeStruct((HOP, chans), F32),
            jax.ShapeDtypeStruct((2, ROWS, HOP, LANES), F32),
            jax.ShapeDtypeStruct((2, ROWS, LANES), F32),
        ),
        in_specs=[far] * 12,
        out_specs=(far,) * 4,
        scratch_shapes=[
            pltpu.VMEM((HOP, chans), BF16),
            pltpu.SMEM((BINS,), jnp.int32),
            pltpu.VMEM((3, ROWS, LANES), jnp.int32),
        ]
        + [pltpu.VMEM(t.shape, F32) for t in tabs]
        + [
            pltpu.VMEM((2 * FRAME, FRAME), BF16),
            pltpu.VMEM((rows, 3 * half), BF16),
            pltpu.VMEM((6 * LANES, 2 * LANES), BF16),
            pltpu.VMEM((6 * LANES, 2 * LANES), BF16),
            pltpu.VMEM((FRAME, 3 * FRAME), BF16),
            pltpu.VMEM((HOP, chans), BF16),
            pltpu.VMEM((HOP, chans), F32),
            pltpu.VMEM((HOP, chans), BF16),
            pltpu.VMEM((FRAME, ROWS, LANES), F32),
            pltpu.VMEM((2, BINS, ROWS, LANES), i16),
            pltpu.VMEM((2, nf, per, ROWS, LANES), i16),
            pltpu.VMEM((2, 1, LANES), F32),
            pltpu.VMEM((2, nf, 1, LANES), F32),
            pltpu.VMEM((2, 3 * half, 2 * LANES), BF16),
            pltpu.VMEM((2, 3 * half, 2 * LANES), BF16),
            pltpu.VMEM((per, nf, 2, ROWS, LANES), i16),
            pltpu.VMEM((BINS, 2, ROWS, LANES), i16),
            pltpu.VMEM((per, 2, 1, LANES), F32),
            pltpu.VMEM((BINS, 1, LANES), F32),
            pltpu.VMEM((2, BINS, ROWS, LANES), F32),
            pltpu.VMEM((ROWS, HOP, LANES), F32),
            pltpu.VMEM((ROWS, HOP, LANES), F32),
            pltpu.VMEM((ROWS, HOP, LANES), i16),
            pltpu.VMEM((ROWS, HOP, LANES), i16),
            pltpu.VMEM((4, 1, LANES), F32),
            pltpu.VMEM((4, 1, LANES), F32),
            pltpu.VMEM((2, ROWS, HOP, LANES), F32),
            pltpu.VMEM((2, ROWS, 8, LANES), F32),
            pltpu.VMEM((2, ROWS, LANES), F32),
            pltpu.VMEM((nt, 2, ROWS, LANES), F32),
            pltpu.VMEM((2, ROWS, LANES), F32),
            pltpu.VMEM((nt, 2, ROWS, LANES), F32),
            pltpu.VMEM((GROUP, HOP, LANES), F32),
            dma((4,)),
            dma((4,)),
            dma((per + 1, nf)),
            dma((per + 1, nf)),
            dma((2, nf)),
            dma((2, nf)),
            dma((per + 1, nf)),
            dma((per + 1, nf)),
            dma((per, nf)),
            dma((per, nf)),
            dma((4,)),
            dma((4,)),
            dma((4,)),
            dma((4,)),
            dma((nt,)),
            dma((nt,)),
            dma((nt,)),
            dma((nt,)),
            dma((12,)),
            dma((4,)),
        ],
        compiler_params=pltpu.CompilerParams(
            collective_id=0, has_side_effects=True, vmem_limit_bytes=64 * 1024 * 1024
        ),
    )(strain, fan_cut, *per_chan[:3], *tabs)
    return pl.pallas_call(
        finish,
        out_shape=(
            jax.ShapeDtypeStruct((HOP, chans), BF16),
            jax.ShapeDtypeStruct((HOP, chans), F32),
            jax.ShapeDtypeStruct((HOP, chans), F32),
        ),
        in_specs=[far] * 5,
        out_specs=(far,) * 3,
        scratch_shapes=[
            pltpu.VMEM((HOP, chans), BF16),
            pltpu.VMEM((HOP, chans), F32),
            pltpu.VMEM((2, ROWS, HOP, LANES), F32),
            pltpu.VMEM((2, ROWS, LANES), F32),
            pltpu.VMEM((ROWS, LANES), jnp.int32),
            pltpu.VMEM((HOP, chans), F32),
            pltpu.VMEM((GROUP, HOP, LANES), F32),
            dma((8,)),
            dma((6,)),
        ],
        compiler_params=pltpu.CompilerParams(vmem_limit_bytes=64 * 1024 * 1024),
    )(*results, per_chan[3])


def solution(mesh):
    return jax.shard_map(
        functools.partial(body, mesh.shape["fiber"], mesh.shape["tm"]),
        mesh=mesh,
        in_specs=(P("tm", "fiber"), P(), P("fiber"), P("fiber"), P("fiber"), P("fiber")),
        out_specs=(P("tm", "fiber"), P("tm", "fiber"), P("tm", "fiber")),
        check_vma=False,
    )
```

```python
import functools
import math

import jax
import jax.numpy as jnp
import numpy as np
from jax import lax
from jax.experimental import pallas as pl
from jax.experimental.pallas import tpu as pltpu
from jax.sharding import PartitionSpec as P

FRAME = 128
HOP = 64
BINS = 64
LANES = 128
ROWS = 16
GROUP = 4
TOP = 32512.0
MESH = pl.DeviceIdType.MESH
F32 = jnp.float32
BF16 = jnp.bfloat16


def time_order():
    rows = np.arange(HOP)
    return 8 * (rows % 8) + rows // 8


def tables(total):
    rows = total // LANES
    nf = rows // ROWS
    half = rows // 2
    n = np.arange(FRAME)
    f = np.arange(BINS)
    angle = 2.0 * math.pi / FRAME * ((f[:, None] * n[None, :]) % FRAME)
    window = 0.5 - 0.5 * np.cos(2.0 * math.pi / FRAME * n)
    analysis = np.concatenate([window * np.cos(angle), -window * np.sin(angle)], 0)
    weight = np.where(f == 0, 1.0, 2.0)[:, None] / FRAME
    synthesis = np.concatenate([weight * np.cos(angle), -weight * np.sin(angle)], 0).T
    order = time_order()
    arrived = np.arange(BINS).reshape(nf, BINS // nf).T.reshape(-1)
    synthesis = synthesis[np.concatenate([order, HOP + order])]
    synthesis = synthesis[:, np.concatenate([arrived, BINS + arrived])]
    a = np.arange(half)
    outer = 2.0 * math.pi / half * ((a[:, None] * a[None, :]) % half)
    outer = np.concatenate([np.cos(outer), -np.sin(outer)], 0)
    step = np.broadcast_to(2.0 * math.pi / rows * a[:, None], (half, LANES))
    step = np.concatenate([np.cos(step), -np.sin(step)], 1)
    b = np.arange(LANES)
    wave = np.concatenate([2 * a, 2 * a + 1])
    turn = 2.0 * math.pi / total * ((wave[:, None] * b[None, :]) % total)
    turn = np.concatenate([np.cos(turn), -np.sin(turn)], 1)
    inner = 2.0 * math.pi / LANES * ((b[:, None] * b[None, :]) % LANES)
    cos, sin = np.cos(inner), np.sin(inner)
    forward = np.block([[cos, -sin], [sin, cos]])
    inverse = np.block([[cos, sin], [-sin, cos]]) / total
    return [t.astype(np.float32) for t in (analysis, outer, forward, inverse, synthesis, step, turn)]


def split(x):
    high = x.astype(BF16)
    return high, (x - high.astype(F32)).astype(BF16)


def across(x):
    high, low = split(x)
    return jnp.concatenate([high, low, high], axis=1)


def peak_of(x):
    top = jnp.max(jnp.max(jnp.abs(x), axis=0, keepdims=True), axis=1, keepdims=True)
    return jnp.maximum(top, 1e-30)


def in_order(temp, g, vectors):
    for i in range(8):
        temp[g, pl.ds(i, 8, stride=8), :] = vectors[i]
    return temp[g]


def coded(x, gain):
    return jnp.round(x * gain).astype(jnp.int32).astype(jnp.int16)


def kernel(
    nf,
    nt,
    *refs,
):
    (
        strain_far,
        cut_far,
        sta_far,
        lta_far,
        drift_far,
        ana_far,
        outer_far,
        fwd_far,
        inv_far,
        syn_far,
        step_far,
        turn_far,
        filtered_far,
        ratio_far,
        lev_far,
        prior_far,
        strain,
        cut,
        chan,
        ana_raw,
        outer_raw,
        fwd_raw,
        inv_raw,
        syn_raw,
        step,
        turn,
        ana,
        outer,
        fwd,
        inv,
        syn,
        filtered,
        ratio,
        rim,
        spec,
        snd1,
        rcva,
        rcvb,
        scs1,
        scr1,
        x3,
        z3,
        snde,
        sndl,
        rcve,
        rcvl,
        scs2,
        scr2,
        deco,
        head,
        tail,
        sps,
        spr,
        sss,
        ssr,
        lev,
        seg,
        cars,
        carr,
        sums,
        sumr,
        temp,
        rim_s,
        rim_r,
        s1s,
        s1r,
        c1s,
        c1r,
        s2s,
        s2r,
        c2s,
        c2r,
        sp_s,
        sp_r,
        ss_s,
        ss_r,
        ca_s,
        ca_r,
        su_s,
        su_r,
        load_sem,
        store_sem,
    ) = refs
    me = lax.axis_index("fiber")
    tm = lax.axis_index("tm")
    per = BINS // nf
    rows = nf * ROWS
    half = rows // 2
    total = rows * LANES
    later, earlier = lax.rem(tm + 1, nt), lax.rem(tm + nt - 1, nt)

    def remote(src, dst, send, recv, **to):
        return pltpu.make_async_remote_copy(
            src_ref=src, dst_ref=dst, send_sem=send, recv_sem=recv, device_id=to, device_id_type=MESH
        )

    barrier = pltpu.get_barrier_semaphore()

    def greet_fiber(j, c):
        pl.semaphore_signal(
            barrier, inc=1, device_id={"fiber": lax.rem(me + j, nf)}, device_id_type=MESH
        )
        return c

    def greet_tm(j, c):
        pl.semaphore_signal(
            barrier, inc=1, device_id={"tm": lax.rem(tm + j, nt)}, device_id_type=MESH
        )
        return c

    lax.fori_loop(1, nt, greet_tm, 0)
    lax.fori_loop(1, nf, greet_fiber, 0)

    loads = [
        pltpu.make_async_copy(src, dst, load_sem.at[i])
        for i, (src, dst) in enumerate(
            [
                (ana_far, ana_raw),
                (strain_far, strain),
                (outer_far, outer_raw),
                (fwd_far, fwd_raw),
                (inv_far, inv_raw),
                (syn_far, syn_raw),
                (step_far, step),
                (turn_far, turn),
                (cut_far, cut),
                (sta_far, chan.at[0]),
                (lta_far, chan.at[1]),
                (drift_far, chan.at[2]),
            ]
        )
    ]
    for load in loads:
        load.start()

    def rates(i, at):
        return chan[i, at, :].astype(F32)

    pl.semaphore_wait(barrier, nf - 1 + nt - 1)

    chunks = 4
    wide = ROWS // chunks

    def rim_copy(c):
        span = pl.ds(c * wide * LANES, wide * LANES)
        return remote(strain_far.at[:, span], rim.at[:, span], rim_s.at[c], rim_r.at[c], tm=later)

    for chunk in range(chunks):
        rim_copy(chunk).start()

    for load in loads[:6]:
        load.wait()
    high, low = split(ana_raw[...])
    ana[...] = jnp.concatenate([high, low], axis=0)
    high, low = split(syn_raw[...])
    syn[...] = jnp.concatenate([high, high, low], axis=1)
    for raw, table in ((fwd_raw, fwd), (inv_raw, inv)):
        high, low = split(raw[...])
        table[...] = jnp.concatenate([high, high, low], axis=0)
    high, low = split(outer_raw[...])
    outer[...] = jnp.concatenate([high, high, low], axis=1)

    tall = ROWS // 2

    def scale1(j):
        to = lax.rem(me + j, nf)
        return remote(scs1, scr1.at[me], c1s.at[0], c1r.at[0], fiber=to)

    def data1(i, j):
        to = lax.rem(me + j, nf)
        if i == 0:
            src, dst = snd1.at[0, pl.ds(to * per, per)], rcva.at[me]
        else:
            src, dst = snd1.at[1, to * per + i - 1], rcvb.at[i - 1, me]
        return remote(src, dst, s1s.at[i], s1r.at[i], fiber=to)

    def of_all(ref, send, recv):
        return remote(ref, ref, send, recv, fiber=lax.rem(me + 1, nf))

    def all1(i):
        ref = rcva.at[pl.ds(0, nf - 1)] if i == 0 else rcvb.at[i - 1, pl.ds(0, nf - 1)]
        return of_all(ref, s1s.at[i], s1r.at[i])

    def all_scales1():
        return of_all(scr1.at[pl.ds(0, nf - 1)], c1s.at[0], c1r.at[0])

    def each_peer(act):
        def one(j, c):
            act(j)
            return c

        lax.fori_loop(1, nf, one, 0)

    for h in range(2):
        peak = jnp.zeros((1, 2 * LANES), F32)
        for chunk in range(h * chunks // 2, (h + 1) * chunks // 2):
            rim_copy(chunk).wait_recv()
            for q in range(chunk * wide, (chunk + 1) * wide, 2):
                cols = slice(q * LANES, (q + 2) * LANES)
                before = jnp.where(tm > 0, rim[:, cols].astype(F32), 0.0).astype(BF16)
                frame = jnp.concatenate([before, strain[:, cols]], axis=0)
                both = jnp.dot(ana[...], frame, preferred_element_type=F32)
                got = both[:FRAME] + both[FRAME:]
                spec[:, q, :] = got[:, :LANES]
                spec[:, q + 1, :] = got[:, LANES:]
                peak = jnp.maximum(peak, jnp.max(jnp.abs(got), axis=0, keepdims=True))
        peak = peak_of(peak)
        gain = TOP / peak
        scs1[h] = jnp.broadcast_to(peak * (1.0 / TOP), (1, LANES))
        scr1[me, h] = scs1[h]

        def code1(i, c):
            half_rows = slice(h * tall, (h + 1) * tall)
            re = spec[pl.ds(i * 8, 8), half_rows, :]
            im = spec[pl.ds(BINS + i * 8, 8), half_rows, :]
            snd1[h, pl.ds(i * 8, 8)] = coded(jnp.concatenate([re, im], axis=1), gain)
            return c

        lax.fori_loop(0, BINS // 8, code1, 0)
        if h == 0:

            each_peer(lambda j: data1(0, j).start())
            rcva[me] = snd1[0, pl.ds(me * per, per)]
        else:

            def send1(j):
                scale1(j).start()
                data1(1, j).start()

            each_peer(send1)
            for b in range(1, per):
                each_peer(lambda j: data1(1 + b, j).start())
            for b in range(per):
                rcvb[b, me] = snd1[1, me * per + b]

    all1(0).wait_recv()
    all_scales1().wait_recv()

    for load in loads[6:]:
        load.wait()
    peers = nf // 2

    final = per - 1

    def scale2(j):
        to = lax.rem(me + j, nf)
        return remote(scs2.at[to // peers], scr2.at[me], c2s.at[0], c2r.at[0], fiber=to)

    def data2(i, j):
        to = lax.rem(me + j, nf)
        if i < final:
            src, dst = snde.at[i, to], rcve.at[i, me]
        else:
            src, dst = sndl.at[i - final, to], rcvl.at[i - final, me]
        return remote(src, dst, s2s.at[i], s2r.at[i], fiber=to)

    def all2(i):
        if i < final:
            ref = rcve.at[i, pl.ds(0, nf - 1)]
        else:
            ref = rcvl.at[i - final, pl.ds(0, nf - 1)]
        return of_all(ref, s2s.at[i], s2r.at[i])

    def all_scales2():
        return of_all(scr2.at[pl.ds(0, nf - 1)], c2s.at[0], c2r.at[0])

    lane = lax.broadcasted_iota(jnp.int32, (half, LANES), 1)
    row = lax.broadcasted_iota(jnp.int32, (half, LANES), 0)

    def parts(x):
        return x[:, :LANES], x[:, LANES:]

    def put(ref, e, at, size, x):
        high, low = split(x)
        for i, part in enumerate((high, low, high)):
            ref[e, pl.ds(pl.multiple_of(i * half + at, ROWS), size), :] = part

    for b in range(per):
        all1(1 + b).wait_recv()
        limit_k = cut[me * per + b]

        def values(p):
            pieces = [x.astype(F32) * scr1[p, h] for h, x in enumerate((rcva[p, b], rcvb[b, p]))]
            return jnp.concatenate(
                [jnp.concatenate([x[i * tall : (i + 1) * tall] for x in pieces], 0) for i in range(2)],
                axis=1,
            )

        def decode(g, c):
            for i in range(GROUP):
                p = g * GROUP + i
                at = pl.multiple_of(p * ROWS, ROWS)
                early, late = values(p), values(p + peers)
                wr, wi = parts(step[pl.ds(at, ROWS), :])
                put(x3, 0, at, ROWS, early + late)
                re, im = parts(early - late)
                x = jnp.concatenate([re * wr - im * wi, re * wi + im * wr], axis=1)
                put(x3, 1, at, ROWS, x)
            return c

        lax.fori_loop(0, peers // GROUP, decode, 0)

        for e in range(2):
            pq = jnp.dot(outer[...], x3[e], preferred_element_type=F32)
            pr, pi = parts(pq[:half])
            qr, qi = parts(pq[half:])
            re, im = pr - qi, pi + qr
            tr, ti = parts(turn[e * half : (e + 1) * half, :])
            y = jnp.concatenate([re * tr - im * ti, re * ti + im * tr], axis=1)
            wr, wi = parts(jnp.dot(across(y), fwd[...], preferred_element_type=F32))
            k = 2 * row + e + rows * lane
            keep = jnp.minimum(k, total - k) <= limit_k
            w = jnp.concatenate([jnp.where(keep, wr, 0.0), jnp.where(keep, wi, 0.0)], axis=1)
            re, im = parts(jnp.dot(across(w), inv[...], preferred_element_type=F32))
            put(z3, e, 0, half, jnp.concatenate([re * tr + im * ti, im * tr - re * ti], axis=1))

        back = []
        for e in range(2):
            pq = jnp.dot(outer[...], z3[e], preferred_element_type=F32)
            pr, pi = parts(pq[:half])
            qr, qi = parts(pq[half:])
            back.append((pr + qi, pi - qr))
        (ur, ui), (re, im) = back
        wr, wi = parts(step[...])
        vr, vi = re * wr + im * wi, im * wr - re * wi
        for blk, (re, im) in enumerate(((ur + vr, ui + vi), (ur - vr, ui - vi))):
            top = peak_of(jnp.maximum(jnp.abs(re), jnp.abs(im)))
            scs2[blk, b] = jnp.broadcast_to(top * (1.0 / TOP), (1, LANES))
            re = re.reshape(peers, 2, tall, LANES)
            im = im.reshape(peers, 2, tall, LANES)
            code = coded(jnp.concatenate([re, im], axis=2), TOP / top)
            span = slice(blk * peers, (blk + 1) * peers)
            if b < final:
                snde[b, span] = code
            else:
                sndl[0, span] = code[:, 0]
                sndl[1, span] = code[:, 1]

        if b < final:
            each_peer(lambda j: data2(b, j).start())
            rcve[b, me] = snde[b, me]
        else:

            def send2(j):
                scale2(j).start()
                data2(final, j).start()

            each_peer(send2)
            each_peer(lambda j: data2(per, j).start())
            for h in range(2):
                rcvl[h, me] = sndl[h, me]
            scr2[me] = scs2[me // peers]

    def back_again(h):
        if h == 0:
            for i in range(per):
                all2(i).wait_recv()
            all_scales2().wait_recv()
        else:
            all2(per).wait_recv()

        def decode2(i, c):
            at = pl.ds(i * 8, 8)
            for b in range(per):
                x = rcve[b, at, h] if b < final else rcvl[h, at]
                x = x.astype(F32) * scr2[at, b]
                to = pl.ds(b * nf + i * 8, 8)
                deco[0, to, h * tall : (h + 1) * tall] = x[:, :tall]
                deco[1, to, h * tall : (h + 1) * tall] = x[:, tall:]
            return c

        lax.fori_loop(0, nf // 8, decode2, 0)

    def spill(c):
        span = pl.ds(c * wide, wide)
        return remote(sps.at[span], spr.at[span], sp_s.at[c], sp_r.at[c], tm=earlier)

    def spill_scale(c):
        return remote(sss.at[c], ssr.at[c], ss_s.at[c], ss_r.at[c], tm=earlier)

    for chunk in range(chunks):
        if chunk % (chunks // 2) == 0:
            back_again(chunk // (chunks // 2))
        top = jnp.full((1, 1), 1e-30, F32)
        for q in range(chunk * wide, (chunk + 1) * wide, 2):
            x = jnp.concatenate(
                [
                    jnp.concatenate([deco[0, :, q, :], deco[1, :, q, :]], axis=0),
                    jnp.concatenate([deco[0, :, q + 1, :], deco[1, :, q + 1, :]], axis=0),
                ],
                axis=1,
            )
            high, low = split(x)
            got = jnp.dot(
                syn[...], jnp.concatenate([high, low, high], axis=0), preferred_element_type=F32
            )
            for i in range(2):
                head[q + i] = got[:HOP, i * LANES : (i + 1) * LANES]
                tail[q + i] = got[HOP:, i * LANES : (i + 1) * LANES]
            top = jnp.maximum(top, peak_of(got[:HOP]))
        sss[chunk] = jnp.broadcast_to(top * (1.0 / TOP), (1, LANES))
        spill_scale(chunk).start()
        for q in range(chunk * wide, (chunk + 1) * wide):
            sps[q] = coded(head[q], TOP / top)
        spill(chunk).start()

    has_next = jnp.where(tm < nt - 1, 1.0, 0.0).astype(F32)
    seg_id = lax.broadcasted_iota(jnp.int32, (8, LANES), 0)

    def shifted(x, by, fill):
        return jnp.where(seg_id >= by, pltpu.roll(x, by, 0), fill)

    def rate_of(length):
        return 1.0 - 1.0 / length

    def natural(g, vectors):
        return in_order(temp, g, vectors)

    def grouped(one):
        def group(i, c):
            for g in range(GROUP):
                one(i * GROUP + g, g)
            return c

        return group

    for chunk in range(chunks):
        spill_scale(chunk).wait_recv()
        spill(chunk).wait_recv()

        def scan_row(q, g):
            at = pl.ds(q, 1)
            cols = pl.ds(pl.multiple_of(q * LANES, LANES), LANES)
            heads = spr[q].astype(F32) * (ssr[chunk] * has_next)
            rounded = (tail[q] + heads).astype(BF16).astype(F32)
            part = [rounded[8 * i : 8 * i + 8] for i in range(8)]
            filtered[:, cols] = natural(g, part).astype(BF16)
            energy = [v * v for v in part]
            for s in range(2):
                keep = jnp.broadcast_to(rate_of(rates(s, at)), (8, LANES))
                gain = 1.0 - keep
                level = gain * energy[0]
                lev[s, q, 0:8] = level
                for i in range(1, 8):
                    level = keep * level + gain * energy[i]
                    lev[s, q, 8 * i : 8 * i + 8] = level
                power = keep * keep
                power = power * power
                power = power * power
                for by in (1, 2, 4):
                    level = level + power * shifted(level, by, 0.0)
                    power = power * power
                seg[s, q] = shifted(level, 1, 0.0)
                cars[s, at, :] = level[7:8]

        for g in range(wide):
            scan_row(chunk * wide + g, g)

    stores = [
        pltpu.make_async_copy(src, dst, store_sem.at[i])
        for i, (src, dst) in enumerate([(filtered, filtered_far), (ratio, ratio_far), (lev, lev_far)])
    ]
    stores[0].start()

    def to_later(snd, rcv, send, recv, j):
        return remote(snd, rcv.at[tm], send.at[j], recv.at[j], tm=lax.rem(tm + j, nt))

    def from_earlier(snd, rcv, send, recv, j):
        back = lax.rem(tm + nt - j, nt)
        return remote(snd, rcv.at[back], send.at[j], recv.at[j], tm=back)

    def pass_on(snd, rcv, send, recv):
        def out(j, c):
            to_later(snd, rcv, send, recv, j).start()
            return c

        lax.fori_loop(1, nt - tm, out, 0)

        def come(j, c):
            from_earlier(snd, rcv, send, recv, j).wait_recv()
            return c

        lax.fori_loop(1, tm + 1, come, 0)

    pass_on(cars, carr, ca_s, ca_r)
    decay = []
    for s in range(2):
        power = rate_of(chan[s].astype(F32))
        for _ in range(6):
            power = power * power
        decay.append(power)

    def lap(k, state):
        return tuple(decay[s] * state[s] + carr[k, s] for s in range(2))

    ones = jnp.ones((ROWS, LANES), F32)
    start = lax.fori_loop(0, tm, lap, (ones, ones))
    head[0, 0:ROWS] = start[0]
    head[1, 0:ROWS] = start[1]

    def climb_row(q, g):
        at = pl.ds(q, 1)
        cols = pl.ds(pl.multiple_of(q * LANES, LANES), LANES)
        avg = []
        for s in range(2):
            keep = jnp.broadcast_to(rate_of(rates(s, at)), (8, LANES))
            carry = jnp.broadcast_to(head[s, at, :], (8, LANES))
            power = keep * keep
            power = power * power
            power = power * power
            for bit in (1, 2, 4):
                carry = jnp.where((seg_id // bit) % 2 == 1, carry * power, carry)
                power = power * power
            entry = seg[s, q] + carry
            values = []
            for i in range(8):
                entry = entry * keep
                values.append(lev[s, q, 8 * i : 8 * i + 8] + entry)
            avg.append(values)
        quotient = [avg[0][i] / avg[1][i] for i in range(8)]
        ratio[:, cols] = natural(g, quotient)
        rate = jnp.broadcast_to(0.5 + rates(2, at) * (1.0 / 64.0), (8, LANES))
        climb = quotient[0] - rate
        low = climb
        climbs, lows = [climb], [low]
        for i in range(1, 8):
            climb = climb + (quotient[i] - rate)
            low = jnp.minimum(low, climb)
            climbs.append(climb)
            lows.append(low)
        whole = climb
        for by in (1, 2, 4):
            whole = whole + shifted(whole, by, 0.0)
        base = shifted(whole, 1, 0.0)
        least = base + low
        for by in (1, 2, 4):
            least = jnp.minimum(least, shifted(least, by, jnp.inf))
        floor = shifted(least, 1, jnp.inf)
        for i in range(8):
            up = base + climbs[i]
            lev[0, q, 8 * i : 8 * i + 8] = up
            lev[1, q, 8 * i : 8 * i + 8] = jnp.minimum(floor, base + lows[i])
        sums[0, at, :] = whole[7:8]
        sums[1, at, :] = least[7:8]

    lax.fori_loop(0, ROWS // GROUP, grouped(climb_row), 0)

    stores[1].start()
    stores[2].start()
    pass_on(sums, sumr, su_s, su_r)

    def lap2(k, state):
        total_up, low = state
        return total_up + sumr[k, 0], jnp.minimum(low, total_up + sumr[k, 1])

    zeros = jnp.zeros((ROWS, LANES), F32)
    before, low = lax.fori_loop(0, tm, lap2, (zeros, zeros))
    head[2, 0:ROWS] = before
    head[3, 0:ROWS] = low
    last = pltpu.make_async_copy(head.at[pl.ds(2, 2), pl.ds(0, ROWS), :], prior_far, store_sem.at[3])
    last.start()

    for chunk in range(chunks):
        rim_copy(chunk).wait_send()

    for i in range(per + 1):
        all1(i).wait_send()
        all2(i).wait_send()
    all_scales1().wait_send()
    all_scales2().wait_send()
    for chunk in range(chunks):
        spill_scale(chunk).wait_send()
        spill(chunk).wait_send()

    def sent_on(j, c):
        to_later(sums, carr, ca_s, ca_r, j).wait_send()
        to_later(sums, sumr, su_s, su_r, j).wait_send()
        return c

    lax.fori_loop(1, nt - tm, sent_on, 0)
    for store in stores:
        store.wait()
    last.wait()


def finish(
    filtered_far,
    ratio_far,
    lev_far,
    prior_far,
    limit_far,
    filtered_out,
    ratio_out,
    ph_out,
    filtered,
    ratio,
    lev,
    prior,
    limit,
    ph,
    temp,
    load_sem,
    store_sem,
):
    groups = ROWS // GROUP
    loads = [
        pltpu.make_async_copy(src, dst, load_sem.at[i])
        for i, (src, dst) in enumerate(
            [(prior_far, prior), (limit_far, limit), (filtered_far, filtered), (ratio_far, ratio)]
            + [(lev_far.at[:, pl.ds(4 * i, 4)], lev.at[:, pl.ds(4 * i, 4)]) for i in range(groups)]
        )
    ]
    for i in (0, 1, 4, 5, 6, 7, 2, 3):
        loads[i].start()
    stores = [
        pltpu.make_async_copy(filtered, filtered_out, store_sem.at[0]),
        pltpu.make_async_copy(ratio, ratio_out, store_sem.at[1]),
    ]
    loads[0].wait()
    loads[1].wait()
    for i in range(groups):
        loads[4 + i].wait()
        for g in range(GROUP):
            q = i * GROUP + g
            base = jnp.broadcast_to(prior[0, q : q + 1, :], (8, LANES))
            low = jnp.broadcast_to(prior[1, q : q + 1, :], (8, LANES))
            scale = jnp.broadcast_to(1.0 / limit[q : q + 1, :].astype(F32), (8, LANES))
            out = []
            for k in range(8):
                climb = base + lev[0, q, 8 * k : 8 * k + 8]
                lowest = jnp.minimum(low, base + lev[1, q, 8 * k : 8 * k + 8])
                out.append((climb - lowest) * scale)
            ph[:, q * LANES : (q + 1) * LANES] = in_order(temp, g, out)
        span = pl.ds(i * GROUP * LANES, GROUP * LANES)
        stores.append(
            pltpu.make_async_copy(ph.at[:, span], ph_out.at[:, span], store_sem.at[2 + i])
        )
        stores[-1].start()
        if i < 2:
            loads[2 + i].wait()
            stores[i].start()
    for store in stores:
        store.wait()


def body(nf, nt, strain, fan_cut, sta_len, lta_len, drift_code, threshold):
    per = BINS // nf
    rows = nf * ROWS
    total = rows * LANES
    half = rows // 2
    tabs = [jnp.asarray(t) for t in tables(total)]
    per_chan = [v.reshape(ROWS, LANES) for v in (sta_len, lta_len, drift_code, threshold)]
    far = pl.BlockSpec(memory_space=pl.ANY)
    dma = pltpu.SemaphoreType.DMA
    i16 = jnp.int16
    chans = ROWS * LANES
    results = pl.pallas_call(
        functools.partial(kernel, nf, nt),
        out_shape=(
            jax.ShapeDtypeStruct((HOP, chans), BF16),
            jax.ShapeDtypeStruct((HOP, chans), F32),
            jax.ShapeDtypeStruct((2, ROWS, HOP, LANES), F32),
            jax.ShapeDtypeStruct((2, ROWS, LANES), F32),
        ),
        in_specs=[far] * 12,
        out_specs=(far,) * 4,
        scratch_shapes=[
            pltpu.VMEM((HOP, chans), BF16),
            pltpu.SMEM((BINS,), jnp.int32),
            pltpu.VMEM((3, ROWS, LANES), jnp.int32),
        ]
        + [pltpu.VMEM(t.shape, F32) for t in tabs]
        + [
            pltpu.VMEM((2 * FRAME, FRAME), BF16),
            pltpu.VMEM((rows, 3 * half), BF16),
            pltpu.VMEM((6 * LANES, 2 * LANES), BF16),
            pltpu.VMEM((6 * LANES, 2 * LANES), BF16),
            pltpu.VMEM((FRAME, 3 * FRAME), BF16),
            pltpu.VMEM((HOP, chans), BF16),
            pltpu.VMEM((HOP, chans), F32),
            pltpu.VMEM((HOP, chans), BF16),
            pltpu.VMEM((FRAME, ROWS, LANES), F32),
            pltpu.VMEM((2, BINS, ROWS, LANES), i16),
            pltpu.VMEM((nf, per, ROWS, LANES), i16),
            pltpu.VMEM((per, nf, ROWS, LANES), i16),
            pltpu.VMEM((2, 1, LANES), F32),
            pltpu.VMEM((nf, 2, 1, LANES), F32),
            pltpu.VMEM((2, 3 * half, 2 * LANES), BF16),
            pltpu.VMEM((2, 3 * half, 2 * LANES), BF16),
            pltpu.VMEM((per - 1, nf, 2, ROWS, LANES), i16),
            pltpu.VMEM((2, nf, ROWS, LANES), i16),
            pltpu.VMEM((per - 1, nf, 2, ROWS, LANES), i16),
            pltpu.VMEM((2, nf, ROWS, LANES), i16),
            pltpu.VMEM((2, per, 1, LANES), F32),
            pltpu.VMEM((nf, per, 1, LANES), F32),
            pltpu.VMEM((2, BINS, ROWS, LANES), F32),
            pltpu.VMEM((ROWS, HOP, LANES), F32),
            pltpu.VMEM((ROWS, HOP, LANES), F32),
            pltpu.VMEM((ROWS, HOP, LANES), i16),
            pltpu.VMEM((ROWS, HOP, LANES), i16),
            pltpu.VMEM((4, 1, LANES), F32),
            pltpu.VMEM((4, 1, LANES), F32),
            pltpu.VMEM((2, ROWS, HOP, LANES), F32),
            pltpu.VMEM((2, ROWS, 8, LANES), F32),
            pltpu.VMEM((2, ROWS, LANES), F32),
            pltpu.VMEM((nt, 2, ROWS, LANES), F32),
            pltpu.VMEM((2, ROWS, LANES), F32),
            pltpu.VMEM((nt, 2, ROWS, LANES), F32),
            pltpu.VMEM((GROUP, HOP, LANES), F32),
            dma((4,)),
            dma((4,)),
            dma((per + 1,)),
            dma((per + 1,)),
            dma((1,)),
            dma((1,)),
            dma((per + 1,)),
            dma((per + 1,)),
            dma((1,)),
            dma((1,)),
            dma((4,)),
            dma((4,)),
            dma((4,)),
            dma((4,)),
            dma((nt,)),
            dma((nt,)),
            dma((nt,)),
            dma((nt,)),
            dma((12,)),
            dma((4,)),
        ],
        compiler_params=pltpu.CompilerParams(
            collective_id=0, has_side_effects=True, vmem_limit_bytes=64 * 1024 * 1024
        ),
    )(strain, fan_cut, *per_chan[:3], *tabs)
    return pl.pallas_call(
        finish,
        out_shape=(
            jax.ShapeDtypeStruct((HOP, chans), BF16),
            jax.ShapeDtypeStruct((HOP, chans), F32),
            jax.ShapeDtypeStruct((HOP, chans), F32),
        ),
        in_specs=[far] * 5,
        out_specs=(far,) * 3,
        scratch_shapes=[
            pltpu.VMEM((HOP, chans), BF16),
            pltpu.VMEM((HOP, chans), F32),
            pltpu.VMEM((2, ROWS, HOP, LANES), F32),
            pltpu.VMEM((2, ROWS, LANES), F32),
            pltpu.VMEM((ROWS, LANES), jnp.int32),
            pltpu.VMEM((HOP, chans), F32),
            pltpu.VMEM((GROUP, HOP, LANES), F32),
            dma((8,)),
            dma((6,)),
        ],
        compiler_params=pltpu.CompilerParams(vmem_limit_bytes=64 * 1024 * 1024),
    )(*results, per_chan[3])


def solution(mesh):
    return jax.shard_map(
        functools.partial(body, mesh.shape["fiber"], mesh.shape["tm"]),
        mesh=mesh,
        in_specs=(P("tm", "fiber"), P(), P("fiber"), P("fiber"), P("fiber"), P("fiber")),
        out_specs=(P("tm", "fiber"), P("tm", "fiber"), P("tm", "fiber")),
        check_vma=False,
    )
```

```python
import functools
import math

import jax
import jax.numpy as jnp
import numpy as np
from jax import lax
from jax.experimental import pallas as pl
from jax.experimental.pallas import tpu as pltpu
from jax.sharding import PartitionSpec as P

FRAME = 128
HOP = 64
BINS = 64
LANES = 128
ROWS = 16
GROUP = 4
TOP = 32512.0
MESH = pl.DeviceIdType.MESH
F32 = jnp.float32
BF16 = jnp.bfloat16


def time_order():
    rows = np.arange(HOP)
    return 8 * (rows % 8) + rows // 8


def tables(total):
    rows = total // LANES
    nf = rows // ROWS
    half = rows // 2
    n = np.arange(FRAME)
    f = np.arange(BINS)
    angle = 2.0 * math.pi / FRAME * ((f[:, None] * n[None, :]) % FRAME)
    window = 0.5 - 0.5 * np.cos(2.0 * math.pi / FRAME * n)
    analysis = np.concatenate([window * np.cos(angle), -window * np.sin(angle)], 0)
    weight = np.where(f == 0, 1.0, 2.0)[:, None] / FRAME
    synthesis = np.concatenate([weight * np.cos(angle), -weight * np.sin(angle)], 0).T
    order = time_order()
    arrived = np.arange(BINS).reshape(nf, BINS // nf).T.reshape(-1)
    synthesis = synthesis[np.concatenate([order, HOP + order])]
    synthesis = synthesis[:, np.concatenate([arrived, BINS + arrived])]
    a = np.arange(half)
    outer = 2.0 * math.pi / half * ((a[:, None] * a[None, :]) % half)
    outer = np.concatenate([np.cos(outer), -np.sin(outer)], 0)
    step = np.broadcast_to(2.0 * math.pi / rows * a[:, None], (half, LANES))
    step = np.concatenate([np.cos(step), -np.sin(step)], 1)
    b = np.arange(LANES)
    wave = np.concatenate([2 * a, 2 * a + 1])
    turn = 2.0 * math.pi / total * ((wave[:, None] * b[None, :]) % total)
    turn = np.concatenate([np.cos(turn), -np.sin(turn)], 1)
    inner = 2.0 * math.pi / LANES * ((b[:, None] * b[None, :]) % LANES)
    cos, sin = np.cos(inner), np.sin(inner)
    forward = np.block([[cos, -sin], [sin, cos]])
    inverse = np.block([[cos, sin], [-sin, cos]]) / total
    return [t.astype(np.float32) for t in (analysis, outer, forward, inverse, synthesis, step, turn)]


def split(x):
    high = x.astype(BF16)
    return high, (x - high.astype(F32)).astype(BF16)


def across(x):
    high, low = split(x)
    return jnp.concatenate([high, low, high], axis=1)


def peak_of(x):
    top = jnp.max(jnp.max(jnp.abs(x), axis=0, keepdims=True), axis=1, keepdims=True)
    return jnp.maximum(top, 1e-30)


def in_order(temp, g, vectors):
    for i in range(8):
        temp[g, pl.ds(i, 8, stride=8), :] = vectors[i]
    return temp[g]


def coded(x, gain):
    return jnp.round(x * gain).astype(jnp.int32).astype(jnp.int16)


def kernel(
    nf,
    nt,
    *refs,
):
    (
        strain_far,
        cut_far,
        sta_far,
        lta_far,
        drift_far,
        ana_far,
        outer_far,
        fwd_far,
        inv_far,
        syn_far,
        step_far,
        turn_far,
        filtered_far,
        ratio_far,
        lev_far,
        prior_far,
        strain,
        cut,
        chan,
        ana_raw,
        outer_raw,
        fwd_raw,
        inv_raw,
        syn_raw,
        step,
        turn,
        ana,
        outer,
        fwd,
        inv,
        syn,
        filtered,
        ratio,
        rim,
        spec,
        snd1,
        rcva,
        rcvb,
        scs1,
        scr1,
        x3,
        z3,
        snd2,
        rcve,
        rcvl,
        scs2,
        scr2,
        deco,
        head,
        tail,
        sps,
        spr,
        sss,
        ssr,
        lev,
        seg,
        cars,
        carsib,
        cartot,
        carall,
        cargift,
        start,
        sums,
        sumsib,
        sumtot,
        sumall,
        sumgift,
        prior,
        temp,
        rim_s,
        rim_r,
        s1s,
        s1r,
        c1s,
        c1r,
        s2s,
        s2r,
        c2s,
        c2r,
        sp_s,
        sp_r,
        ss_s,
        ss_r,
        sib_s,
        sib_r,
        z_s,
        z_r,
        load_sem,
        store_sem,
    ) = refs
    me = lax.axis_index("fiber")
    tm = lax.axis_index("tm")
    per = BINS // nf
    rows = nf * ROWS
    half = rows // 2
    total = rows * LANES
    later, earlier = lax.rem(tm + 1, nt), lax.rem(tm + nt - 1, nt)

    def remote(src, dst, send, recv, **to):
        return pltpu.make_async_remote_copy(
            src_ref=src, dst_ref=dst, send_sem=send, recv_sem=recv, device_id=to, device_id_type=MESH
        )

    barrier = pltpu.get_barrier_semaphore()

    width = 4
    lines = nf // width

    def each_peer(act):
        def one(i, c):
            g = i // width
            back = (g + 1) // 2
            down = lines // 2 + jnp.where(g % 2 == 0, back, -back)
            over = lax.rem(i, width) + jnp.where(g == lines - 1, 1, 0)
            act(lax.rem(me // width + down, lines) * width + lax.rem(me + over, width))
            return c

        lax.fori_loop(0, nf - 1, one, 0)

    def greet(**to):
        pl.semaphore_signal(barrier, inc=1, device_id=to, device_id_type=MESH)

    nz = nt // 2
    friends = list(dict.fromkeys((1, nt - 1, *range(2, nt, 2))))
    for j in friends:
        greet(tm=lax.rem(tm + j, nt))
    line = me // width
    mine = lax.rem(me, width)
    beside = [lax.rem(mine + i, width) for i in range(width)]
    for g in range(lines):
        down = lines // 2 + (g + 1) // 2 * (1 if g % 2 == 0 else -1)
        at = lax.rem(line + down, lines) * width
        for i in range(1 if g == lines - 1 else 0, width):
            greet(fiber=at + beside[i])

    loads = [
        pltpu.make_async_copy(src, dst, load_sem.at[i])
        for i, (src, dst) in enumerate(
            [
                (ana_far, ana_raw),
                (strain_far, strain),
                (outer_far, outer_raw),
                (fwd_far, fwd_raw),
                (inv_far, inv_raw),
                (syn_far, syn_raw),
                (step_far, step),
                (turn_far, turn),
                (cut_far, cut),
                (sta_far, chan.at[0]),
                (lta_far, chan.at[1]),
                (drift_far, chan.at[2]),
            ]
        )
    ]
    for load in loads:
        load.start()

    def rates(i, at):
        return chan[i, at, :].astype(F32)

    pl.semaphore_wait(barrier, nf - 1 + len(friends))

    chunks = 4
    wide = ROWS // chunks

    def rim_copy(c):
        span = pl.ds(c * wide * LANES, wide * LANES)
        return remote(strain_far.at[:, span], rim.at[:, span], rim_s.at[c], rim_r.at[c], tm=later)

    @pl.when(tm < nt - 1)
    def _():
        for chunk in range(chunks):
            rim_copy(chunk).start()

    for load in loads[:6]:
        load.wait()
    high, low = split(ana_raw[...])
    ana[...] = jnp.concatenate([high, low], axis=0)
    high, low = split(syn_raw[...])
    syn[...] = jnp.concatenate([high, high, low], axis=1)
    for raw, table in ((fwd_raw, fwd), (inv_raw, inv)):
        high, low = split(raw[...])
        table[...] = jnp.concatenate([high, high, low], axis=0)
    high, low = split(outer_raw[...])
    outer[...] = jnp.concatenate([high, high, low], axis=1)

    tall = ROWS // 2

    def scale1(to):
        return remote(scs1, scr1.at[me], c1s.at[0], c1r.at[0], fiber=to)

    def data1(i, to):
        if i == 0:
            src, dst = snd1.at[0, pl.ds(to * per, per)], rcva.at[me]
        else:
            src, dst = snd1.at[1, to * per + i - 1], rcvb.at[i - 1, me]
        return remote(src, dst, s1s.at[i], s1r.at[i], fiber=to)

    def of_all(ref, send, recv):
        return remote(ref, ref, send, recv, fiber=lax.rem(me + 1, nf))

    def all1(i):
        ref = rcva.at[pl.ds(0, nf - 1)] if isinstance(i, int) and i == 0 else rcvb.at[i - 1, pl.ds(0, nf - 1)]
        return of_all(ref, s1s.at[i], s1r.at[i])

    def all_scales1():
        return of_all(scr1.at[pl.ds(0, nf - 1)], c1s.at[0], c1r.at[0])

    for h in range(2):
        peak = jnp.zeros((1, 2 * LANES), F32)
        for chunk in range(h * chunks // 2, (h + 1) * chunks // 2):
            pl.when(tm > 0)(rim_copy(chunk).wait_recv)
            for q in range(chunk * wide, (chunk + 1) * wide, 2):
                cols = slice(q * LANES, (q + 2) * LANES)
                before = jnp.where(tm > 0, rim[:, cols].astype(F32), 0.0).astype(BF16)
                frame = jnp.concatenate([before, strain[:, cols]], axis=0)
                both = jnp.dot(ana[...], frame, preferred_element_type=F32)
                got = both[:FRAME] + both[FRAME:]
                spec[:, q, :] = got[:, :LANES]
                spec[:, q + 1, :] = got[:, LANES:]
                peak = jnp.maximum(peak, jnp.max(jnp.abs(got), axis=0, keepdims=True))
        peak = peak_of(peak)
        gain = TOP / peak
        scs1[h] = jnp.broadcast_to(peak * (1.0 / TOP), (1, LANES))
        scr1[me, h] = scs1[h]

        half_rows = slice(h * tall, (h + 1) * tall)
        re, im = spec[:BINS, half_rows, :], spec[BINS:, half_rows, :]
        snd1[h] = coded(jnp.concatenate([re, im], axis=1), gain)
        if h == 0:

            each_peer(lambda to: data1(0, to).start())
            rcva[me] = snd1[0, pl.ds(me * per, per)]
        else:

            def send1(j):
                scale1(j).start()
                data1(1, j).start()

            each_peer(send1)
            for b in range(1, per):
                each_peer(lambda to: data1(1 + b, to).start())
            for b in range(per):
                rcvb[b, me] = snd1[1, me * per + b]

    all1(0).wait_recv()
    all_scales1().wait_recv()

    for load in loads[6:]:
        load.wait()
    peers = nf // 2

    final = per - 1

    def scale2(to):
        return remote(scs2.at[to // peers], scr2.at[me], c2s.at[0], c2r.at[0], fiber=to)

    def early2(b, to):
        return remote(snd2.at[b, to], rcve.at[b, me], s2s.at[b], s2r.at[b], fiber=to)

    def last2(h, to):
        i = final + h
        return remote(snd2.at[final, to, h], rcvl.at[h, me], s2s.at[i], s2r.at[i], fiber=to)

    def all2(i):
        if i < final:
            ref = rcve.at[i, pl.ds(0, nf - 1)]
        else:
            ref = rcvl.at[i - final, pl.ds(0, nf - 1)]
        return of_all(ref, s2s.at[i], s2r.at[i])

    def all_scales2():
        return of_all(scr2.at[pl.ds(0, nf - 1)], c2s.at[0], c2r.at[0])

    lane = lax.broadcasted_iota(jnp.int32, (half, LANES), 1)
    row = lax.broadcasted_iota(jnp.int32, (half, LANES), 0)

    def parts(x):
        return x[:, :LANES], x[:, LANES:]

    def put(ref, e, at, size, x):
        high, low = split(x)
        for i, part in enumerate((high, low, high)):
            ref[e, pl.ds(pl.multiple_of(i * half + at, ROWS), size), :] = part

    def transform(b):
        all1(1 + b).wait_recv()
        limit_k = cut[me * per + b]

        def values(p):
            pieces = [x.astype(F32) * scr1[p, h] for h, x in enumerate((rcva[p, b], rcvb[b, p]))]
            return jnp.concatenate(
                [jnp.concatenate([x[i * tall : (i + 1) * tall] for x in pieces], 0) for i in range(2)],
                axis=1,
            )

        def decode(g, c):
            for i in range(GROUP):
                p = g * GROUP + i
                at = pl.multiple_of(p * ROWS, ROWS)
                early, late = values(p), values(p + peers)
                wr, wi = parts(step[pl.ds(at, ROWS), :])
                put(x3, 0, at, ROWS, early + late)
                re, im = parts(early - late)
                x = jnp.concatenate([re * wr - im * wi, re * wi + im * wr], axis=1)
                put(x3, 1, at, ROWS, x)
            return c

        lax.fori_loop(0, peers // GROUP, decode, 0)

        def waves(e, c):
            pq = jnp.dot(outer[...], x3[e], preferred_element_type=F32)
            pr, pi = parts(pq[:half])
            qr, qi = parts(pq[half:])
            re, im = pr - qi, pi + qr
            tr, ti = parts(turn[pl.ds(pl.multiple_of(e * half, half), half), :])
            y = jnp.concatenate([re * tr - im * ti, re * ti + im * tr], axis=1)
            wr, wi = parts(jnp.dot(across(y), fwd[...], preferred_element_type=F32))
            k = 2 * row + e + rows * lane
            keep = jnp.minimum(k, total - k) <= limit_k
            w = jnp.concatenate([jnp.where(keep, wr, 0.0), jnp.where(keep, wi, 0.0)], axis=1)
            re, im = parts(jnp.dot(across(w), inv[...], preferred_element_type=F32))
            put(z3, e, 0, half, jnp.concatenate([re * tr + im * ti, im * tr - re * ti], axis=1))
            return c

        lax.fori_loop(0, 2, waves, 0)

        back = []
        for e in range(2):
            pq = jnp.dot(outer[...], z3[e], preferred_element_type=F32)
            pr, pi = parts(pq[:half])
            qr, qi = parts(pq[half:])
            back.append((pr + qi, pi - qr))
        (ur, ui), (re, im) = back
        wr, wi = parts(step[...])
        vr, vi = re * wr + im * wi, im * wr - re * wi
        for blk, (re, im) in enumerate(((ur + vr, ui + vi), (ur - vr, ui - vi))):
            top = peak_of(jnp.maximum(jnp.abs(re), jnp.abs(im)))
            scs2[blk, b] = jnp.broadcast_to(top * (1.0 / TOP), (1, LANES))
            re = re.reshape(peers, 2, tall, LANES)
            im = im.reshape(peers, 2, tall, LANES)
            code = coded(jnp.concatenate([re, im], axis=2), TOP / top)
            span = slice(blk * peers, (blk + 1) * peers)
            snd2[b, span] = code

    def bin_step(b, c):
        transform(b)

        @pl.when(b < final)
        def _():
            each_peer(lambda to: early2(b, to).start())

        return c

    lax.fori_loop(0, per, bin_step, 0)

    def send2(to):
        scale2(to).start()
        last2(0, to).start()

    each_peer(send2)
    each_peer(lambda to: last2(1, to).start())
    for b in range(final):
        rcve[b, me] = snd2[b, me]
    for h in range(2):
        rcvl[h, me] = snd2[final, me, h]
    scr2[me] = scs2[me // peers]

    def back_again(h):
        if h == 0:
            for i in range(per):
                all2(i).wait_recv()
            all_scales2().wait_recv()
        else:
            all2(per).wait_recv()

        for b in range(per):
            x = rcve[b, :, h] if b < final else rcvl[h]
            x = x.astype(F32) * scr2[:, b]
            to = slice(b * nf, (b + 1) * nf)
            deco[0, to, h * tall : (h + 1) * tall] = x[:, :tall]
            deco[1, to, h * tall : (h + 1) * tall] = x[:, tall:]

    def spill(c):
        span = pl.ds(c * wide, wide)
        return remote(sps.at[span], spr.at[span], sp_s.at[c], sp_r.at[c], tm=earlier)

    def spill_scale(c):
        return remote(sss.at[c], ssr.at[c], ss_s.at[c], ss_r.at[c], tm=earlier)

    for chunk in range(chunks):
        if chunk % (chunks // 2) == 0:
            back_again(chunk // (chunks // 2))
        top = jnp.full((1, 1), 1e-30, F32)
        for q in range(chunk * wide, (chunk + 1) * wide, 2):
            x = jnp.concatenate(
                [
                    jnp.concatenate([deco[0, :, q, :], deco[1, :, q, :]], axis=0),
                    jnp.concatenate([deco[0, :, q + 1, :], deco[1, :, q + 1, :]], axis=0),
                ],
                axis=1,
            )
            high, low = split(x)
            got = jnp.dot(
                syn[...], jnp.concatenate([high, low, high], axis=0), preferred_element_type=F32
            )
            for i in range(2):
                head[q + i] = got[:HOP, i * LANES : (i + 1) * LANES]
                tail[q + i] = got[HOP:, i * LANES : (i + 1) * LANES]
            top = jnp.maximum(top, peak_of(got[:HOP]))
        sss[chunk] = jnp.broadcast_to(top * (1.0 / TOP), (1, LANES))
        pl.when(tm > 0)(spill_scale(chunk).start)
        for q in range(chunk * wide, (chunk + 1) * wide):
            sps[q] = coded(head[q], TOP / top)
        pl.when(tm > 0)(spill(chunk).start)

    seg_id = lax.broadcasted_iota(jnp.int32, (8, LANES), 0)

    def shifted(x, by, fill):
        return jnp.where(seg_id >= by, pltpu.roll(x, by, 0), fill)

    def rate_of(length):
        return 1.0 - 1.0 / length

    def natural(g, vectors):
        return in_order(temp, g, vectors)

    def scan_chunk(chunk, c):
        @pl.when(tm < nt - 1)
        def _():
            spill_scale(chunk).wait_recv()
            spill(chunk).wait_recv()

        def scan_row(q, g):
            at = pl.ds(q, 1)
            cols = pl.ds(pl.multiple_of(q * LANES, LANES), LANES)
            heads = jnp.where(tm < nt - 1, spr[q].astype(F32) * ssr[chunk], 0.0)
            rounded = (tail[q] + heads).astype(BF16).astype(F32)
            part = [rounded[8 * i : 8 * i + 8] for i in range(8)]
            filtered[:, cols] = natural(g, part).astype(BF16)
            energy = [v * v for v in part]
            for s in range(2):
                keep = jnp.broadcast_to(rate_of(rates(s, at)), (8, LANES))
                gain = 1.0 - keep
                level = gain * energy[0]
                lev[s, q, 0:8] = level
                for i in range(1, 8):
                    level = keep * level + gain * energy[i]
                    lev[s, q, 8 * i : 8 * i + 8] = level
                power = keep * keep
                power = power * power
                power = power * power
                for by in (1, 2, 4):
                    level = level + power * shifted(level, by, 0.0)
                    power = power * power
                seg[s, q] = shifted(level, 1, 0.0)
                cars[q // tall, s, pl.ds(lax.rem(q, tall), 1), :] = level[7:8]

        for g in range(wide):
            scan_row(chunk * wide + g, g)
        return c

    lax.fori_loop(0, chunks, scan_chunk, 0)

    stores = [
        pltpu.make_async_copy(src, dst, store_sem.at[i])
        for i, (src, dst) in enumerate([(filtered, filtered_far), (ratio, ratio_far), (lev, lev_far)])
    ]
    stores[0].start()

    core = lax.rem(tm, 2)
    chip = tm // 2
    sibling = tm + 1 - 2 * core

    def give(src, dst, i):
        return remote(src, dst, sib_s.at[i], sib_r.at[i], tm=sibling)

    def to_later(snd, rcv, i, j):
        to = lax.rem(tm + 2 * j, nt)
        return remote(snd, rcv.at[chip], z_s.at[i, j], z_r.at[i, j], tm=to)

    def from_earlier(snd, rcv, i, j):
        back = lax.rem(tm + nt - 2 * j, nt)
        return remote(snd, rcv.at[chip - j], z_s.at[i, j], z_r.at[i, j], tm=back)

    def pair_of(ref):
        return ref[0], ref[1]

    def chosen(first, second):
        return tuple(jnp.where(core == 0, a, b) for a, b in zip(first, second))

    def pass_on(i, own, sib, tot, totr, gift, entry, join, apply, step, begin):
        half_away = give(own.at[1 - core], sib, 2 * i)
        half_away.start()
        half_away.wait_recv()
        mine, other = pair_of(own.at[core]), pair_of(sib)
        early, late = chosen(mine, other), chosen(other, mine)
        tot[0], tot[1] = join(early, late)

        def out(j, c):
            to_later(tot, totr, i, j).start()
            return c

        lax.fori_loop(1, nz - chip, out, 0)

        def come(j, c):
            from_earlier(tot, totr, i, j).wait_recv()
            return c

        lax.fori_loop(1, chip + 1, come, 0)
        state = lax.fori_loop(0, chip, lambda k, state: apply(state, pair_of(totr.at[k])), begin)
        after = step(state, early)
        entry[core, 0], entry[core, 1] = chosen(state, after)
        gift[0], gift[1] = chosen(after, state)
        give(gift, entry.at[core], 2 * i + 1).start()

    my_rows = pl.ds(pl.multiple_of(core * tall, tall), tall)
    decay = []
    for s in range(2):
        power = rate_of(chan[s, my_rows, :].astype(F32))
        for _ in range(6):
            power = power * power
        decay.append(power)

    def later_by(times, state, more):
        return tuple(g**times * x + y for g, x, y in zip(decay, state, more))

    ones = jnp.ones((tall, LANES), F32)
    pass_on(
        0,
        cars,
        carsib,
        cartot,
        carall,
        cargift,
        start,
        functools.partial(later_by, 1),
        functools.partial(later_by, 2),
        functools.partial(later_by, 1),
        (ones, ones),
    )

    def climb_row(h, r, g):
        q = h * tall + r
        at = pl.ds(q, 1)
        here = pl.ds(r, 1)
        cols = pl.ds(pl.multiple_of(q * LANES, LANES), LANES)
        avg = []
        for s in range(2):
            keep = jnp.broadcast_to(rate_of(rates(s, at)), (8, LANES))
            carry = jnp.broadcast_to(start[h, s, here, :], (8, LANES))
            power = keep * keep
            power = power * power
            power = power * power
            for bit in (1, 2, 4):
                carry = jnp.where((seg_id // bit) % 2 == 1, carry * power, carry)
                power = power * power
            entry = seg[s, q] + carry
            values = []
            for i in range(8):
                entry = entry * keep
                values.append(lev[s, q, 8 * i : 8 * i + 8] + entry)
            avg.append(values)
        quotient = [avg[0][i] / avg[1][i] for i in range(8)]
        ratio[:, cols] = natural(g, quotient)
        rate = jnp.broadcast_to(0.5 + rates(2, at) * (1.0 / 64.0), (8, LANES))
        climb = quotient[0] - rate
        low = climb
        climbs, lows = [climb], [low]
        for i in range(1, 8):
            climb = climb + (quotient[i] - rate)
            low = jnp.minimum(low, climb)
            climbs.append(climb)
            lows.append(low)
        whole = climb
        for by in (1, 2, 4):
            whole = whole + shifted(whole, by, 0.0)
        base = shifted(whole, 1, 0.0)
        least = base + low
        for by in (1, 2, 4):
            least = jnp.minimum(least, shifted(least, by, jnp.inf))
        floor = shifted(least, 1, jnp.inf)
        for i in range(8):
            up = base + climbs[i]
            lev[0, q, 8 * i : 8 * i + 8] = up
            lev[1, q, 8 * i : 8 * i + 8] = jnp.minimum(floor, base + lows[i])
        sums[h, 0, here, :] = whole[7:8]
        sums[h, 1, here, :] = least[7:8]

    def climb_group(i, c):
        second = i * GROUP // tall

        @pl.when(i * GROUP == tall)
        def _():
            give(cargift, start.at[1 - core], 1).wait_recv()

        h = jnp.where(second == 0, core, 1 - core)
        for g in range(GROUP):
            climb_row(h, i * GROUP - second * tall + g, g)
        return c

    lax.fori_loop(0, ROWS // GROUP, climb_group, 0)

    stores[1].start()
    stores[2].start()

    def add_up(state, more):
        return state[0] + more[0], jnp.minimum(state[1], state[0] + more[1])

    zeros = jnp.zeros((tall, LANES), F32)
    pass_on(
        1, sums, sumsib, sumtot, sumall, sumgift, prior, add_up, add_up, add_up, (zeros, zeros)
    )
    give(sumgift, prior.at[1 - core], 3).wait_recv()
    last = pltpu.make_async_copy(prior, prior_far, store_sem.at[3])
    last.start()

    @pl.when(tm < nt - 1)
    def _():
        for chunk in range(chunks):
            rim_copy(chunk).wait_send()

    for i in range(per + 1):
        all1(i).wait_send()
    for i in range(per + 1):
        all2(i).wait_send()
    all_scales1().wait_send()
    all_scales2().wait_send()
    @pl.when(tm > 0)
    def _():
        for chunk in range(chunks):
            spill_scale(chunk).wait_send()
            spill(chunk).wait_send()

    for i, (own, sib, gift, entry) in enumerate(
        ((cars, carsib, cargift, start), (sums, sumsib, sumgift, prior))
    ):
        give(own.at[1 - core], sib, 2 * i).wait_send()
        give(gift, entry.at[core], 2 * i + 1).wait_send()

    def sent_on(j, c):
        to_later(cartot, carall, 0, j).wait_send()
        to_later(sumtot, sumall, 1, j).wait_send()
        return c

    lax.fori_loop(1, nz - chip, sent_on, 0)
    for store in stores:
        store.wait()
    last.wait()


def finish(
    filtered_far,
    ratio_far,
    lev_far,
    prior_far,
    limit_far,
    filtered_out,
    ratio_out,
    ph_out,
    filtered,
    ratio,
    lev,
    prior,
    limit,
    ph,
    temp,
    load_sem,
    store_sem,
):
    groups = ROWS // GROUP
    loads = [
        pltpu.make_async_copy(src, dst, load_sem.at[i])
        for i, (src, dst) in enumerate(
            [(prior_far, prior), (limit_far, limit), (filtered_far, filtered), (ratio_far, ratio)]
            + [(lev_far.at[:, pl.ds(4 * i, 4)], lev.at[:, pl.ds(4 * i, 4)]) for i in range(groups)]
        )
    ]
    for i in (0, 1, 4, 5, 6, 7, 2, 3):
        loads[i].start()
    stores = [
        pltpu.make_async_copy(filtered, filtered_out, store_sem.at[0]),
        pltpu.make_async_copy(ratio, ratio_out, store_sem.at[1]),
    ]
    loads[0].wait()
    loads[1].wait()
    for i in range(groups):
        loads[4 + i].wait()
        for g in range(GROUP):
            q = i * GROUP + g
            h, r = divmod(q, ROWS // 2)
            base = jnp.broadcast_to(prior[h, 0, r : r + 1, :], (8, LANES))
            low = jnp.broadcast_to(prior[h, 1, r : r + 1, :], (8, LANES))
            scale = jnp.broadcast_to(1.0 / limit[q : q + 1, :].astype(F32), (8, LANES))
            out = []
            for k in range(8):
                climb = base + lev[0, q, 8 * k : 8 * k + 8]
                lowest = jnp.minimum(low, base + lev[1, q, 8 * k : 8 * k + 8])
                out.append((climb - lowest) * scale)
            ph[:, q * LANES : (q + 1) * LANES] = in_order(temp, g, out)
        span = pl.ds(i * GROUP * LANES, GROUP * LANES)
        stores.append(
            pltpu.make_async_copy(ph.at[:, span], ph_out.at[:, span], store_sem.at[2 + i])
        )
        stores[-1].start()
        if i < 2:
            loads[2 + i].wait()
            stores[i].start()
    for store in stores:
        store.wait()


def body(nf, nt, strain, fan_cut, sta_len, lta_len, drift_code, threshold):
    per = BINS // nf
    rows = nf * ROWS
    total = rows * LANES
    half = rows // 2
    tabs = [jnp.asarray(t) for t in tables(total)]
    per_chan = [v.reshape(ROWS, LANES) for v in (sta_len, lta_len, drift_code, threshold)]
    far = pl.BlockSpec(memory_space=pl.ANY)
    dma = pltpu.SemaphoreType.DMA
    i16 = jnp.int16
    chans = ROWS * LANES
    results = pl.pallas_call(
        functools.partial(kernel, nf, nt),
        out_shape=(
            jax.ShapeDtypeStruct((HOP, chans), BF16),
            jax.ShapeDtypeStruct((HOP, chans), F32),
            jax.ShapeDtypeStruct((2, ROWS, HOP, LANES), F32),
            jax.ShapeDtypeStruct((2, 2, ROWS // 2, LANES), F32),
        ),
        in_specs=[far] * 12,
        out_specs=(far,) * 4,
        scratch_shapes=[
            pltpu.VMEM((HOP, chans), BF16),
            pltpu.SMEM((BINS,), jnp.int32),
            pltpu.VMEM((3, ROWS, LANES), jnp.int32),
        ]
        + [pltpu.VMEM(t.shape, F32) for t in tabs]
        + [
            pltpu.VMEM((2 * FRAME, FRAME), BF16),
            pltpu.VMEM((rows, 3 * half), BF16),
            pltpu.VMEM((6 * LANES, 2 * LANES), BF16),
            pltpu.VMEM((6 * LANES, 2 * LANES), BF16),
            pltpu.VMEM((FRAME, 3 * FRAME), BF16),
            pltpu.VMEM((HOP, chans), BF16),
            pltpu.VMEM((HOP, chans), F32),
            pltpu.VMEM((HOP, chans), BF16),
            pltpu.VMEM((FRAME, ROWS, LANES), F32),
            pltpu.VMEM((2, BINS, ROWS, LANES), i16),
            pltpu.VMEM((nf, per, ROWS, LANES), i16),
            pltpu.VMEM((per, nf, ROWS, LANES), i16),
            pltpu.VMEM((2, 1, LANES), F32),
            pltpu.VMEM((nf, 2, 1, LANES), F32),
            pltpu.VMEM((2, 3 * half, 2 * LANES), BF16),
            pltpu.VMEM((2, 3 * half, 2 * LANES), BF16),
            pltpu.VMEM((per, nf, 2, ROWS, LANES), i16),
            pltpu.VMEM((per - 1, nf, 2, ROWS, LANES), i16),
            pltpu.VMEM((2, nf, ROWS, LANES), i16),
            pltpu.VMEM((2, per, 1, LANES), F32),
            pltpu.VMEM((nf, per, 1, LANES), F32),
            pltpu.VMEM((2, BINS, ROWS, LANES), F32),
            pltpu.VMEM((ROWS, HOP, LANES), F32),
            pltpu.VMEM((ROWS, HOP, LANES), F32),
            pltpu.VMEM((ROWS, HOP, LANES), i16),
            pltpu.VMEM((ROWS, HOP, LANES), i16),
            pltpu.VMEM((4, 1, LANES), F32),
            pltpu.VMEM((4, 1, LANES), F32),
            pltpu.VMEM((2, ROWS, HOP, LANES), F32),
            pltpu.VMEM((2, ROWS, 8, LANES), F32),
        ]
        + 2
        * [
            pltpu.VMEM((2, 2, ROWS // 2, LANES), F32),
            pltpu.VMEM((2, ROWS // 2, LANES), F32),
            pltpu.VMEM((2, ROWS // 2, LANES), F32),
            pltpu.VMEM((nt // 2, 2, ROWS // 2, LANES), F32),
            pltpu.VMEM((2, ROWS // 2, LANES), F32),
            pltpu.VMEM((2, 2, ROWS // 2, LANES), F32),
        ]
        + [
            pltpu.VMEM((GROUP, HOP, LANES), F32),
            dma((4,)),
            dma((4,)),
            dma((per + 1,)),
            dma((per + 1,)),
            dma((1,)),
            dma((1,)),
            dma((per + 1,)),
            dma((per + 1,)),
            dma((1,)),
            dma((1,)),
            dma((4,)),
            dma((4,)),
            dma((4,)),
            dma((4,)),
            dma((4,)),
            dma((4,)),
            dma((2, nt // 2)),
            dma((2, nt // 2)),
            dma((12,)),
            dma((4,)),
        ],
        compiler_params=pltpu.CompilerParams(
            collective_id=0, has_side_effects=True, vmem_limit_bytes=64 * 1024 * 1024
        ),
    )(strain, fan_cut, *per_chan[:3], *tabs)
    return pl.pallas_call(
        finish,
        out_shape=(
            jax.ShapeDtypeStruct((HOP, chans), BF16),
            jax.ShapeDtypeStruct((HOP, chans), F32),
            jax.ShapeDtypeStruct((HOP, chans), F32),
        ),
        in_specs=[far] * 5,
        out_specs=(far,) * 3,
        scratch_shapes=[
            pltpu.VMEM((HOP, chans), BF16),
            pltpu.VMEM((HOP, chans), F32),
            pltpu.VMEM((2, ROWS, HOP, LANES), F32),
            pltpu.VMEM((2, 2, ROWS // 2, LANES), F32),
            pltpu.VMEM((ROWS, LANES), jnp.int32),
            pltpu.VMEM((HOP, chans), F32),
            pltpu.VMEM((GROUP, HOP, LANES), F32),
            dma((8,)),
            dma((6,)),
        ],
        compiler_params=pltpu.CompilerParams(vmem_limit_bytes=64 * 1024 * 1024),
    )(*results, per_chan[3])


def solution(mesh):
    return jax.shard_map(
        functools.partial(body, mesh.shape["fiber"], mesh.shape["tm"]),
        mesh=mesh,
        in_specs=(P("tm", "fiber"), P(), P("fiber"), P("fiber"), P("fiber"), P("fiber")),
        out_specs=(P("tm", "fiber"), P("tm", "fiber"), P("tm", "fiber")),
        check_vma=False,
    )
```

```python
import functools
import math

import jax
import jax.numpy as jnp
import numpy as np
from jax import lax
from jax.experimental import pallas as pl
from jax.experimental.pallas import tpu as pltpu
from jax.sharding import PartitionSpec as P

FRAME = 128
HOP = 64
BINS = 64
LANES = 128
ROWS = 16
GROUP = 4
TOP = 32512.0
MESH = pl.DeviceIdType.MESH
F32 = jnp.float32
BF16 = jnp.bfloat16


def time_order():
    rows = np.arange(HOP)
    return 8 * (rows % 8) + rows // 8


def tables(total):
    rows = total // LANES
    nf = rows // ROWS
    half = rows // 2
    n = np.arange(FRAME)
    f = np.arange(BINS)
    angle = 2.0 * math.pi / FRAME * ((f[:, None] * n[None, :]) % FRAME)
    window = 0.5 - 0.5 * np.cos(2.0 * math.pi / FRAME * n)
    analysis = np.concatenate([window * np.cos(angle), -window * np.sin(angle)], 0)
    weight = np.where(f == 0, 1.0, 2.0)[:, None] / FRAME
    synthesis = np.concatenate([weight * np.cos(angle), -weight * np.sin(angle)], 0).T
    order = time_order()
    arrived = np.arange(BINS).reshape(nf, BINS // nf).T.reshape(-1)
    synthesis = synthesis[np.concatenate([order, HOP + order])]
    synthesis = synthesis[:, np.concatenate([arrived, BINS + arrived])]
    a = np.arange(half)
    outer = 2.0 * math.pi / half * ((a[:, None] * a[None, :]) % half)
    outer = np.concatenate([np.cos(outer), -np.sin(outer)], 0)
    step = np.broadcast_to(2.0 * math.pi / rows * a[:, None], (half, LANES))
    step = np.concatenate([np.cos(step), -np.sin(step)], 1)
    b = np.arange(LANES)
    wave = np.concatenate([2 * a, 2 * a + 1])
    turn = 2.0 * math.pi / total * ((wave[:, None] * b[None, :]) % total)
    turn = np.concatenate([np.cos(turn), -np.sin(turn)], 1)
    inner = 2.0 * math.pi / LANES * ((b[:, None] * b[None, :]) % LANES)
    cos, sin = np.cos(inner), np.sin(inner)
    forward = np.block([[cos, -sin], [sin, cos]])
    inverse = np.block([[cos, sin], [-sin, cos]]) / total
    return [t.astype(np.float32) for t in (analysis, outer, forward, inverse, synthesis, step, turn)]


def split(x):
    high = x.astype(BF16)
    return high, (x - high.astype(F32)).astype(BF16)


def across(x):
    high, low = split(x)
    return jnp.concatenate([high, low, high], axis=1)


def peak_of(x):
    top = jnp.max(jnp.max(jnp.abs(x), axis=0, keepdims=True), axis=1, keepdims=True)
    return jnp.maximum(top, 1e-30)


def in_order(temp, g, vectors):
    for i in range(8):
        temp[g, pl.ds(i, 8, stride=8), :] = vectors[i]
    return temp[g]


def coded(x, gain):
    return jnp.round(x * gain).astype(jnp.int32).astype(jnp.int16)


def kernel(
    nf,
    nt,
    *refs,
):
    (
        strain_far,
        cut_far,
        sta_far,
        lta_far,
        drift_far,
        ana_far,
        outer_far,
        fwd_far,
        inv_far,
        syn_far,
        step_far,
        turn_far,
        filtered_far,
        ratio_far,
        lev_far,
        prior_far,
        strain,
        cut,
        chan,
        ana_raw,
        outer_raw,
        fwd_raw,
        inv_raw,
        syn_raw,
        step,
        turn,
        ana,
        outer,
        fwd,
        inv,
        syn,
        filtered,
        ratio,
        rim,
        spec,
        snd1,
        rcv1,
        scs1,
        scr1,
        x3,
        z3,
        snd2,
        rcve,
        rcvl,
        scs2,
        scr2,
        deco,
        head,
        tail,
        sps,
        spr,
        sss,
        ssr,
        lev,
        seg,
        cars,
        carsib,
        cartot,
        carall,
        cargift,
        start,
        sums,
        sumsib,
        sumtot,
        sumall,
        sumgift,
        prior,
        temp,
        rim_s,
        rim_r,
        s1s,
        s1r,
        c1s,
        c1r,
        s2s,
        s2r,
        c2s,
        c2r,
        sp_s,
        sp_r,
        ss_s,
        ss_r,
        sib_s,
        sib_r,
        z_s,
        z_r,
        load_sem,
        store_sem,
    ) = refs
    me = lax.axis_index("fiber")
    tm = lax.axis_index("tm")
    per = BINS // nf
    rows = nf * ROWS
    half = rows // 2
    total = rows * LANES
    later, earlier = lax.rem(tm + 1, nt), lax.rem(tm + nt - 1, nt)

    def remote(src, dst, send, recv, **to):
        return pltpu.make_async_remote_copy(
            src_ref=src, dst_ref=dst, send_sem=send, recv_sem=recv, device_id=to, device_id_type=MESH
        )

    barrier = pltpu.get_barrier_semaphore()

    width = 4
    lines = nf // width

    line = me // width
    mine = lax.rem(me, width)
    beside = [lax.rem(mine + i, width) for i in range(width)]

    def each_peer(act):
        def four(g, c):
            back = (g + 1) // 2
            down = lines // 2 + jnp.where(g % 2 == 0, back, -back)
            at = lax.rem(line + down, lines) * width
            for i in range(width):
                act(at + beside[i])
            return c

        lax.fori_loop(0, lines - 1, four, 0)
        for i in range(1, width):
            act(me - mine + beside[i])

    def greet(**to):
        pl.semaphore_signal(barrier, inc=1, device_id=to, device_id_type=MESH)

    nz = nt // 2
    friends = list(dict.fromkeys((1, nt - 1, *range(2, nt, 2))))
    for j in friends:
        greet(tm=lax.rem(tm + j, nt))
    for g in range(lines):
        down = lines // 2 + (g + 1) // 2 * (1 if g % 2 == 0 else -1)
        at = lax.rem(line + down, lines) * width
        for i in range(1 if g == lines - 1 else 0, width):
            greet(fiber=at + beside[i])

    loads = [
        pltpu.make_async_copy(src, dst, load_sem.at[i])
        for i, (src, dst) in enumerate(
            [
                (ana_far, ana_raw),
                (strain_far, strain),
                (outer_far, outer_raw),
                (fwd_far, fwd_raw),
                (inv_far, inv_raw),
                (syn_far, syn_raw),
                (step_far, step),
                (turn_far, turn),
                (cut_far, cut),
                (sta_far, chan.at[0]),
                (lta_far, chan.at[1]),
                (drift_far, chan.at[2]),
            ]
        )
    ]
    for load in loads:
        load.start()

    def rates(i, at):
        return chan[i, at, :].astype(F32)

    pl.semaphore_wait(barrier, nf - 1 + len(friends))

    chunks = 4
    wide = ROWS // chunks

    def rim_copy(c):
        span = pl.ds(c * wide * LANES, wide * LANES)
        return remote(strain_far.at[:, span], rim.at[:, span], rim_s.at[c], rim_r.at[c], tm=later)

    @pl.when(tm < nt - 1)
    def _():
        for chunk in range(chunks):
            rim_copy(chunk).start()

    for load in loads[:6]:
        load.wait()
    high, low = split(ana_raw[...])
    ana[...] = jnp.concatenate([high, low], axis=0)
    high, low = split(syn_raw[...])
    syn[...] = jnp.concatenate([high, high, low], axis=1)
    for raw, table in ((fwd_raw, fwd), (inv_raw, inv)):
        high, low = split(raw[...])
        table[...] = jnp.concatenate([high, high, low], axis=0)
    high, low = split(outer_raw[...])
    outer[...] = jnp.concatenate([high, high, low], axis=1)

    tall = ROWS // 2

    def scale1(to):
        return remote(scs1, scr1.at[me], c1s.at[0], c1r.at[0], fiber=to)

    def data1(i, to):
        if i < 2:
            src, dst = snd1.at[to * per, i], rcv1.at[0, me, i]
        else:
            src, dst = snd1.at[to * per + i - 1], rcv1.at[i - 1, me]
        return remote(src, dst, s1s.at[i], s1r.at[i], fiber=to)

    def of_all(ref, send, recv):
        return remote(ref, ref, send, recv, fiber=lax.rem(me + 1, nf))

    def all1(i):
        if isinstance(i, int) and i < 2:
            ref = rcv1.at[0, pl.ds(0, nf - 1), i]
        else:
            ref = rcv1.at[i - 1, pl.ds(0, nf - 1)]
        return of_all(ref, s1s.at[i], s1r.at[i])

    def all_scales1():
        return of_all(scr1.at[pl.ds(0, nf - 1)], c1s.at[0], c1r.at[0])

    for h in range(2):
        peak = jnp.zeros((1, 2 * LANES), F32)
        for chunk in range(h * chunks // 2, (h + 1) * chunks // 2):
            pl.when(tm > 0)(rim_copy(chunk).wait_recv)
            for q in range(chunk * wide, (chunk + 1) * wide, 2):
                cols = slice(q * LANES, (q + 2) * LANES)
                before = jnp.where(tm > 0, rim[:, cols].astype(F32), 0.0).astype(BF16)
                frame = jnp.concatenate([before, strain[:, cols]], axis=0)
                both = jnp.dot(ana[...], frame, preferred_element_type=F32)
                got = both[:FRAME] + both[FRAME:]
                spec[:, q, :] = got[:, :LANES]
                spec[:, q + 1, :] = got[:, LANES:]
                peak = jnp.maximum(peak, jnp.max(jnp.abs(got), axis=0, keepdims=True))
        peak = peak_of(peak)
        gain = TOP / peak
        scs1[h] = jnp.broadcast_to(peak * (1.0 / TOP), (1, LANES))
        scr1[me, h] = scs1[h]

        half_rows = slice(h * tall, (h + 1) * tall)
        re, im = spec[:BINS, half_rows, :], spec[BINS:, half_rows, :]
        snd1[:, h] = coded(jnp.concatenate([re, im], axis=1), gain)
        if h == 0:

            each_peer(lambda to: data1(0, to).start())
        else:

            def send1(j):
                scale1(j).start()
                data1(1, j).start()

            each_peer(send1)
            for b in range(1, per):
                each_peer(lambda to: data1(1 + b, to).start())
            for b in range(per):
                rcv1[b, me] = snd1[me * per + b]

    all1(0).wait_recv()
    all1(1).wait_recv()
    all_scales1().wait_recv()

    for load in loads[6:]:
        load.wait()
    peers = nf // 2

    final = per - 1

    def scale2(to):
        return remote(scs2.at[to // peers], scr2.at[me], c2s.at[0], c2r.at[0], fiber=to)

    def early2(b, to):
        return remote(snd2.at[b, to], rcve.at[b, me], s2s.at[b], s2r.at[b], fiber=to)

    def last2(h, to):
        i = final + h
        return remote(snd2.at[final, to, h], rcvl.at[h, me], s2s.at[i], s2r.at[i], fiber=to)

    def all2(i):
        if i < final:
            ref = rcve.at[i, pl.ds(0, nf - 1)]
        else:
            ref = rcvl.at[i - final, pl.ds(0, nf - 1)]
        return of_all(ref, s2s.at[i], s2r.at[i])

    def all_scales2():
        return of_all(scr2.at[pl.ds(0, nf - 1)], c2s.at[0], c2r.at[0])

    lane = lax.broadcasted_iota(jnp.int32, (half, LANES), 1)
    row = lax.broadcasted_iota(jnp.int32, (half, LANES), 0)

    def parts(x):
        return x[:, :LANES], x[:, LANES:]

    def put(ref, e, at, size, x):
        high, low = split(x)
        for i, part in enumerate((high, low, high)):
            ref[e, i * half + at : i * half + at + size, :] = part

    def transform(b):
        pl.when(b > 0)(all1(1 + b).wait_recv)
        limit_k = cut[me * per + b]

        def values(p):
            pieces = [rcv1[b, p, h].astype(F32) * scr1[p, h] for h in range(2)]
            return jnp.concatenate(
                [jnp.concatenate([x[i * tall : (i + 1) * tall] for x in pieces], 0) for i in range(2)],
                axis=1,
            )

        for p in range(peers):
            at = p * ROWS
            early, late = values(p), values(p + peers)
            wr, wi = parts(step[at : at + ROWS, :])
            put(x3, 0, at, ROWS, early + late)
            re, im = parts(early - late)
            x = jnp.concatenate([re * wr - im * wi, re * wi + im * wr], axis=1)
            put(x3, 1, at, ROWS, x)

        def waves(e, c):
            pq = jnp.dot(outer[...], x3[e], preferred_element_type=F32)
            pr, pi = parts(pq[:half])
            qr, qi = parts(pq[half:])
            re, im = pr - qi, pi + qr
            tr, ti = parts(turn[pl.ds(pl.multiple_of(e * half, half), half), :])
            y = jnp.concatenate([re * tr - im * ti, re * ti + im * tr], axis=1)
            wr, wi = parts(jnp.dot(across(y), fwd[...], preferred_element_type=F32))
            k = 2 * row + e + rows * lane
            keep = jnp.minimum(k, total - k) <= limit_k
            w = jnp.concatenate([jnp.where(keep, wr, 0.0), jnp.where(keep, wi, 0.0)], axis=1)
            re, im = parts(jnp.dot(across(w), inv[...], preferred_element_type=F32))
            put(z3, e, 0, half, jnp.concatenate([re * tr + im * ti, im * tr - re * ti], axis=1))
            return c

        lax.fori_loop(0, 2, waves, 0)

        back = []
        for e in range(2):
            pq = jnp.dot(outer[...], z3[e], preferred_element_type=F32)
            pr, pi = parts(pq[:half])
            qr, qi = parts(pq[half:])
            back.append((pr + qi, pi - qr))
        (ur, ui), (re, im) = back
        wr, wi = parts(step[...])
        vr, vi = re * wr + im * wi, im * wr - re * wi
        for blk, (re, im) in enumerate(((ur + vr, ui + vi), (ur - vr, ui - vi))):
            top = peak_of(jnp.maximum(jnp.abs(re), jnp.abs(im)))
            scs2[blk, b] = jnp.broadcast_to(top * (1.0 / TOP), (1, LANES))
            re = re.reshape(peers, 2, tall, LANES)
            im = im.reshape(peers, 2, tall, LANES)
            code = coded(jnp.concatenate([re, im], axis=2), TOP / top)
            span = slice(blk * peers, (blk + 1) * peers)
            snd2[b, span] = code

    def bin_step(b, c):
        transform(b)

        @pl.when(b < final)
        def _():
            each_peer(lambda to: early2(b, to).start())

        return c

    lax.fori_loop(0, per, bin_step, 0)

    def send2(to):
        scale2(to).start()
        last2(0, to).start()

    each_peer(send2)
    each_peer(lambda to: last2(1, to).start())
    for b in range(final):
        rcve[b, me] = snd2[b, me]
    for h in range(2):
        rcvl[h, me] = snd2[final, me, h]
    scr2[me] = scs2[me // peers]

    def back_again(h):
        if h == 0:
            for i in range(per):
                all2(i).wait_recv()
            all_scales2().wait_recv()
        else:
            all2(per).wait_recv()

        for b in range(per):
            x = rcve[b, :, h] if b < final else rcvl[h]
            x = x.astype(F32) * scr2[:, b]
            to = slice(b * nf, (b + 1) * nf)
            deco[0, to, h * tall : (h + 1) * tall] = x[:, :tall]
            deco[1, to, h * tall : (h + 1) * tall] = x[:, tall:]

    def spill(c):
        span = pl.ds(c * wide, wide)
        return remote(sps.at[span], spr.at[span], sp_s.at[c], sp_r.at[c], tm=earlier)

    def spill_scale(c):
        return remote(sss.at[c], ssr.at[c], ss_s.at[c], ss_r.at[c], tm=earlier)

    for chunk in range(chunks):
        if chunk % (chunks // 2) == 0:
            back_again(chunk // (chunks // 2))
        top = jnp.full((1, 1), 1e-30, F32)
        for q in range(chunk * wide, (chunk + 1) * wide, 2):
            x = jnp.concatenate(
                [
                    jnp.concatenate([deco[0, :, q, :], deco[1, :, q, :]], axis=0),
                    jnp.concatenate([deco[0, :, q + 1, :], deco[1, :, q + 1, :]], axis=0),
                ],
                axis=1,
            )
            high, low = split(x)
            got = jnp.dot(
                syn[...], jnp.concatenate([high, low, high], axis=0), preferred_element_type=F32
            )
            for i in range(2):
                head[q + i] = got[:HOP, i * LANES : (i + 1) * LANES]
                tail[q + i] = got[HOP:, i * LANES : (i + 1) * LANES]
            top = jnp.maximum(top, peak_of(got[:HOP]))
        sss[chunk] = jnp.broadcast_to(top * (1.0 / TOP), (1, LANES))
        for q in range(chunk * wide, (chunk + 1) * wide):
            sps[q] = coded(head[q], TOP / top)

        @pl.when(tm > 0)
        def _():
            spill_scale(chunk).start()
            spill(chunk).start()


    seg_id = lax.broadcasted_iota(jnp.int32, (8, LANES), 0)

    def shifted(x, by, fill):
        return jnp.where(seg_id >= by, pltpu.roll(x, by, 0), fill)

    def rate_of(length):
        return 1.0 - 1.0 / length

    def natural(g, vectors):
        return in_order(temp, g, vectors)

    for chunk in range(chunks):
        @pl.when(tm < nt - 1)
        def _():
            spill_scale(chunk).wait_recv()
            spill(chunk).wait_recv()

        def scan_row(q, g):
            at = pl.ds(q, 1)
            cols = slice(q * LANES, (q + 1) * LANES)
            heads = jnp.where(tm < nt - 1, spr[q].astype(F32) * ssr[chunk], 0.0)
            rounded = (tail[q] + heads).astype(BF16).astype(F32)
            part = [rounded[8 * i : 8 * i + 8] for i in range(8)]
            filtered[:, cols] = natural(g, part).astype(BF16)
            energy = [v * v for v in part]
            for s in range(2):
                keep = jnp.broadcast_to(rate_of(rates(s, at)), (8, LANES))
                gain = 1.0 - keep
                level = gain * energy[0]
                lev[s, q, 0:8] = level
                for i in range(1, 8):
                    level = keep * level + gain * energy[i]
                    lev[s, q, 8 * i : 8 * i + 8] = level
                power = keep * keep
                power = power * power
                power = power * power
                for by in (1, 2, 4):
                    level = level + power * shifted(level, by, 0.0)
                    power = power * power
                seg[s, q] = shifted(level, 1, 0.0)
                cars[q // tall, s, q % tall : q % tall + 1, :] = level[7:8]

        for g in range(wide):
            scan_row(chunk * wide + g, g)

    stores = [
        pltpu.make_async_copy(src, dst, store_sem.at[i])
        for i, (src, dst) in enumerate([(filtered, filtered_far), (ratio, ratio_far), (lev, lev_far)])
    ]
    stores[0].start()

    core = lax.rem(tm, 2)
    chip = tm // 2
    sibling = tm + 1 - 2 * core

    def give(src, dst, i):
        return remote(src, dst, sib_s.at[i], sib_r.at[i], tm=sibling)

    def to_later(snd, rcv, i, j):
        to = lax.rem(tm + 2 * j, nt)
        return remote(snd, rcv.at[chip], z_s.at[i, j], z_r.at[i, j], tm=to)

    def from_earlier(snd, rcv, i, j):
        back = lax.rem(tm + nt - 2 * j, nt)
        return remote(snd, rcv.at[chip - j], z_s.at[i, j], z_r.at[i, j], tm=back)

    def pair_of(ref):
        return ref[0], ref[1]

    def chosen(first, second):
        return tuple(jnp.where(core == 0, a, b) for a, b in zip(first, second))

    def pass_on(i, own, sib, tot, totr, gift, entry, join, apply, step, begin):
        half_away = give(own.at[1 - core], sib, 2 * i)
        half_away.start()
        half_away.wait_recv()
        mine, other = pair_of(own.at[core]), pair_of(sib)
        early, late = chosen(mine, other), chosen(other, mine)
        tot[0], tot[1] = join(early, late)

        def out(j, c):
            to_later(tot, totr, i, j).start()
            return c

        lax.fori_loop(1, nz - chip, out, 0)

        def come(j, c):
            from_earlier(tot, totr, i, j).wait_recv()
            return c

        lax.fori_loop(1, chip + 1, come, 0)
        state = lax.fori_loop(0, chip, lambda k, state: apply(state, pair_of(totr.at[k])), begin)
        after = step(state, early)
        entry[core, 0], entry[core, 1] = chosen(state, after)
        gift[0], gift[1] = chosen(after, state)
        give(gift, entry.at[core], 2 * i + 1).start()

    my_rows = pl.ds(pl.multiple_of(core * tall, tall), tall)
    decay = []
    for s in range(2):
        power = rate_of(chan[s, my_rows, :].astype(F32))
        for _ in range(6):
            power = power * power
        decay.append(power)

    def later_by(times, state, more):
        return tuple(g**times * x + y for g, x, y in zip(decay, state, more))

    ones = jnp.ones((tall, LANES), F32)
    pass_on(
        0,
        cars,
        carsib,
        cartot,
        carall,
        cargift,
        start,
        functools.partial(later_by, 1),
        functools.partial(later_by, 2),
        functools.partial(later_by, 1),
        (ones, ones),
    )

    def climb_row(h, r):
        q = h * tall + r
        g = r % GROUP
        at = pl.ds(q, 1)
        here = slice(r, r + 1)
        cols = pl.ds(pl.multiple_of(q * LANES, LANES), LANES)
        avg = []
        for s in range(2):
            keep = jnp.broadcast_to(rate_of(rates(s, at)), (8, LANES))
            carry = jnp.broadcast_to(start[h, s, here, :], (8, LANES))
            power = keep * keep
            power = power * power
            power = power * power
            for bit in (1, 2, 4):
                carry = jnp.where((seg_id // bit) % 2 == 1, carry * power, carry)
                power = power * power
            entry = seg[s, q] + carry
            values = []
            for i in range(8):
                entry = entry * keep
                values.append(lev[s, q, 8 * i : 8 * i + 8] + entry)
            avg.append(values)
        quotient = [avg[0][i] / avg[1][i] for i in range(8)]
        ratio[:, cols] = natural(g, quotient)
        rate = jnp.broadcast_to(0.5 + rates(2, at) * (1.0 / 64.0), (8, LANES))
        climb = quotient[0] - rate
        low = climb
        climbs, lows = [climb], [low]
        for i in range(1, 8):
            climb = climb + (quotient[i] - rate)
            low = jnp.minimum(low, climb)
            climbs.append(climb)
            lows.append(low)
        whole = climb
        for by in (1, 2, 4):
            whole = whole + shifted(whole, by, 0.0)
        base = shifted(whole, 1, 0.0)
        least = base + low
        for by in (1, 2, 4):
            least = jnp.minimum(least, shifted(least, by, jnp.inf))
        floor = shifted(least, 1, jnp.inf)
        for i in range(8):
            up = base + climbs[i]
            lev[0, q, 8 * i : 8 * i + 8] = up
            lev[1, q, 8 * i : 8 * i + 8] = jnp.minimum(floor, base + lows[i])
        sums[h, 0, here, :] = whole[7:8]
        sums[h, 1, here, :] = least[7:8]

    for r in range(tall):
        climb_row(core, r)
    give(cargift, start.at[1 - core], 1).wait_recv()
    for r in range(tall):
        climb_row(1 - core, r)

    stores[1].start()
    stores[2].start()

    def add_up(state, more):
        return state[0] + more[0], jnp.minimum(state[1], state[0] + more[1])

    zeros = jnp.zeros((tall, LANES), F32)
    pass_on(
        1, sums, sumsib, sumtot, sumall, sumgift, prior, add_up, add_up, add_up, (zeros, zeros)
    )
    give(sumgift, prior.at[1 - core], 3).wait_recv()
    last = pltpu.make_async_copy(prior, prior_far, store_sem.at[3])
    last.start()

    @pl.when(tm < nt - 1)
    def _():
        for chunk in range(chunks):
            rim_copy(chunk).wait_send()

    for i in range(per + 1):
        all1(i).wait_send()
    for i in range(per + 1):
        all2(i).wait_send()
    all_scales1().wait_send()
    all_scales2().wait_send()
    @pl.when(tm > 0)
    def _():
        for chunk in range(chunks):
            spill_scale(chunk).wait_send()
            spill(chunk).wait_send()

    for i, (own, sib, gift, entry) in enumerate(
        ((cars, carsib, cargift, start), (sums, sumsib, sumgift, prior))
    ):
        give(own.at[1 - core], sib, 2 * i).wait_send()
        give(gift, entry.at[core], 2 * i + 1).wait_send()

    def sent_on(j, c):
        to_later(cartot, carall, 0, j).wait_send()
        to_later(sumtot, sumall, 1, j).wait_send()
        return c

    lax.fori_loop(1, nz - chip, sent_on, 0)
    for store in stores:
        store.wait()
    last.wait()


def finish(
    filtered_far,
    ratio_far,
    lev_far,
    prior_far,
    limit_far,
    filtered_out,
    ratio_out,
    ph_out,
    filtered,
    ratio,
    lev,
    prior,
    limit,
    ph,
    temp,
    load_sem,
    store_sem,
):
    groups = ROWS // GROUP
    loads = [
        pltpu.make_async_copy(src, dst, load_sem.at[i])
        for i, (src, dst) in enumerate(
            [(prior_far, prior), (limit_far, limit), (filtered_far, filtered), (ratio_far, ratio)]
            + [(lev_far.at[:, pl.ds(4 * i, 4)], lev.at[:, pl.ds(4 * i, 4)]) for i in range(groups)]
        )
    ]
    for i in (0, 1, 4, 5, 6, 7, 2, 3):
        loads[i].start()
    stores = [
        pltpu.make_async_copy(filtered, filtered_out, store_sem.at[0]),
        pltpu.make_async_copy(ratio, ratio_out, store_sem.at[1]),
    ]
    loads[0].wait()
    loads[1].wait()
    for i in range(groups):
        loads[4 + i].wait()
        for g in range(GROUP):
            q = i * GROUP + g
            h, r = divmod(q, ROWS // 2)
            base = jnp.broadcast_to(prior[h, 0, r : r + 1, :], (8, LANES))
            low = jnp.broadcast_to(prior[h, 1, r : r + 1, :], (8, LANES))
            scale = jnp.broadcast_to(1.0 / limit[q : q + 1, :].astype(F32), (8, LANES))
            out = []
            for k in range(8):
                climb = base + lev[0, q, 8 * k : 8 * k + 8]
                lowest = jnp.minimum(low, base + lev[1, q, 8 * k : 8 * k + 8])
                out.append((climb - lowest) * scale)
            ph[:, q * LANES : (q + 1) * LANES] = in_order(temp, g, out)
        span = pl.ds(i * GROUP * LANES, GROUP * LANES)
        stores.append(
            pltpu.make_async_copy(ph.at[:, span], ph_out.at[:, span], store_sem.at[2 + i])
        )
        stores[-1].start()
        if i < 2:
            loads[2 + i].wait()
            stores[i].start()
    for store in stores:
        store.wait()


def body(nf, nt, strain, fan_cut, sta_len, lta_len, drift_code, threshold):
    per = BINS // nf
    rows = nf * ROWS
    total = rows * LANES
    half = rows // 2
    tabs = [jnp.asarray(t) for t in tables(total)]
    per_chan = [v.reshape(ROWS, LANES) for v in (sta_len, lta_len, drift_code, threshold)]
    far = pl.BlockSpec(memory_space=pl.ANY)
    dma = pltpu.SemaphoreType.DMA
    i16 = jnp.int16
    chans = ROWS * LANES
    results = pl.pallas_call(
        functools.partial(kernel, nf, nt),
        out_shape=(
            jax.ShapeDtypeStruct((HOP, chans), BF16),
            jax.ShapeDtypeStruct((HOP, chans), F32),
            jax.ShapeDtypeStruct((2, ROWS, HOP, LANES), F32),
            jax.ShapeDtypeStruct((2, 2, ROWS // 2, LANES), F32),
        ),
        in_specs=[far] * 12,
        out_specs=(far,) * 4,
        scratch_shapes=[
            pltpu.VMEM((HOP, chans), BF16),
            pltpu.SMEM((BINS,), jnp.int32),
            pltpu.VMEM((3, ROWS, LANES), jnp.int32),
        ]
        + [pltpu.VMEM(t.shape, F32) for t in tabs]
        + [
            pltpu.VMEM((2 * FRAME, FRAME), BF16),
            pltpu.VMEM((rows, 3 * half), BF16),
            pltpu.VMEM((6 * LANES, 2 * LANES), BF16),
            pltpu.VMEM((6 * LANES, 2 * LANES), BF16),
            pltpu.VMEM((FRAME, 3 * FRAME), BF16),
            pltpu.VMEM((HOP, chans), BF16),
            pltpu.VMEM((HOP, chans), F32),
            pltpu.VMEM((HOP, chans), BF16),
            pltpu.VMEM((FRAME, ROWS, LANES), F32),
            pltpu.VMEM((BINS, 2, ROWS, LANES), i16),
            pltpu.VMEM((per, nf, 2, ROWS, LANES), i16),
            pltpu.VMEM((2, 1, LANES), F32),
            pltpu.VMEM((nf, 2, 1, LANES), F32),
            pltpu.VMEM((2, 3 * half, 2 * LANES), BF16),
            pltpu.VMEM((2, 3 * half, 2 * LANES), BF16),
            pltpu.VMEM((per, nf, 2, ROWS, LANES), i16),
            pltpu.VMEM((per - 1, nf, 2, ROWS, LANES), i16),
            pltpu.VMEM((2, nf, ROWS, LANES), i16),
            pltpu.VMEM((2, per, 1, LANES), F32),
            pltpu.VMEM((nf, per, 1, LANES), F32),
            pltpu.VMEM((2, BINS, ROWS, LANES), F32),
            pltpu.VMEM((ROWS, HOP, LANES), F32),
            pltpu.VMEM((ROWS, HOP, LANES), F32),
            pltpu.VMEM((ROWS, HOP, LANES), i16),
            pltpu.VMEM((ROWS, HOP, LANES), i16),
            pltpu.VMEM((4, 1, LANES), F32),
            pltpu.VMEM((4, 1, LANES), F32),
            pltpu.VMEM((2, ROWS, HOP, LANES), F32),
            pltpu.VMEM((2, ROWS, 8, LANES), F32),
        ]
        + 2
        * [
            pltpu.VMEM((2, 2, ROWS // 2, LANES), F32),
            pltpu.VMEM((2, ROWS // 2, LANES), F32),
            pltpu.VMEM((2, ROWS // 2, LANES), F32),
            pltpu.VMEM((nt // 2, 2, ROWS // 2, LANES), F32),
            pltpu.VMEM((2, ROWS // 2, LANES), F32),
            pltpu.VMEM((2, 2, ROWS // 2, LANES), F32),
        ]
        + [
            pltpu.VMEM((GROUP, HOP, LANES), F32),
            dma((4,)),
            dma((4,)),
            dma((per + 1,)),
            dma((per + 1,)),
            dma((1,)),
            dma((1,)),
            dma((per + 1,)),
            dma((per + 1,)),
            dma((1,)),
            dma((1,)),
            dma((4,)),
            dma((4,)),
            dma((4,)),
            dma((4,)),
            dma((4,)),
            dma((4,)),
            dma((2, nt // 2)),
            dma((2, nt // 2)),
            dma((12,)),
            dma((4,)),
        ],
        compiler_params=pltpu.CompilerParams(
            collective_id=0, has_side_effects=True, vmem_limit_bytes=64 * 1024 * 1024
        ),
    )(strain, fan_cut, *per_chan[:3], *tabs)
    return pl.pallas_call(
        finish,
        out_shape=(
            jax.ShapeDtypeStruct((HOP, chans), BF16),
            jax.ShapeDtypeStruct((HOP, chans), F32),
            jax.ShapeDtypeStruct((HOP, chans), F32),
        ),
        in_specs=[far] * 5,
        out_specs=(far,) * 3,
        scratch_shapes=[
            pltpu.VMEM((HOP, chans), BF16),
            pltpu.VMEM((HOP, chans), F32),
            pltpu.VMEM((2, ROWS, HOP, LANES), F32),
            pltpu.VMEM((2, 2, ROWS // 2, LANES), F32),
            pltpu.VMEM((ROWS, LANES), jnp.int32),
            pltpu.VMEM((HOP, chans), F32),
            pltpu.VMEM((GROUP, HOP, LANES), F32),
            dma((8,)),
            dma((6,)),
        ],
        compiler_params=pltpu.CompilerParams(vmem_limit_bytes=64 * 1024 * 1024),
    )(*results, per_chan[3])


def solution(mesh):
    return jax.shard_map(
        functools.partial(body, mesh.shape["fiber"], mesh.shape["tm"]),
        mesh=mesh,
        in_specs=(P("tm", "fiber"), P(), P("fiber"), P("fiber"), P("fiber"), P("fiber")),
        out_specs=(P("tm", "fiber"), P("tm", "fiber"), P("tm", "fiber")),
        check_vma=False,
    )
```

```python
import functools
import math

import jax
import jax.numpy as jnp
import numpy as np
from jax import lax
from jax.experimental import pallas as pl
from jax.experimental.pallas import tpu as pltpu
from jax.sharding import PartitionSpec as P

FRAME = 128
HOP = 64
BINS = 64
LANES = 128
ROWS = 16
GROUP = 4
TOP = 32512.0
MESH = pl.DeviceIdType.MESH
F32 = jnp.float32
BF16 = jnp.bfloat16


def time_order():
    rows = np.arange(HOP)
    return 8 * (rows % 8) + rows // 8


def tables(total):
    rows = total // LANES
    nf = rows // ROWS
    half = rows // 2
    n = np.arange(FRAME)
    f = np.arange(BINS)
    angle = 2.0 * math.pi / FRAME * ((f[:, None] * n[None, :]) % FRAME)
    window = 0.5 - 0.5 * np.cos(2.0 * math.pi / FRAME * n)
    analysis = np.concatenate([window * np.cos(angle), -window * np.sin(angle)], 0)
    weight = np.where(f == 0, 1.0, 2.0)[:, None] / FRAME
    synthesis = np.concatenate([weight * np.cos(angle), -weight * np.sin(angle)], 0).T
    order = time_order()
    arrived = np.arange(BINS).reshape(nf, BINS // nf).T.reshape(-1)
    synthesis = synthesis[np.concatenate([order, HOP + order])]
    synthesis = synthesis[:, np.concatenate([arrived, BINS + arrived])]
    a = np.arange(half)
    outer = 2.0 * math.pi / half * ((a[:, None] * a[None, :]) % half)
    outer = np.concatenate([np.cos(outer), -np.sin(outer)], 0)
    step = np.broadcast_to(2.0 * math.pi / rows * a[:, None], (half, LANES))
    step = np.concatenate([np.cos(step), -np.sin(step)], 1)
    b = np.arange(LANES)
    wave = np.concatenate([2 * a, 2 * a + 1])
    turn = 2.0 * math.pi / total * ((wave[:, None] * b[None, :]) % total)
    turn = np.concatenate([np.cos(turn), -np.sin(turn)], 1)
    inner = 2.0 * math.pi / LANES * ((b[:, None] * b[None, :]) % LANES)
    cos, sin = np.cos(inner), np.sin(inner)
    forward = np.block([[cos, -sin], [sin, cos]])
    inverse = np.block([[cos, sin], [-sin, cos]]) / total
    return [t.astype(np.float32) for t in (analysis, outer, forward, inverse, synthesis, step, turn)]


def split(x):
    high = x.astype(BF16)
    return high, (x - high.astype(F32)).astype(BF16)


def across(x):
    high, low = split(x)
    return jnp.concatenate([high, low, high], axis=1)


def peak_of(x):
    top = jnp.max(jnp.max(jnp.abs(x), axis=0, keepdims=True), axis=1, keepdims=True)
    return jnp.maximum(top, 1e-30)


def in_order(temp, g, vectors):
    for i in range(8):
        temp[g, pl.ds(i, 8, stride=8), :] = vectors[i]
    return temp[g]


def coded(x, gain):
    return jnp.round(x * gain).astype(jnp.int32).astype(jnp.int16)


def kernel(
    nf,
    nt,
    *refs,
):
    (
        strain_far,
        cut_far,
        sta_far,
        lta_far,
        drift_far,
        ana_far,
        outer_far,
        fwd_far,
        inv_far,
        syn_far,
        step_far,
        turn_far,
        filtered_far,
        ratio_far,
        lev_far,
        prior_far,
        strain,
        cut,
        chan,
        ana_raw,
        outer_raw,
        fwd_raw,
        inv_raw,
        syn_raw,
        step,
        turn,
        ana,
        outer,
        fwd,
        inv,
        syn,
        filtered,
        ratio,
        rim,
        spec,
        snd1,
        rcv1,
        scs1,
        scr1,
        x3,
        z3,
        snd2,
        rcve,
        rcvl,
        scs2,
        scr2,
        deco,
        head,
        tail,
        sps,
        spr,
        sss,
        ssr,
        lev,
        seg,
        cars,
        carsib,
        cartot,
        carall,
        cargift,
        start,
        sums,
        sumsib,
        sumtot,
        sumall,
        sumgift,
        prior,
        temp,
        rim_s,
        rim_r,
        s1s,
        s1r,
        c1s,
        c1r,
        s2s,
        s2r,
        c2s,
        c2r,
        sp_s,
        sp_r,
        ss_s,
        ss_r,
        sib_s,
        sib_r,
        z_s,
        z_r,
        load_sem,
        store_sem,
    ) = refs
    me = lax.axis_index("fiber")
    tm = lax.axis_index("tm")
    per = BINS // nf
    rows = nf * ROWS
    half = rows // 2
    total = rows * LANES
    later, earlier = lax.rem(tm + 1, nt), lax.rem(tm + nt - 1, nt)

    def remote(src, dst, send, recv, **to):
        return pltpu.make_async_remote_copy(
            src_ref=src, dst_ref=dst, send_sem=send, recv_sem=recv, device_id=to, device_id_type=MESH
        )

    barrier = pltpu.get_barrier_semaphore()

    width = 4
    lines = nf // width

    line = me // width
    mine = lax.rem(me, width)
    beside = [lax.rem(mine + i, width) for i in range(width)]

    def each_peer(act):
        def four(g, c):
            back = (g + 1) // 2
            down = lines // 2 + jnp.where(g % 2 == 0, back, -back)
            at = lax.rem(line + down, lines) * width
            for i in range(width):
                act(at + beside[i])
            return c

        lax.fori_loop(0, lines - 1, four, 0)
        for i in range(1, width):
            act(me - mine + beside[i])

    def greet(**to):
        pl.semaphore_signal(barrier, inc=1, device_id=to, device_id_type=MESH)

    nz = nt // 2
    friends = list(dict.fromkeys((1, nt - 1, *range(2, nt, 2))))
    for j in friends:
        greet(tm=lax.rem(tm + j, nt))
    for g in range(lines):
        down = lines // 2 + (g + 1) // 2 * (1 if g % 2 == 0 else -1)
        at = lax.rem(line + down, lines) * width
        for i in range(1 if g == lines - 1 else 0, width):
            greet(fiber=at + beside[i])

    loads = [
        pltpu.make_async_copy(src, dst, load_sem.at[i])
        for i, (src, dst) in enumerate(
            [
                (ana_far, ana_raw),
                (strain_far, strain),
                (outer_far, outer_raw),
                (fwd_far, fwd_raw),
                (inv_far, inv_raw),
                (syn_far, syn_raw),
                (step_far, step),
                (turn_far, turn),
                (cut_far, cut),
                (sta_far, chan.at[0]),
                (lta_far, chan.at[1]),
                (drift_far, chan.at[2]),
            ]
        )
    ]
    for load in loads:
        load.start()

    def rates(i, at):
        return chan[i, at, :].astype(F32)

    pl.semaphore_wait(barrier, nf - 1 + len(friends))

    chunks = 4
    wide = ROWS // chunks

    def rim_copy(c):
        span = pl.ds(c * wide * LANES, wide * LANES)
        return remote(strain_far.at[:, span], rim.at[:, span], rim_s.at[c], rim_r.at[c], tm=later)

    @pl.when(tm < nt - 1)
    def _():
        for chunk in range(chunks):
            rim_copy(chunk).start()

    for load in loads[:6]:
        load.wait()
    high, low = split(ana_raw[...])
    ana[...] = jnp.concatenate([high, low], axis=0)
    high, low = split(syn_raw[...])
    syn[...] = jnp.concatenate([high, high, low], axis=1)
    for raw, table in ((fwd_raw, fwd), (inv_raw, inv)):
        high, low = split(raw[...])
        table[...] = jnp.concatenate([high, high, low], axis=0)
    high, low = split(outer_raw[...])
    outer[...] = jnp.concatenate([high, high, low], axis=1)

    tall = ROWS // 2

    def scale1(to):
        return remote(scs1, scr1.at[me], c1s.at[0], c1r.at[0], fiber=to)

    def data1(i, to):
        if i < 2:
            src, dst = snd1.at[to * per, i], rcv1.at[0, me, i]
        else:
            src, dst = snd1.at[to * per + i - 1], rcv1.at[i - 1, me]
        return remote(src, dst, s1s.at[i], s1r.at[i], fiber=to)

    def of_all(ref, send, recv):
        return remote(ref, ref, send, recv, fiber=lax.rem(me + 1, nf))

    def all1(i):
        if isinstance(i, int) and i < 2:
            ref = rcv1.at[0, pl.ds(0, nf - 1), i]
        else:
            ref = rcv1.at[i - 1, pl.ds(0, nf - 1)]
        return of_all(ref, s1s.at[i], s1r.at[i])

    def all_scales1():
        return of_all(scr1.at[pl.ds(0, nf - 1)], c1s.at[0], c1r.at[0])

    for h in range(2):
        peak = jnp.zeros((1, 2 * LANES), F32)
        for chunk in range(h * chunks // 2, (h + 1) * chunks // 2):
            pl.when(tm > 0)(rim_copy(chunk).wait_recv)
            for q in range(chunk * wide, (chunk + 1) * wide, 2):
                cols = slice(q * LANES, (q + 2) * LANES)
                before = jnp.where(tm > 0, rim[:, cols].astype(F32), 0.0).astype(BF16)
                frame = jnp.concatenate([before, strain[:, cols]], axis=0)
                both = jnp.dot(ana[...], frame, preferred_element_type=F32)
                got = both[:FRAME] + both[FRAME:]
                spec[:, q, :] = got[:, :LANES]
                spec[:, q + 1, :] = got[:, LANES:]
                peak = jnp.maximum(peak, jnp.max(jnp.abs(got), axis=0, keepdims=True))
        peak = peak_of(peak)
        gain = TOP / peak
        scs1[h] = jnp.broadcast_to(peak * (1.0 / TOP), (1, LANES))
        scr1[me, h] = scs1[h]

        half_rows = slice(h * tall, (h + 1) * tall)
        re, im = spec[:BINS, half_rows, :], spec[BINS:, half_rows, :]
        snd1[:, h] = coded(jnp.concatenate([re, im], axis=1), gain)
        if h == 0:

            each_peer(lambda to: data1(0, to).start())
        else:

            def send1(j):
                scale1(j).start()
                data1(1, j).start()

            each_peer(send1)
            for b in range(1, per):
                each_peer(lambda to: data1(1 + b, to).start())
            for b in range(per):
                rcv1[b, me] = snd1[me * per + b]

    all1(0).wait_recv()
    all1(1).wait_recv()
    all_scales1().wait_recv()

    for load in loads[6:]:
        load.wait()
    peers = nf // 2

    final = per - 1

    def scale2(to):
        return remote(scs2.at[to // peers], scr2.at[me], c2s.at[0], c2r.at[0], fiber=to)

    def early2(b, to):
        return remote(snd2.at[b, to], rcve.at[b, me], s2s.at[b], s2r.at[b], fiber=to)

    def last2(h, to):
        i = final + h
        return remote(snd2.at[final, to, h], rcvl.at[h, me], s2s.at[i], s2r.at[i], fiber=to)

    def all2(i):
        if i < final:
            ref = rcve.at[i, pl.ds(0, nf - 1)]
        else:
            ref = rcvl.at[i - final, pl.ds(0, nf - 1)]
        return of_all(ref, s2s.at[i], s2r.at[i])

    def all_scales2():
        return of_all(scr2.at[pl.ds(0, nf - 1)], c2s.at[0], c2r.at[0])

    lane = lax.broadcasted_iota(jnp.int32, (half, LANES), 1)
    row = lax.broadcasted_iota(jnp.int32, (half, LANES), 0)

    def parts(x):
        return x[:, :LANES], x[:, LANES:]

    def put(ref, e, at, size, x):
        high, low = split(x)
        for i, part in enumerate((high, low, high)):
            ref[e, i * half + at : i * half + at + size, :] = part

    def transform(b):
        pl.when(b > 0)(all1(1 + b).wait_recv)
        limit_k = cut[me * per + b]

        def values(p):
            pieces = [rcv1[b, p, h].astype(F32) * scr1[p, h] for h in range(2)]
            return jnp.concatenate(
                [jnp.concatenate([x[i * tall : (i + 1) * tall] for x in pieces], 0) for i in range(2)],
                axis=1,
            )

        for p in range(peers):
            at = p * ROWS
            early, late = values(p), values(p + peers)
            wr, wi = parts(step[at : at + ROWS, :])
            put(x3, 0, at, ROWS, early + late)
            re, im = parts(early - late)
            x = jnp.concatenate([re * wr - im * wi, re * wi + im * wr], axis=1)
            put(x3, 1, at, ROWS, x)

        def waves(e, c):
            pq = jnp.dot(outer[...], x3[e], preferred_element_type=F32)
            pr, pi = parts(pq[:half])
            qr, qi = parts(pq[half:])
            re, im = pr - qi, pi + qr
            tr, ti = parts(turn[e * half : (e + 1) * half, :])
            y = jnp.concatenate([re * tr - im * ti, re * ti + im * tr], axis=1)
            wr, wi = parts(jnp.dot(across(y), fwd[...], preferred_element_type=F32))
            k = 2 * row + e + rows * lane
            keep = jnp.minimum(k, total - k) <= limit_k
            w = jnp.concatenate([jnp.where(keep, wr, 0.0), jnp.where(keep, wi, 0.0)], axis=1)
            re, im = parts(jnp.dot(across(w), inv[...], preferred_element_type=F32))
            put(z3, e, 0, half, jnp.concatenate([re * tr + im * ti, im * tr - re * ti], axis=1))
            return c

        for e in range(2):
            waves(e, 0)

        back = []
        for e in range(2):
            pq = jnp.dot(outer[...], z3[e], preferred_element_type=F32)
            pr, pi = parts(pq[:half])
            qr, qi = parts(pq[half:])
            back.append((pr + qi, pi - qr))
        (ur, ui), (re, im) = back
        wr, wi = parts(step[...])
        vr, vi = re * wr + im * wi, im * wr - re * wi
        for blk, (re, im) in enumerate(((ur + vr, ui + vi), (ur - vr, ui - vi))):
            top = peak_of(jnp.maximum(jnp.abs(re), jnp.abs(im)))
            scs2[blk, b] = jnp.broadcast_to(top * (1.0 / TOP), (1, LANES))
            re = re.reshape(peers, 2, tall, LANES)
            im = im.reshape(peers, 2, tall, LANES)
            code = coded(jnp.concatenate([re, im], axis=2), TOP / top)
            span = slice(blk * peers, (blk + 1) * peers)
            snd2[b, span] = code

    def bin_step(b, c):
        transform(b)

        @pl.when(b < final)
        def _():
            each_peer(lambda to: early2(b, to).start())

        return c

    lax.fori_loop(0, per, bin_step, 0)

    def send2(to):
        scale2(to).start()
        last2(0, to).start()

    each_peer(send2)
    each_peer(lambda to: last2(1, to).start())
    for b in range(final):
        rcve[b, me] = snd2[b, me]
    for h in range(2):
        rcvl[h, me] = snd2[final, me, h]
    scr2[me] = scs2[me // peers]

    def back_again(h):
        if h == 0:
            for i in range(per):
                all2(i).wait_recv()
            all_scales2().wait_recv()
        else:
            all2(per).wait_recv()

        for b in range(per):
            x = rcve[b, :, h] if b < final else rcvl[h]
            x = x.astype(F32) * scr2[:, b]
            to = slice(b * nf, (b + 1) * nf)
            deco[0, to, h * tall : (h + 1) * tall] = x[:, :tall]
            deco[1, to, h * tall : (h + 1) * tall] = x[:, tall:]

    def spill(c):
        span = pl.ds(c * wide, wide)
        return remote(sps.at[span], spr.at[span], sp_s.at[c], sp_r.at[c], tm=earlier)

    def spill_scale(c):
        return remote(sss.at[c], ssr.at[c], ss_s.at[c], ss_r.at[c], tm=earlier)

    for chunk in range(chunks):
        if chunk % (chunks // 2) == 0:
            back_again(chunk // (chunks // 2))
        top = jnp.full((1, 1), 1e-30, F32)
        for q in range(chunk * wide, (chunk + 1) * wide, 2):
            x = jnp.concatenate(
                [
                    jnp.concatenate([deco[0, :, q, :], deco[1, :, q, :]], axis=0),
                    jnp.concatenate([deco[0, :, q + 1, :], deco[1, :, q + 1, :]], axis=0),
                ],
                axis=1,
            )
            high, low = split(x)
            got = jnp.dot(
                syn[...], jnp.concatenate([high, low, high], axis=0), preferred_element_type=F32
            )
            for i in range(2):
                head[q + i] = got[:HOP, i * LANES : (i + 1) * LANES]
                tail[q + i] = got[HOP:, i * LANES : (i + 1) * LANES]
            top = jnp.maximum(top, peak_of(got[:HOP]))
        sss[chunk] = jnp.broadcast_to(top * (1.0 / TOP), (1, LANES))
        for q in range(chunk * wide, (chunk + 1) * wide):
            sps[q] = coded(head[q], TOP / top)

        @pl.when(tm > 0)
        def _():
            spill_scale(chunk).start()
            spill(chunk).start()


    seg_id = lax.broadcasted_iota(jnp.int32, (8, LANES), 0)

    def shifted(x, by, fill):
        return jnp.where(seg_id >= by, pltpu.roll(x, by, 0), fill)

    def rate_of(length):
        return 1.0 - 1.0 / length

    def natural(g, vectors):
        return in_order(temp, g, vectors)

    for chunk in range(chunks):
        @pl.when(tm < nt - 1)
        def _():
            spill_scale(chunk).wait_recv()
            spill(chunk).wait_recv()

        def scan_row(q, g):
            at = pl.ds(q, 1)
            cols = slice(q * LANES, (q + 1) * LANES)
            heads = jnp.where(tm < nt - 1, spr[q].astype(F32) * ssr[chunk], 0.0)
            rounded = (tail[q] + heads).astype(BF16).astype(F32)
            part = [rounded[8 * i : 8 * i + 8] for i in range(8)]
            filtered[:, cols] = natural(g, part).astype(BF16)
            energy = [v * v for v in part]
            for s in range(2):
                keep = jnp.broadcast_to(rate_of(rates(s, at)), (8, LANES))
                gain = 1.0 - keep
                level = gain * energy[0]
                lev[s, q, 0:8] = level
                for i in range(1, 8):
                    level = keep * level + gain * energy[i]
                    lev[s, q, 8 * i : 8 * i + 8] = level
                power = keep * keep
                power = power * power
                power = power * power
                for by in (1, 2, 4):
                    level = level + power * shifted(level, by, 0.0)
                    power = power * power
                seg[s, q] = shifted(level, 1, 0.0)
                cars[q // tall, s, q % tall : q % tall + 1, :] = level[7:8]

        for g in range(wide):
            scan_row(chunk * wide + g, g)

    stores = [
        pltpu.make_async_copy(src, dst, store_sem.at[i])
        for i, (src, dst) in enumerate([(filtered, filtered_far), (ratio, ratio_far), (lev, lev_far)])
    ]
    stores[0].start()

    core = lax.rem(tm, 2)
    chip = tm // 2
    sibling = tm + 1 - 2 * core

    def give(src, dst, i):
        return remote(src, dst, sib_s.at[i], sib_r.at[i], tm=sibling)

    def to_later(snd, rcv, i, j):
        to = lax.rem(tm + 2 * j, nt)
        return remote(snd, rcv.at[chip], z_s.at[i, j], z_r.at[i, j], tm=to)

    def from_earlier(snd, rcv, i, j):
        back = lax.rem(tm + nt - 2 * j, nt)
        return remote(snd, rcv.at[chip - j], z_s.at[i, j], z_r.at[i, j], tm=back)

    def pair_of(ref):
        return ref[0], ref[1]

    def chosen(first, second):
        return tuple(jnp.where(core == 0, a, b) for a, b in zip(first, second))

    def pass_on(i, own, sib, tot, totr, gift, entry, join, apply, step, begin):
        half_away = give(own.at[1 - core], sib, 2 * i)
        half_away.start()
        half_away.wait_recv()
        mine, other = pair_of(own.at[core]), pair_of(sib)
        early, late = chosen(mine, other), chosen(other, mine)
        tot[0], tot[1] = join(early, late)

        def out(j, c):
            to_later(tot, totr, i, j).start()
            return c

        lax.fori_loop(1, nz - chip, out, 0)

        def come(j, c):
            from_earlier(tot, totr, i, j).wait_recv()
            return c

        lax.fori_loop(1, chip + 1, come, 0)
        state = lax.fori_loop(0, chip, lambda k, state: apply(state, pair_of(totr.at[k])), begin)
        after = step(state, early)
        entry[core, 0], entry[core, 1] = chosen(state, after)
        gift[0], gift[1] = chosen(after, state)
        give(gift, entry.at[core], 2 * i + 1).start()

    my_rows = pl.ds(pl.multiple_of(core * tall, tall), tall)
    decay = []
    for s in range(2):
        power = rate_of(chan[s, my_rows, :].astype(F32))
        for _ in range(6):
            power = power * power
        decay.append(power)

    def later_by(times, state, more):
        return tuple(g**times * x + y for g, x, y in zip(decay, state, more))

    ones = jnp.ones((tall, LANES), F32)
    pass_on(
        0,
        cars,
        carsib,
        cartot,
        carall,
        cargift,
        start,
        functools.partial(later_by, 1),
        functools.partial(later_by, 2),
        functools.partial(later_by, 1),
        (ones, ones),
    )

    def climb_row(h, r):
        q = h * tall + r
        g = r % GROUP
        at = pl.ds(q, 1)
        here = slice(r, r + 1)
        cols = pl.ds(pl.multiple_of(q * LANES, LANES), LANES)
        avg = []
        for s in range(2):
            keep = jnp.broadcast_to(rate_of(rates(s, at)), (8, LANES))
            carry = jnp.broadcast_to(start[h, s, here, :], (8, LANES))
            power = keep * keep
            power = power * power
            power = power * power
            for bit in (1, 2, 4):
                carry = jnp.where((seg_id // bit) % 2 == 1, carry * power, carry)
                power = power * power
            entry = seg[s, q] + carry
            values = []
            for i in range(8):
                entry = entry * keep
                values.append(lev[s, q, 8 * i : 8 * i + 8] + entry)
            avg.append(values)
        quotient = [avg[0][i] / avg[1][i] for i in range(8)]
        ratio[:, cols] = natural(g, quotient)
        rate = jnp.broadcast_to(0.5 + rates(2, at) * (1.0 / 64.0), (8, LANES))
        climb = quotient[0] - rate
        low = climb
        climbs, lows = [climb], [low]
        for i in range(1, 8):
            climb = climb + (quotient[i] - rate)
            low = jnp.minimum(low, climb)
            climbs.append(climb)
            lows.append(low)
        whole = climb
        for by in (1, 2, 4):
            whole = whole + shifted(whole, by, 0.0)
        base = shifted(whole, 1, 0.0)
        least = base + low
        for by in (1, 2, 4):
            least = jnp.minimum(least, shifted(least, by, jnp.inf))
        floor = shifted(least, 1, jnp.inf)
        for i in range(8):
            up = base + climbs[i]
            lev[0, q, 8 * i : 8 * i + 8] = up
            lev[1, q, 8 * i : 8 * i + 8] = jnp.minimum(floor, base + lows[i])
        sums[h, 0, here, :] = whole[7:8]
        sums[h, 1, here, :] = least[7:8]

    for r in range(tall):
        climb_row(core, r)
    give(cargift, start.at[1 - core], 1).wait_recv()
    for r in range(tall):
        climb_row(1 - core, r)

    stores[1].start()
    stores[2].start()

    def add_up(state, more):
        return state[0] + more[0], jnp.minimum(state[1], state[0] + more[1])

    zeros = jnp.zeros((tall, LANES), F32)
    pass_on(
        1, sums, sumsib, sumtot, sumall, sumgift, prior, add_up, add_up, add_up, (zeros, zeros)
    )
    give(sumgift, prior.at[1 - core], 3).wait_recv()
    last = pltpu.make_async_copy(prior, prior_far, store_sem.at[3])
    last.start()

    @pl.when(tm < nt - 1)
    def _():
        for chunk in range(chunks):
            rim_copy(chunk).wait_send()

    for i in range(per + 1):
        all1(i).wait_send()
    for i in range(per + 1):
        all2(i).wait_send()
    all_scales1().wait_send()
    all_scales2().wait_send()
    @pl.when(tm > 0)
    def _():
        for chunk in range(chunks):
            spill_scale(chunk).wait_send()
            spill(chunk).wait_send()

    for i, (own, sib, gift, entry) in enumerate(
        ((cars, carsib, cargift, start), (sums, sumsib, sumgift, prior))
    ):
        give(own.at[1 - core], sib, 2 * i).wait_send()
        give(gift, entry.at[core], 2 * i + 1).wait_send()

    def sent_on(j, c):
        to_later(cartot, carall, 0, j).wait_send()
        to_later(sumtot, sumall, 1, j).wait_send()
        return c

    lax.fori_loop(1, nz - chip, sent_on, 0)
    for store in stores:
        store.wait()
    last.wait()


def finish(
    filtered_far,
    ratio_far,
    lev_far,
    prior_far,
    limit_far,
    filtered_out,
    ratio_out,
    ph_out,
    filtered,
    ratio,
    lev,
    prior,
    limit,
    ph,
    temp,
    load_sem,
    store_sem,
):
    groups = ROWS // GROUP
    loads = [
        pltpu.make_async_copy(src, dst, load_sem.at[i])
        for i, (src, dst) in enumerate(
            [(prior_far, prior), (limit_far, limit), (filtered_far, filtered), (ratio_far, ratio)]
            + [(lev_far.at[:, pl.ds(4 * i, 4)], lev.at[:, pl.ds(4 * i, 4)]) for i in range(groups)]
        )
    ]
    for i in (0, 1, 4, 5, 6, 7, 2, 3):
        loads[i].start()
    stores = [
        pltpu.make_async_copy(filtered, filtered_out, store_sem.at[0]),
        pltpu.make_async_copy(ratio, ratio_out, store_sem.at[1]),
    ]
    loads[0].wait()
    loads[1].wait()
    for i in range(groups):
        loads[4 + i].wait()
        for g in range(GROUP):
            q = i * GROUP + g
            h, r = divmod(q, ROWS // 2)
            base = jnp.broadcast_to(prior[h, 0, r : r + 1, :], (8, LANES))
            low = jnp.broadcast_to(prior[h, 1, r : r + 1, :], (8, LANES))
            scale = jnp.broadcast_to(1.0 / limit[q : q + 1, :].astype(F32), (8, LANES))
            out = []
            for k in range(8):
                climb = base + lev[0, q, 8 * k : 8 * k + 8]
                lowest = jnp.minimum(low, base + lev[1, q, 8 * k : 8 * k + 8])
                out.append((climb - lowest) * scale)
            ph[:, q * LANES : (q + 1) * LANES] = in_order(temp, g, out)
        span = pl.ds(i * GROUP * LANES, GROUP * LANES)
        stores.append(
            pltpu.make_async_copy(ph.at[:, span], ph_out.at[:, span], store_sem.at[2 + i])
        )
        stores[-1].start()
        if i < 2:
            loads[2 + i].wait()
            stores[i].start()
    for store in stores:
        store.wait()


def body(nf, nt, strain, fan_cut, sta_len, lta_len, drift_code, threshold):
    per = BINS // nf
    rows = nf * ROWS
    total = rows * LANES
    half = rows // 2
    tabs = [jnp.asarray(t) for t in tables(total)]
    per_chan = [v.reshape(ROWS, LANES) for v in (sta_len, lta_len, drift_code, threshold)]
    far = pl.BlockSpec(memory_space=pl.ANY)
    dma = pltpu.SemaphoreType.DMA
    i16 = jnp.int16
    chans = ROWS * LANES
    results = pl.pallas_call(
        functools.partial(kernel, nf, nt),
        out_shape=(
            jax.ShapeDtypeStruct((HOP, chans), BF16),
            jax.ShapeDtypeStruct((HOP, chans), F32),
            jax.ShapeDtypeStruct((2, ROWS, HOP, LANES), F32),
            jax.ShapeDtypeStruct((2, 2, ROWS // 2, LANES), F32),
        ),
        in_specs=[far] * 12,
        out_specs=(far,) * 4,
        scratch_shapes=[
            pltpu.VMEM((HOP, chans), BF16),
            pltpu.SMEM((BINS,), jnp.int32),
            pltpu.VMEM((3, ROWS, LANES), jnp.int32),
        ]
        + [pltpu.VMEM(t.shape, F32) for t in tabs]
        + [
            pltpu.VMEM((2 * FRAME, FRAME), BF16),
            pltpu.VMEM((rows, 3 * half), BF16),
            pltpu.VMEM((6 * LANES, 2 * LANES), BF16),
            pltpu.VMEM((6 * LANES, 2 * LANES), BF16),
            pltpu.VMEM((FRAME, 3 * FRAME), BF16),
            pltpu.VMEM((HOP, chans), BF16),
            pltpu.VMEM((HOP, chans), F32),
            pltpu.VMEM((HOP, chans), BF16),
            pltpu.VMEM((FRAME, ROWS, LANES), F32),
            pltpu.VMEM((BINS, 2, ROWS, LANES), i16),
            pltpu.VMEM((per, nf, 2, ROWS, LANES), i16),
            pltpu.VMEM((2, 1, LANES), F32),
            pltpu.VMEM((nf, 2, 1, LANES), F32),
            pltpu.VMEM((2, 3 * half, 2 * LANES), BF16),
            pltpu.VMEM((2, 3 * half, 2 * LANES), BF16),
            pltpu.VMEM((per, nf, 2, ROWS, LANES), i16),
            pltpu.VMEM((per - 1, nf, 2, ROWS, LANES), i16),
            pltpu.VMEM((2, nf, ROWS, LANES), i16),
            pltpu.VMEM((2, per, 1, LANES), F32),
            pltpu.VMEM((nf, per, 1, LANES), F32),
            pltpu.VMEM((2, BINS, ROWS, LANES), F32),
            pltpu.VMEM((ROWS, HOP, LANES), F32),
            pltpu.VMEM((ROWS, HOP, LANES), F32),
            pltpu.VMEM((ROWS, HOP, LANES), i16),
            pltpu.VMEM((ROWS, HOP, LANES), i16),
            pltpu.VMEM((4, 1, LANES), F32),
            pltpu.VMEM((4, 1, LANES), F32),
            pltpu.VMEM((2, ROWS, HOP, LANES), F32),
            pltpu.VMEM((2, ROWS, 8, LANES), F32),
        ]
        + 2
        * [
            pltpu.VMEM((2, 2, ROWS // 2, LANES), F32),
            pltpu.VMEM((2, ROWS // 2, LANES), F32),
            pltpu.VMEM((2, ROWS // 2, LANES), F32),
            pltpu.VMEM((nt // 2, 2, ROWS // 2, LANES), F32),
            pltpu.VMEM((2, ROWS // 2, LANES), F32),
            pltpu.VMEM((2, 2, ROWS // 2, LANES), F32),
        ]
        + [
            pltpu.VMEM((GROUP, HOP, LANES), F32),
            dma((4,)),
            dma((4,)),
            dma((per + 1,)),
            dma((per + 1,)),
            dma((1,)),
            dma((1,)),
            dma((per + 1,)),
            dma((per + 1,)),
            dma((1,)),
            dma((1,)),
            dma((4,)),
            dma((4,)),
            dma((4,)),
            dma((4,)),
            dma((4,)),
            dma((4,)),
            dma((2, nt // 2)),
            dma((2, nt // 2)),
            dma((12,)),
            dma((4,)),
        ],
        compiler_params=pltpu.CompilerParams(
            collective_id=0, has_side_effects=True, vmem_limit_bytes=64 * 1024 * 1024
        ),
    )(strain, fan_cut, *per_chan[:3], *tabs)
    return pl.pallas_call(
        finish,
        out_shape=(
            jax.ShapeDtypeStruct((HOP, chans), BF16),
            jax.ShapeDtypeStruct((HOP, chans), F32),
            jax.ShapeDtypeStruct((HOP, chans), F32),
        ),
        in_specs=[far] * 5,
        out_specs=(far,) * 3,
        scratch_shapes=[
            pltpu.VMEM((HOP, chans), BF16),
            pltpu.VMEM((HOP, chans), F32),
            pltpu.VMEM((2, ROWS, HOP, LANES), F32),
            pltpu.VMEM((2, 2, ROWS // 2, LANES), F32),
            pltpu.VMEM((ROWS, LANES), jnp.int32),
            pltpu.VMEM((HOP, chans), F32),
            pltpu.VMEM((GROUP, HOP, LANES), F32),
            dma((8,)),
            dma((6,)),
        ],
        compiler_params=pltpu.CompilerParams(vmem_limit_bytes=64 * 1024 * 1024),
    )(*results, per_chan[3])


def solution(mesh):
    return jax.shard_map(
        functools.partial(body, mesh.shape["fiber"], mesh.shape["tm"]),
        mesh=mesh,
        in_specs=(P("tm", "fiber"), P(), P("fiber"), P("fiber"), P("fiber"), P("fiber")),
        out_specs=(P("tm", "fiber"), P("tm", "fiber"), P("tm", "fiber")),
        check_vma=False,
    )
```
